32 devices in a mesh: head: 4 (over y, x), blk: 8 (over z, core).
Axes of the slice: x: 2, y: 2, z: 4, core: 2. Of those that a mesh axis runs over, the one named last changes fastest.
Arguments:
- hidden_in: bfloat16 [4096, 2, 2048], P(('blk', 'head')), may hold values from -6 to 6
- attn_gain: float32 [2048], replicated, may hold values from 0.5 to 1.5
- w_query: bfloat16 [2048, 2048], P('blk', 'head'), may hold values from -0.125 to 0.125
- w_key: bfloat16 [2048, 2048], P('blk', 'head'), may hold values from -0.125 to 0.125
- w_value: bfloat16 [2048, 2048], P('blk', 'head'), may hold values from -0.125 to 0.125
- query_gain: float32 [2048], replicated, may hold values from 0.5 to 1.5
- key_gain: float32 [2048], replicated, may hold values from 0.5 to 1.5
- w_out: bfloat16 [2048, 2048], P('head', 'blk'), may hold values from -2 to 2
- ffn_gain: float32 [2048], replicated, may hold values from 0.5 to 1.5
- w_gate: bfloat16 [32, 2048, 512], P(('blk', 'head')), may hold values from -0.125 to 0.125
- w_up: bfloat16 [32, 2048, 512], P(('blk', 'head')), may hold values from -0.125 to 0.125
- w_down: bfloat16 [32, 512, 2048], P(('blk', 'head')), may hold values from -0.75 to 0.75
- routes: int32 [4096, 2, 8], P(('blk', 'head')), may hold values from 0 to 15, all different within a row; in each aligned block of 256 rows (0 to 255, 256 to 511, ..., all dimensions but the last counted through in order) at most 160 rows name the same one
- gate_weights: float32 [4096, 2, 8], P(('blk', 'head')), may hold values from 0.05 to 0.25
- block_starts: int32 [2, 16], replicated, may hold values from 0 to 15, as said below
- cotangent: bfloat16 [4096, 2, 2048], P(('blk', 'head')), may hold values from -6 to 6
Outputs:
- layer_out: bfloat16 [4096, 2, 2048], P(('blk', 'head'))
- grad_in: bfloat16 [4096, 2, 2048], P(('blk', 'head'))
- grad_attn_gain: float32 [2048], replicated
- grad_query: float32 [2048, 2048], P('blk', 'head')
- grad_key: float32 [2048, 2048], P('blk', 'head')
- grad_value: float32 [2048, 2048], P('blk', 'head')
- grad_query_gain: float32 [2048], replicated
- grad_key_gain: float32 [2048], replicated
- grad_out: float32 [2048, 2048], P('head', 'blk')
- grad_ffn_gain: float32 [2048], replicated
- grad_gate: float32 [32, 2048, 512], P(('blk', 'head'))
- grad_up: float32 [32, 2048, 512], P(('blk', 'head'))
- grad_down: float32 [32, 512, 2048], P(('blk', 'head'))
- stream_stats: float32 [3], replicated
The draws below stay inside these ranges and needn't reach their ends.
Inputs may be any that keep to these rules, and one draw needn't show every extreme that they name: `routes`: among the rows of one device (position-major, then sequence), no expert is named more than 160 times, a bound that some block reaches. block_starts[s, 0] = 0 and block_starts[s, k] is k or block_starts[s, k - 1]. In every draw, in some sequence the document of block 0 reaches block 14 or further, and in some sequence the last block starts its own document.
All inputs are finite; a program needn't handle non-finite values.
Results may differ from the reference program's by a relative error of at most 0.023.
Values may be sent and summed in bfloat16 or wider, within the bound.
A program may use at most 384 MiB of HBM per device.

```python
import math
import jax
import jax.numpy as jnp
import numpy as np
from jax import lax

D = 2048
HEADS = 16
HEAD_DIM = 128
FF = 1024
TOP = 8
BLOCK = 256
SEQS = 2
NBLOCKS = 16
SEQLEN = 4096
TOK_DEV = 256
EXPERTS = 16
HALVES = 32
HALF = 512
CAP = 160


def draw_block_starts(key, part):
    key = jax.random.fold_in(key, 7)
    cut_key, pick_key = jax.random.split(key, 2)
    marks = jax.random.randint(cut_key, (SEQS, NBLOCKS), 0, 3) == 0
    chosen = jax.random.randint(pick_key, (), 0, SEQS)
    sequence_ids = jnp.arange(SEQS, dtype=jnp.int32)[:, None]
    places = jnp.arange(NBLOCKS, dtype=jnp.int32)[None, :]
    marks = marks & (places > 0) & (sequence_ids != chosen)
    marks = marks | (sequence_ids == chosen) & (places == NBLOCKS - 1)
    firsts = jnp.where(marks, places, 0)
    return lax.cummax(firsts, axis=1).astype(jnp.int32)


def block_levels(stream_key, shape, cuts, least, high):
    gain, own = 1.0, jax.random.fold_in(stream_key, 6)
    for position, parts in cuts:
        heights = jnp.exp(jax.random.uniform(jax.random.fold_in(own, position), (parts,), jnp.float32, least / len(cuts), high / len(cuts)))
        gain = gain * jnp.repeat(heights, shape[position] // parts).reshape([-1 if axis == position else 1 for axis in range(len(shape))])
    return gain


def shared_out(stream_key, own, number, rows, count, top, reach, lean):
    ranking = jax.random.permutation(stream_key, count)
    packed, usual = portions_of(count, rows * top, reach, lean, True), portions_of(count, rows * top, reach, lean, False)
    places = jnp.arange(count)

    def named(sizes, offset_by):
        used = int((sizes > 0).sum())
        fixed = max(1, used // 4)
        moved = fixed + (places - fixed + offset_by * (used - fixed)) % max(1, count - fixed)
        return jnp.zeros((count,), jnp.int32).at[ranking[jnp.where(places < fixed, places, moved)]].set(jnp.asarray(sizes, jnp.int32))

    sizes = jnp.where(number % 4 == 0, named(packed, number // 4), named(usual, number - number // 4 - 1))
    mixed = jax.random.permutation(jax.random.fold_in(own, 3), count)
    source_of, taker = mixed[0:count // 2 * 2:2], mixed[1:count // 2 * 2:2]
    margin = jnp.minimum(sizes[source_of] - 1, reach - sizes[taker]) // 2
    margin = jnp.where((source_of == ranking[0]) | (taker == ranking[0]) | (sizes[taker] == 0), 0, jnp.maximum(margin, 0))
    moved = jax.random.randint(jax.random.fold_in(own, 4), (count // 2,), 0, 1 << 20) % (margin + 1)
    sizes = sizes.at[source_of].add(-moved).at[taker].add(moved)
    members = jnp.searchsorted(jnp.cumsum(sizes), jnp.arange(rows * top), side="right").astype(jnp.int32)
    table = members.reshape(top, rows).T
    table = table[jax.random.permutation(jax.random.fold_in(own, 1), rows)]
    offset_by = jax.random.randint(jax.random.fold_in(own, 2), (rows, 1), 0, top)
    return jnp.take_along_axis(table, (jnp.arange(top)[None, :] + offset_by) % top, axis=1)


def portions_of(amount, total, most, lean, full):
    portions = [(1 << 20) // math.isqrt(grade ** lean) + 1 for grade in range(1, amount + 1)]
    largest = most if full else min(most, max(-(-total // amount), total * portions[0] // sum(portions)))
    least = 1 if total - largest >= amount - 1 else 0
    counts, rest = [largest] + [least] * (amount - 1), total - largest - least * (amount - 1)
    while rest > 0:
        movable = [i for i in range(1, amount) if counts[i] < largest] or [i for i in range(1, amount) if counts[i] < most]
        mass, remaining = sum([portions[i] for i in movable]), rest
        for i in movable:
            extra = min(most - counts[i], max(1, remaining * portions[i] // mass), rest)
            counts[i] = counts[i] + extra
            rest = rest - extra
    return np.array(counts)


def scatter_about(stream_key, extent, width, bound, cuts=(), held_as=jnp.bfloat16):
    drawn = width * jax.random.normal(stream_key, extent, jnp.float32)
    if cuts:
        drawn = drawn * block_levels(stream_key, extent, cuts, -0.22, 0.18)
    return jnp.clip(drawn, -bound, bound).astype(held_as)


def setup_inputs(seed: int = 0) -> dict:
    streams_of = jax.random.split(jax.random.key(seed), 17)
    hidden_in = scatter_about(streams_of[0], (SEQLEN, SEQS, D), 1.0, 6.0, ((0, 32),))
    attn_gain = jnp.clip(1.0 + 0.1 * jax.random.normal(streams_of[1], (D,), jnp.float32), 0.5, 1.5)
    w_query = scatter_about(streams_of[2], (D, D), D ** -0.5, 0.125, ((0, 8), (1, 4)))
    w_key = scatter_about(streams_of[3], (D, D), D ** -0.5, 0.125, ((0, 8), (1, 4)))
    w_value = scatter_about(streams_of[4], (D, D), D ** -0.5, 0.125, ((0, 8), (1, 4)))
    query_gain = jnp.clip(1.0 + 0.1 * jax.random.normal(streams_of[5], (D,), jnp.float32), 0.5, 1.5)
    key_gain = jnp.clip(1.0 + 0.1 * jax.random.normal(streams_of[6], (D,), jnp.float32), 0.5, 1.5)
    w_out = scatter_about(streams_of[7], (D, D), (max(1, D // 256)) ** -0.5, 2.0, ((0, 4), (1, 8)))
    ffn_gain = jnp.clip(1.0 + 0.1 * jax.random.normal(streams_of[8], (D,), jnp.float32), 0.5, 1.5)
    w_gate = scatter_about(streams_of[9], (HALVES, D, HALF), D ** -0.5, 0.125, ((0, 32),))
    w_up = scatter_about(streams_of[10], (HALVES, D, HALF), D ** -0.5, 0.125, ((0, 32),))
    w_down = scatter_about(streams_of[11], (HALVES, HALF, D), (FF // 16) ** -0.5, 0.75, ((0, 32),))
    routes_keys = jax.random.split(jax.random.fold_in(streams_of[12], 1), SEQLEN * SEQS // TOK_DEV)
    routes_turns = jax.random.permutation(jax.random.fold_in(streams_of[12], 3), SEQLEN * SEQS // TOK_DEV)
    routes = jax.vmap(lambda own, number: shared_out(jax.random.fold_in(streams_of[12], 2), own, number, TOK_DEV, EXPERTS, TOP, CAP, 1))(routes_keys, routes_turns).reshape((SEQLEN, SEQS, TOP))
    gate_weights = jnp.clip(jnp.exp(math.log(0.25) - 1.609438 * jax.random.uniform(streams_of[13], (SEQLEN, SEQS, TOP), jnp.float32) ** block_levels(streams_of[13], (SEQLEN, SEQS, TOP), ((0, 32),), -0.2, 0.2)), 0.05, 0.25)
    block_starts = draw_block_starts(jax.random.fold_in(streams_of[16], 71), 0)
    cotangent = scatter_about(streams_of[15], (SEQLEN, SEQS, D), 1.0, 6.0, ((0, 32),))
    return dict(hidden_in=hidden_in, attn_gain=attn_gain, w_query=w_query, w_key=w_key, w_value=w_value, query_gain=query_gain, key_gain=key_gain, w_out=w_out, ffn_gain=ffn_gain, w_gate=w_gate, w_up=w_up, w_down=w_down, routes=routes, gate_weights=gate_weights, block_starts=block_starts, cotangent=cotangent)


EPSILON = 1e-06
PRECISE = lax.Precision.HIGHEST

@jax.custom_vjp
def low(v):
    return lax.optimization_barrier(v.astype(jnp.bfloat16)).astype(jnp.float32)

@jax.custom_vjp
def low_back(v):
    return v

def low_keep(v):
    return (low(v), None)

def low_pass(kept, grad):
    return (grad,)

def back_keep(v):
    return (v, None)

def back_low(kept, grad):
    return (low(grad),)
low.defvjp(low_keep, low_pass)
low_back.defvjp(back_keep, back_low)

def matmul(left, right):
    return jnp.matmul(left, right, precision=PRECISE)

def rms_norm(values, scale):
    return values * lax.rsqrt(lax.optimization_barrier(jnp.mean(values * values, axis=-1, keepdims=True)) + EPSILON) * scale

def attend_sequence(item):
    queries, keys, values, first = item
    blocks = jnp.arange(SEQLEN, dtype=jnp.int32) // BLOCK
    allowed = (blocks[None, :] >= first[blocks][:, None]) & (blocks[None, :] <= blocks[:, None])

    def one_head(inner):
        query_h, key_h, value_h = inner
        scores = low_back(matmul(query_h, key_h.T) * (1.0 / math.sqrt(HEAD_DIM)))
        scores = jnp.where(allowed, scores, -1e+30)
        shifted = jnp.exp(scores - lax.optimization_barrier(jnp.max(scores, axis=-1, keepdims=True)))
        probs = shifted / lax.optimization_barrier(jnp.sum(shifted, axis=-1, keepdims=True))
        return matmul(low(probs), value_h)
    result = lax.map(jax.checkpoint(one_head), (queries.transpose(1, 0, 2), keys.transpose(1, 0, 2), values.transpose(1, 0, 2)))
    return result.transpose(1, 0, 2)

def make_forward(routes, gate_weights, block_starts):
    route_rows = routes.reshape(SEQLEN * SEQS, TOP)
    gate_rows = gate_weights.reshape(SEQLEN * SEQS, TOP)

    def by_sequence(values):
        return values.reshape(SEQLEN, SEQS, HEADS, HEAD_DIM).transpose(1, 0, 2, 3)

    def forward(hidden, attn_gain, w_query, w_key, w_value, query_gain, key_gain, w_out, ffn_gain, w_gate, w_up, w_down):
        normed = low(low_back(rms_norm(hidden, attn_gain)))
        query_raw = low_back(matmul(normed, w_query))
        key_raw = low_back(matmul(normed, w_key))
        query_n = low(low_back(rms_norm(query_raw, query_gain)))
        key_n = low(low_back(rms_norm(key_raw, key_gain)))
        values = low(low_back(matmul(normed, w_value)))
        attended = lax.map(jax.checkpoint(attend_sequence), (by_sequence(query_n), by_sequence(key_n), by_sequence(values), block_starts))
        attended = attended.transpose(1, 0, 2, 3).reshape(SEQLEN, SEQS, D)
        attended = low(low_back(attended))
        branch = low_back(matmul(attended, w_out))
        middle = hidden + branch
        normed_two = low(low_back(rms_norm(middle, ffn_gain)))
        token_rows = normed_two.reshape(SEQLEN * SEQS, D)

        def expert_step(total, expert):
            weight = lax.optimization_barrier(jnp.sum(jnp.where(route_rows == expert, gate_rows, 0.0), axis=1))
            combined = jnp.zeros_like(total)
            for half in range(2):
                index = 2 * expert + half
                gate_pre = low_back(matmul(token_rows, lax.dynamic_index_in_dim(w_gate, index, 0, keepdims=False)))
                up_pre = low_back(matmul(token_rows, lax.dynamic_index_in_dim(w_up, index, 0, keepdims=False)))
                activated = gate_pre / (1.0 + jnp.exp(-gate_pre))
                hidden_units = low(low_back(activated * up_pre))
                combined = combined + low(matmul(hidden_units, lax.dynamic_index_in_dim(w_down, index, 0, keepdims=False)))
            return (total + weight[:, None] * low_back(combined), None)
        start_total = jnp.zeros((SEQLEN * SEQS, D), jnp.float32)
        expert_sum, _ = lax.scan(jax.checkpoint(expert_step), start_total, jnp.arange(EXPERTS, dtype=jnp.int32))
        expert_sum = expert_sum.reshape(SEQLEN, SEQS, D)
        result = middle + expert_sum
        return (result, (branch, expert_sum))
    return forward

def reference(hidden_in, attn_gain, w_query, w_key, w_value, query_gain, key_gain, w_out, ffn_gain, w_gate, w_up, w_down, routes, gate_weights, block_starts, cotangent):
    forward = make_forward(routes, gate_weights.astype(jnp.float32), block_starts)
    params = (hidden_in.astype(jnp.float32), attn_gain.astype(jnp.float32), w_query.astype(jnp.float32), w_key.astype(jnp.float32), w_value.astype(jnp.float32), query_gain.astype(jnp.float32), key_gain.astype(jnp.float32), w_out.astype(jnp.float32), ffn_gain.astype(jnp.float32), w_gate.astype(jnp.float32), w_up.astype(jnp.float32), w_down.astype(jnp.float32))
    result, pullback, extras = jax.vjp(forward, *params, has_aux=True)
    grads = pullback(cotangent.astype(jnp.float32))
    branch, expert_sum = extras

    def root_mean(values):
        return jnp.sqrt(jnp.mean(values * values) + EPSILON)
    stream_stats = jnp.stack([root_mean(result), root_mean(branch), root_mean(expert_sum)])
    return (result.astype(jnp.bfloat16), grads[0].astype(jnp.bfloat16), grads[1], grads[2], grads[3], grads[4], grads[5], grads[6], grads[7], grads[8], grads[9], grads[10], grads[11], stream_stats)
```

```python
import functools
import math

import jax
import jax.numpy as jnp
from jax import lax
from jax.experimental import pallas as pl
from jax.experimental.pallas import tpu as pltpu
from jax.sharding import PartitionSpec as P

HEAD_DIM = 128
BLOCK = 256
EPSILON = 1e-06
F32 = jnp.float32
BF16 = jnp.bfloat16
VMEM_BYTES = 58 * 1024 * 1024

NN = (((1,), (0,)), ((), ()))
NT = (((1,), (1,)), ((), ()))
TN = (((0,), (0,)), ((), ()))


def mm(left, right, dims=NN):
    return lax.dot_general(left, right, dims, preferred_element_type=F32)


def rounded(values):
    return lax.optimization_barrier(values.astype(BF16)).astype(F32)


def inverse_rms(values):
    return lax.rsqrt(jnp.mean(values * values, axis=-1, keepdims=True) + EPSILON)


def attend_forward(starts, own, qkv, scale, share):
    src, _, per, block, dim = qkv.shape
    blocks = src * per

    def kernel(starts_ref, own_ref, qkv_ref, out_ref, out_t_ref, lse_ref, vt_ref):
        step = pl.program_id(0)

        @pl.when(step == 0)
        def _():
            def flip(j, carry):
                vt_ref[j] = qkv_ref[j // per, 2, j % per].astype(F32).T.astype(BF16)
                return carry

            lax.fori_loop(0, blocks, flip, 0)

        def work():
            query = qkv_ref[step // per, 0, step % per]

            def body(j, carry):
                top, total, acc = carry
                scores = mm(qkv_ref[j // per, 1, j % per], query, NT) * scale
                new_top = jnp.maximum(top, jnp.max(scores, axis=0, keepdims=True))
                weights = jnp.exp(scores - new_top)
                shrink = jnp.exp(top - new_top)
                total = total * shrink + jnp.sum(weights, axis=0, keepdims=True)
                acc = acc * shrink + mm(vt_ref[j], weights.astype(BF16))
                return new_top, total, acc

            top, total, acc = lax.fori_loop(
                starts_ref[step],
                step + 1,
                body,
                (
                    jnp.full((1, block), -1e30, F32),
                    jnp.zeros((1, block), F32),
                    jnp.zeros((dim, block), F32),
                ),
            )
            result = acc / total
            out_t_ref[0] = result
            out_ref[0] = result.T.astype(BF16)
            lse_ref[0] = top + jnp.log(total)

        if share == 1:
            work()
        else:
            mine = step % share == own_ref[0]
            pl.when(mine)(work)

            @pl.when(jnp.logical_not(mine))
            def _():
                out_t_ref[...] = jnp.zeros_like(out_t_ref)
                out_ref[...] = jnp.zeros_like(out_ref)
                lse_ref[...] = jnp.zeros_like(lse_ref)

    return pl.pallas_call(
        kernel,
        grid_spec=pltpu.PrefetchScalarGridSpec(
            num_scalar_prefetch=2,
            grid=(blocks,),
            in_specs=[pl.BlockSpec(qkv.shape, lambda i, *_: (0, 0, 0, 0, 0))],
            out_specs=[
                pl.BlockSpec((1, block, dim), lambda i, *_: (i, 0, 0)),
                pl.BlockSpec((1, dim, block), lambda i, *_: (i, 0, 0)),
                pl.BlockSpec((1, 1, block), lambda i, *_: (i, 0, 0)),
            ],
            scratch_shapes=[pltpu.VMEM((blocks, dim, block), BF16)],
        ),
        out_shape=[
            jax.ShapeDtypeStruct((blocks, block, dim), BF16),
            jax.ShapeDtypeStruct((blocks, dim, block), F32),
            jax.ShapeDtypeStruct((blocks, 1, block), F32),
        ],
        compiler_params=pltpu.CompilerParams(vmem_limit_bytes=VMEM_BYTES),
        name="attend_forward",
    )(starts, own, qkv)


def attend_backward(starts, own, qkv, grad_out, out_t, lse, scale, share):
    src, _, per, block, dim = qkv.shape
    blocks = src * per

    def kernel(
        starts_ref, own_ref, qkv_ref, go_ref, out_t_ref, lse_ref, grad_ref, dk_ref, dv_ref
    ):
        step = pl.program_id(0)

        @pl.when(step == 0)
        def _():
            dk_ref[...] = jnp.zeros_like(dk_ref)
            dv_ref[...] = jnp.zeros_like(dv_ref)

        def work():
            query = qkv_ref[step // per, 0, step % per]
            go = go_ref[0]
            delta = jnp.sum(go.astype(F32).T * out_t_ref[0], axis=0, keepdims=True)
            log_total = lse_ref[0]

            def body(j, dq):
                key = qkv_ref[j // per, 1, j % per]
                value = qkv_ref[j // per, 2, j % per]
                probs = jnp.exp(mm(key, query, NT) * scale - log_total)
                grad_scores = (probs * (mm(value, go, NT) - delta)).astype(BF16)
                dv_ref[j] += mm(probs.astype(BF16), go)
                dk_ref[j] += mm(grad_scores, query)
                return dq + mm(grad_scores, key, TN)

            dq = lax.fori_loop(starts_ref[step], step + 1, body, jnp.zeros((block, dim), F32))
            grad_ref[step // per, 0, step % per] = (dq * scale).astype(BF16)

        if share == 1:
            work()
        else:
            mine = step % share == own_ref[0]
            pl.when(mine)(work)

            @pl.when(jnp.logical_not(mine))
            def _():
                grad_ref[step // per, 0, step % per] = jnp.zeros((block, dim), BF16)

        @pl.when(step == blocks - 1)
        def _():
            def store(j, carry):
                grad_ref[j // per, 1, j % per] = (dk_ref[j] * scale).astype(BF16)
                grad_ref[j // per, 2, j % per] = dv_ref[j].astype(BF16)
                return carry

            lax.fori_loop(0, blocks, store, 0)

    return pl.pallas_call(
        kernel,
        grid_spec=pltpu.PrefetchScalarGridSpec(
            num_scalar_prefetch=2,
            grid=(blocks,),
            in_specs=[
                pl.BlockSpec(qkv.shape, lambda i, *_: (0, 0, 0, 0, 0)),
                pl.BlockSpec((1, block, dim), lambda i, *_: (i, 0, 0)),
                pl.BlockSpec((1, dim, block), lambda i, *_: (i, 0, 0)),
                pl.BlockSpec((1, 1, block), lambda i, *_: (i, 0, 0)),
            ],
            out_specs=pl.BlockSpec(qkv.shape, lambda i, *_: (0, 0, 0, 0, 0)),
            scratch_shapes=[
                pltpu.VMEM((blocks, block, dim), F32),
                pltpu.VMEM((blocks, block, dim), F32),
            ],
        ),
        out_shape=jax.ShapeDtypeStruct(qkv.shape, BF16),
        compiler_params=pltpu.CompilerParams(vmem_limit_bytes=VMEM_BYTES),
        name="attend_backward",
    )(starts, own, qkv, grad_out, out_t, lse)


def expert_rows(tokens, cots, slots, gates, w_gate, w_up, w_down, rows, step_blocks):
    blocks, tok, width = tokens.shape
    half = w_gate.shape[1]
    count = step_blocks * rows
    steps = blocks // step_blocks
    chunk = min(512, width)

    def kernel(
        tok_ref, cot_ref, slot_ref, gate_ref, wg_ref, wu_ref, wd_ref,
        moe_ref, dx_ref, xr_ref, er_ref, hid_ref, dgp_ref, dup_ref,
    ):
        lanes = lax.broadcasted_iota(jnp.int32, (rows, tok), 0)
        picks = []
        weights = []
        for b in range(step_blocks):
            hit = lanes == slot_ref[b]
            pick = jnp.where(hit, 1.0, 0.0).astype(BF16)
            weight = jnp.sum(jnp.where(hit, gate_ref[b], 0.0), axis=1, keepdims=True)
            here = slice(b * rows, (b + 1) * rows)
            picks.append(pick)
            weights.append(weight)
            for c in range(0, width, chunk):
                cols = slice(c, c + chunk)
                xr_ref[0, here, cols] = mm(pick, tok_ref[b, :, cols]).astype(BF16)
                er_ref[0, here, cols] = (weight * mm(pick, cot_ref[b, :, cols])).astype(BF16)
        x = xr_ref[0]
        gate_pre = mm(x, wg_ref[...])
        up_pre = mm(x, wu_ref[...])
        sig = jax.nn.sigmoid(gate_pre)
        act = gate_pre * sig
        hid = (act * up_pre).astype(BF16)
        hid_ref[0] = hid
        dhid = mm(er_ref[0], wd_ref[...], NT).astype(BF16).astype(F32)
        dgp = (dhid * up_pre * sig * (1.0 + gate_pre * (1.0 - sig))).astype(BF16)
        dup = (dhid * act).astype(BF16)
        dgp_ref[0] = dgp
        dup_ref[0] = dup
        for c in range(0, width, chunk):
            cols = slice(c, c + chunk)
            part = mm(hid, wd_ref[:, cols]).astype(BF16).astype(F32)
            drow = (mm(dgp, wg_ref[cols, :], NT) + mm(dup, wu_ref[cols, :], NT)).astype(BF16)
            for b in range(step_blocks):
                here = slice(b * rows, (b + 1) * rows)
                weighted = (part[here] * weights[b]).astype(BF16)
                moe_ref[b, :, cols] = mm(picks[b], weighted, TN).astype(BF16)
                dx_ref[b, :, cols] = mm(picks[b], drow[here], TN).astype(BF16)

    whole = lambda shape: pl.BlockSpec(shape, lambda i: (0,) * len(shape), pipeline_mode=pl.Buffered(1))
    per_step = lambda *shape: pl.BlockSpec(shape, lambda i: (i,) + (0,) * (len(shape) - 1))
    return pl.pallas_call(
        kernel,
        grid=(steps,),
        in_specs=[
            per_step(step_blocks, tok, width),
            per_step(step_blocks, tok, width),
            per_step(step_blocks, 1, tok),
            per_step(step_blocks, 1, tok),
            whole(w_gate.shape),
            whole(w_up.shape),
            whole(w_down.shape),
        ],
        out_specs=[
            per_step(step_blocks, tok, width),
            per_step(step_blocks, tok, width),
            per_step(1, count, width),
            per_step(1, count, width),
            per_step(1, count, half),
            per_step(1, count, half),
            per_step(1, count, half),
        ],
        out_shape=[
            jax.ShapeDtypeStruct((blocks, tok, width), BF16),
            jax.ShapeDtypeStruct((blocks, tok, width), BF16),
            jax.ShapeDtypeStruct((steps, count, width), BF16),
            jax.ShapeDtypeStruct((steps, count, width), BF16),
            jax.ShapeDtypeStruct((steps, count, half), BF16),
            jax.ShapeDtypeStruct((steps, count, half), BF16),
            jax.ShapeDtypeStruct((steps, count, half), BF16),
        ],
        compiler_params=pltpu.CompilerParams(vmem_limit_bytes=VMEM_BYTES),
        name="expert_rows",
    )(tokens, cots, slots, gates, w_gate, w_up, w_down)


def local(
    hidden_in,
    attn_gain,
    w_query,
    w_key,
    w_value,
    query_gain,
    key_gain,
    w_out,
    ffn_gain,
    w_gate,
    w_up,
    w_down,
    routes,
    gate_weights,
    block_starts,
    cotangent,
):
    head_count = lax.axis_size("head")
    blk_count = lax.axis_size("blk")
    head_index = lax.axis_index("head")
    blk_index = lax.axis_index("blk")
    piece, seqs, width = hidden_in.shape
    span = piece * head_count
    per = span // BLOCK
    columns = w_query.shape[1]
    heads_here = columns // HEAD_DIM
    top_count = routes.shape[2]
    experts = blk_count * head_count // 2
    devices = blk_count * head_count
    tok = piece * seqs
    capacity = max(2, 5 * tok * top_count // (4 * experts))
    rows = -(-capacity // 32) * 32
    items = seqs * heads_here
    share = blk_count // items
    scale = 1.0 / math.sqrt(HEAD_DIM)
    everyone = ("blk", "head")

    def own_rows(values):
        return values.transpose(1, 0, 2).reshape(tok, values.shape[2])

    def out_rows(values):
        return values.reshape(seqs, piece, width).transpose(1, 0, 2)

    expert = (blk_index * head_count + head_index) // 2
    all_routes = lax.all_gather(own_rows(routes), everyone, axis=0, tiled=False)
    all_gates = lax.all_gather(own_rows(gate_weights), everyone, axis=0, tiled=False)
    named = all_routes == expert
    hit = jnp.any(named, axis=-1)
    gates = jnp.sum(jnp.where(named, all_gates, 0.0), axis=-1)[:, None, :]
    before = jnp.triu(jnp.ones((tok, tok), BF16), 1)
    places = jnp.dot(hit.astype(BF16), before, preferred_element_type=F32).astype(jnp.int32)
    slots = jnp.where(hit, places, -1)[:, None, :]

    hidden_f = own_rows(hidden_in).astype(F32)
    grad_y_b = own_rows(cotangent)
    grad_y = grad_y_b.astype(F32)

    inv_one = inverse_rms(hidden_f)
    normed = (hidden_f * inv_one * attn_gain).astype(BF16)
    group = lax.all_gather(normed, "head", axis=0, tiled=True)
    query_cols = lax.all_gather(w_query, "blk", axis=0, tiled=True)
    key_cols = lax.all_gather(w_key, "blk", axis=0, tiled=True)
    value_cols = lax.all_gather(w_value, "blk", axis=0, tiled=True)
    out_w = lax.all_gather(w_out, "blk", axis=1, tiled=True)
    all_cots = lax.all_gather(grad_y_b, everyone, axis=0, tiled=False)

    query_raw = mm(group, query_cols)
    key_raw = mm(group, key_cols)
    value_raw = mm(group, value_cols)
    square_sums = lax.psum(
        jnp.stack([jnp.sum(query_raw * query_raw, -1), jnp.sum(key_raw * key_raw, -1)]), "head"
    )
    inv_query = lax.rsqrt(square_sums[0][:, None] / width + EPSILON)
    inv_key = lax.rsqrt(square_sums[1][:, None] / width + EPSILON)
    gain_query = lax.dynamic_slice_in_dim(query_gain, head_index * columns, columns)
    gain_key = lax.dynamic_slice_in_dim(key_gain, head_index * columns, columns)
    query_n = (query_raw * inv_query * gain_query).astype(BF16)
    key_n = (key_raw * inv_key * gain_key).astype(BF16)
    value_n = value_raw.astype(BF16)

    def to_items(values):
        parts = values.reshape(head_count, seqs, piece, heads_here, HEAD_DIM)
        parts = parts.transpose(1, 3, 0, 2, 4).reshape(items, span, HEAD_DIM)
        return jnp.repeat(parts, share, axis=0) if share > 1 else parts

    def from_items(values):
        if share > 1:
            values = values.reshape(items, share, span, HEAD_DIM).astype(F32).sum(1)
        parts = values.reshape(seqs, heads_here, head_count, piece, HEAD_DIM)
        return parts.transpose(2, 0, 3, 1, 4).reshape(head_count * tok, columns)

    def swap(values):
        return lax.all_to_all(values, "blk", split_axis=0, concat_axis=0, tiled=True)

    item = blk_index // share
    own = (blk_index % share).reshape(1).astype(jnp.int32)
    starts = lax.dynamic_index_in_dim(block_starts, item // heads_here, 0, keepdims=False)
    qkv = swap(jnp.stack([to_items(query_n), to_items(key_n), to_items(value_n)], axis=1))
    qkv = qkv.reshape(blk_count, 3, per, BLOCK, HEAD_DIM)
    heads_out, heads_out_t, log_total = attend_forward(starts, own, qkv, scale, share)
    attended = from_items(swap(heads_out.reshape(blk_count, span, HEAD_DIM))).astype(BF16)
    branch = lax.psum_scatter(
        mm(attended, out_w).astype(BF16), "head", scatter_dimension=0, tiled=True
    ).astype(F32)
    middle = hidden_f + branch
    inv_two = inverse_rms(middle)
    normed_two = (middle * inv_two * ffn_gain).astype(BF16)

    all_tokens = lax.all_gather(normed_two, everyone, axis=0, tiled=False)
    step_blocks = 2
    moe_parts, dx_parts, xr, er, hid, dgp, dup = expert_rows(
        all_tokens, all_cots, slots, gates, w_gate[0], w_up[0], w_down[0], rows, step_blocks
    )

    def give_back(parts):
        parts = parts.reshape(devices * tok, width)
        parts = lax.psum_scatter(parts, "blk", scatter_dimension=0, tiled=True)
        return lax.psum_scatter(parts, "head", scatter_dimension=0, tiled=True)

    grad_normed_two = give_back(dx_parts).astype(F32)
    expert_sum = give_back(moe_parts).astype(F32)

    xr, er = xr.reshape(-1, width), er.reshape(-1, width)
    hid, dgp, dup = [v.reshape(-1, v.shape[-1]) for v in (hid, dgp, dup)]
    grad_down = mm(hid, er, TN)[None]
    grad_gate = mm(xr, dgp, TN)[None]
    grad_up = mm(xr, dup, TN)[None]

    result = middle + expert_sum
    gained_two = grad_normed_two * ffn_gain
    ffn_gain_part = jnp.sum(grad_normed_two * middle * inv_two, 0)
    grad_middle = (
        grad_y
        + inv_two * gained_two
        - middle * inv_two * inv_two * inv_two * jnp.mean(gained_two * middle, -1, keepdims=True)
    )
    grad_branch = grad_middle.astype(BF16)
    grad_group = lax.all_gather(grad_branch, "head", axis=0, tiled=True)
    grad_attended = mm(grad_group, out_w, NT).astype(BF16)
    out_part = mm(attended, grad_group, TN)
    grad_heads = swap(to_items(grad_attended)).reshape(blk_count * per, BLOCK, HEAD_DIM)
    grad_qkv = attend_backward(
        starts, own, qkv, grad_heads, heads_out_t, log_total, scale, share
    ).reshape(blk_count, 3, span, HEAD_DIM)
    grad_qkv = swap(grad_qkv)
    grad_query_n = rounded(from_items(grad_qkv[:, 0]))
    grad_key_n = rounded(from_items(grad_qkv[:, 1]))
    grad_value_b = from_items(grad_qkv[:, 2]).astype(BF16)
    gained_query = grad_query_n * gain_query
    gained_key = grad_key_n * gain_key
    row_sums = lax.psum(
        jnp.stack([jnp.sum(gained_query * query_raw, -1), jnp.sum(gained_key * key_raw, -1)]),
        "head",
    )
    grad_query_b = (
        inv_query * gained_query
        - query_raw * inv_query * inv_query * inv_query * row_sums[0][:, None] / width
    ).astype(BF16)
    grad_key_b = (
        inv_key * gained_key
        - key_raw * inv_key * inv_key * inv_key * row_sums[1][:, None] / width
    ).astype(BF16)
    query_gain_part = jnp.sum(grad_query_n * query_raw * inv_query, 0)
    key_gain_part = jnp.sum(grad_key_n * key_raw * inv_key, 0)
    total = (
        mm(grad_query_b, query_cols, NT)
        + mm(grad_key_b, key_cols, NT)
        + mm(grad_value_b, value_cols, NT)
    )
    grad_normed = rounded(
        lax.psum_scatter(total.astype(BF16), "head", scatter_dimension=0, tiled=True).astype(F32)
    )
    query_part = mm(group, grad_query_b, TN)
    key_part = mm(group, grad_key_b, TN)
    value_part = mm(group, grad_value_b, TN)
    gained_one = grad_normed * attn_gain
    attn_gain_part = jnp.sum(grad_normed * hidden_f * inv_one, 0)
    grad_hidden_in = (
        grad_middle
        + inv_one * gained_one
        - hidden_f
        * inv_one
        * inv_one
        * inv_one
        * jnp.mean(gained_one * hidden_f, -1, keepdims=True)
    )

    def over_blk(values, dim):
        return lax.psum_scatter(
            values.astype(BF16), "blk", scatter_dimension=dim, tiled=True
        ).astype(F32)

    grad_query = over_blk(query_part, 0)
    grad_key = over_blk(key_part, 0)
    grad_value = over_blk(value_part, 0)
    grad_out = over_blk(out_part, 1)
    zero_width = jnp.zeros((width,), F32)
    query_gain_full = lax.dynamic_update_slice_in_dim(
        zero_width, query_gain_part, head_index * columns, 0
    )
    key_gain_full = lax.dynamic_update_slice_in_dim(
        zero_width, key_gain_part, head_index * columns, 0
    )
    square_parts = jnp.stack(
        [jnp.sum(result * result), jnp.sum(branch * branch), jnp.sum(expert_sum * expert_sum)]
    )
    totals = lax.psum(
        (square_parts, attn_gain_part, ffn_gain_part, query_gain_full, key_gain_full),
        everyone,
    )
    entry_count = tok * width * devices
    stream_stats = jnp.sqrt(totals[0] / entry_count + EPSILON)
    return (
        out_rows(result.astype(BF16)),
        out_rows(grad_hidden_in.astype(BF16)),
        totals[1],
        grad_query,
        grad_key,
        grad_value,
        totals[3],
        totals[4],
        grad_out,
        totals[2],
        grad_gate,
        grad_up,
        grad_down,
        stream_stats,
    )


def solution(mesh):
    rows3 = P(("blk", "head"), None, None)
    placed = (
        rows3, P(), P("blk", "head"), P("blk", "head"), P("blk", "head"), P(), P(),
        P("head", "blk"), P(), rows3, rows3, rows3, rows3, rows3, P(), rows3,
    )
    return jax.shard_map(
        local,
        mesh=mesh,
        in_specs=placed,
        out_specs=(
            rows3, rows3, P(), P("blk", "head"), P("blk", "head"), P("blk", "head"), P(), P(),
            P("head", "blk"), P(), rows3, rows3, rows3, P(),
        ),
        check_vma=False,
    )
```

```python
import functools
import math

import jax
import jax.numpy as jnp
from jax import lax
from jax.experimental import pallas as pl
from jax.experimental.pallas import tpu as pltpu
from jax.sharding import PartitionSpec as P

HEAD_DIM = 128
BLOCK = 256
EPSILON = 1e-06
F32 = jnp.float32
BF16 = jnp.bfloat16
VMEM_BYTES = 58 * 1024 * 1024

NN = (((1,), (0,)), ((), ()))
NT = (((1,), (1,)), ((), ()))
TN = (((0,), (0,)), ((), ()))


def mm(left, right, dims=NN):
    return lax.dot_general(left, right, dims, preferred_element_type=F32)


def rounded(values):
    return lax.optimization_barrier(values.astype(BF16)).astype(F32)


def inverse_rms(values):
    return lax.rsqrt(jnp.mean(values * values, axis=-1, keepdims=True) + EPSILON)


def nearest(here, rank, count):
    below = here
    above = count - 1 - here
    swing = jnp.where(rank % 2 == 1, here - (rank + 1) // 2, here + rank // 2)
    far = jnp.where(below < above, rank, count - 1 - rank)
    return jnp.where(rank <= 2 * jnp.minimum(below, above), swing, far)


def greet(peers):
    barrier = pltpu.get_barrier_semaphore()
    count = 0
    for device, condition in peers:

        def signal(device=device):
            pl.semaphore_signal(
                barrier, inc=1, device_id=device, device_id_type=pl.DeviceIdType.MESH
            )

        if condition is None:
            signal()
            count = count + 1
        else:
            pl.when(condition)(signal)
            count = count + jnp.where(condition, 1, 0)
    pl.semaphore_wait(barrier, count)


class Relay:
    def __init__(self, arrays, nz, ny, send_sem, recv_sem):
        self.arrays, self.nz, self.ny = arrays, nz, ny
        self.send_sem, self.recv_sem = send_sem, recv_sem
        head, blk = lax.axis_index("head"), lax.axis_index("blk")
        self.x, self.y = x, y = head % 2, head // 2
        self.core, self.z = core, z = blk % 2, blk // 2

        def device(z_at, y_at, core_at):
            return {"blk": z_at * 2 + core_at, "head": y_at * 2 + x}

        self.sibling = device(z, y, 1 - core)
        self.targets = [
            self.sibling, device(z, y + 1, core), device(z, y - 1, core),
            device(z + 1, y, core), device(z - 1, y, core),
        ]
        self.present = [None, y < ny - 1, y > 0, z < nz - 1, z > 0]
        self.pieces = []
        for n, (own, everything, parts) in enumerate(arrays):
            rows = own.shape[0] // parts
            for part in range(parts):
                self.pieces.append((n, pl.ds(part * rows, rows)))

    @staticmethod
    def when(condition, work):
        if condition is None:
            work()
        else:
            pl.when(condition)(work)

    def peers(self):
        return list(zip(self.targets, self.present))

    def conditions(self, z_at, y_at):
        column = y_at == self.y
        there = self.present
        return [
            None, (y_at <= self.y) & there[1], (y_at >= self.y) & there[2],
            column & (z_at <= self.z) & there[3], column & (z_at >= self.z) & there[4],
        ]

    def copy(self, z_at, y_at, core_at, piece, way, own=False):
        n, here = self.pieces[piece]
        everything = self.arrays[n][1]
        place = everything.at[z_at, core_at, y_at, here]
        return pltpu.make_async_remote_copy(
            src_ref=self.arrays[n][0].at[here] if own else place,
            dst_ref=place,
            send_sem=self.send_sem.at[way, z_at * self.ny + y_at, piece],
            recv_sem=self.recv_sem.at[core_at, z_at * self.ny + y_at, piece],
            device_id=self.targets[way],
            device_id_type=pl.DeviceIdType.MESH,
        )

    def start(self):
        for piece in range(len(self.pieces)):
            for way in (3, 4, 1, 2, 0):
                self.when(self.present[way], lambda way=way, piece=piece: self.copy(
                    self.z, self.y, self.core, piece, way, own=True).start())

    def keep(self, stages, sems):
        loads = [
            pltpu.make_async_copy(own, stage, sems.at[n])
            for n, ((own, _, _), stage) in enumerate(zip(self.arrays, stages))
        ]
        for copy in loads:
            copy.start()
        for copy in loads:
            copy.wait()
        stores = [
            pltpu.make_async_copy(stage, everything.at[self.z, self.core, self.y], sems.at[n])
            for n, ((_, everything, _), stage) in enumerate(zip(self.arrays, stages))
        ]
        for copy in stores:
            copy.start()
        return stores

    def arrived(self, z_at, y_at, core_at):
        for piece in range(len(self.pieces)):
            self.copy(z_at, y_at, core_at, piece, 0).wait_recv()

    def pass_on(self, z_at, y_at):
        for piece in range(len(self.pieces)):
            self.copy(z_at, y_at, self.core, piece, 0).wait_recv()
            for way, condition in enumerate(self.conditions(z_at, y_at)):
                self.when(condition, lambda way=way, piece=piece: self.copy(
                    z_at, y_at, self.core, piece, way).start())

    def pass_on_z(self, away):
        pl.when(self.z - away >= 0)(lambda: self.pass_on(self.z - away, self.y))
        pl.when(self.z + away < self.nz)(lambda: self.pass_on(self.z + away, self.y))

    def drain(self):
        def one(index, carry):
            z_at, y_at = index // self.ny, index % self.ny
            for way, condition in enumerate(self.conditions(z_at, y_at)):
                for piece in range(len(self.pieces)):
                    self.when(condition, lambda way=way, piece=piece: self.copy(
                        z_at, y_at, self.core, piece, way).wait_send())
            return carry

        lax.fori_loop(0, self.nz * self.ny, one, 0)


class Swap:
    def __init__(self, pairs, send_sem, recv_sem):
        head, blk = lax.axis_index("head"), lax.axis_index("blk")
        self.neighbour = {"blk": blk, "head": head + 1 - 2 * (head % 2)}
        self.copies = [
            pltpu.make_async_remote_copy(
                src_ref=source,
                dst_ref=target,
                send_sem=send_sem.at[n],
                recv_sem=recv_sem.at[n],
                device_id=self.neighbour,
                device_id_type=pl.DeviceIdType.MESH,
            )
            for n, (source, target) in enumerate(pairs)
        ]

    def peers(self):
        return [(self.neighbour, None)]

    def start(self):
        for copy in self.copies:
            copy.start()

    def wait(self):
        for copy in self.copies:
            copy.wait()


class Return:
    parts = 2

    @classmethod
    def scratch(cls, nz, tok, width):
        return [
            pltpu.VMEM((nz, tok, width), BF16),
            pltpu.VMEM((nz, tok, width), BF16),
            pltpu.VMEM((2, nz, tok, width), BF16),
            pltpu.SemaphoreType.DMA((nz, cls.parts)),
            pltpu.SemaphoreType.DMA((nz, cls.parts)),
            pltpu.SemaphoreType.DMA((nz, cls.parts)),
            pltpu.SemaphoreType.DMA((nz, cls.parts)),
            pltpu.SemaphoreType.DMA((2, nz, cls.parts)),
        ]

    def __init__(self, share_ref, out_ref, scratch):
        self.share_ref, self.out_ref = share_ref, out_ref
        (
            self.mine, self.from_y, self.from_z,
            self.mine_sem, self.y_send, self.y_recv, self.z_send, self.z_recv,
        ) = scratch
        self.nz, _, tok, _ = share_ref.shape
        self.piece = tok // self.parts
        self.step_rows = min(64, self.piece)
        head, blk = lax.axis_index("head"), lax.axis_index("blk")
        x, self.y, self.z = head % 2, head // 2, blk // 2
        self.beside = {"blk": blk, "head": (1 - self.y) * 2 + x}
        self.onward = [{"blk": blk + 2, "head": head}, {"blk": blk - 2, "head": head}]
        self.has = [self.z > 0, self.z < self.nz - 1]
        self.targets = [nearest(self.z, rank, self.nz) for rank in reversed(range(self.nz))]

    def peers(self):
        return [(self.beside, None), (self.onward[1], self.has[0]), (self.onward[0], self.has[1])]

    def cut(self, part):
        return pl.ds(part * self.piece, self.piece)

    def own_copy(self, target, part):
        return pltpu.make_async_copy(
            self.share_ref.at[target, self.y, self.cut(part)],
            self.mine.at[target, self.cut(part)],
            self.mine_sem.at[target, part],
        )

    def y_copy(self, target, part):
        return pltpu.make_async_remote_copy(
            src_ref=self.share_ref.at[target, 1 - self.y, self.cut(part)],
            dst_ref=self.from_y.at[target, self.cut(part)],
            send_sem=self.y_send.at[target, part],
            recv_sem=self.y_recv.at[target, part],
            device_id=self.beside,
            device_id_type=pl.DeviceIdType.MESH,
        )

    def z_copy(self, way, target, part):
        return pltpu.make_async_remote_copy(
            src_ref=self.mine.at[target, self.cut(part)],
            dst_ref=self.from_z.at[way, target, self.cut(part)],
            send_sem=self.z_send.at[target, part],
            recv_sem=self.z_recv.at[way, target, part],
            device_id=self.onward[way],
            device_id_type=pl.DeviceIdType.MESH,
        )

    def start(self):
        for target in self.targets:
            for part in range(self.parts):
                self.y_copy(target, part).start()
                self.own_copy(target, part).start()

    def add(self, target, part, ways, out=None):
        for r in range(part * self.piece, (part + 1) * self.piece, self.step_rows):
            here = pl.ds(r, self.step_rows)
            total = self.mine[target, here, :].astype(F32) + self.from_y[target, here, :].astype(F32)
            for way in ways:
                total = total + self.from_z[way, target, here, :].astype(F32)
            if out is None:
                self.mine[target, here, :] = total.astype(BF16)
            else:
                out[here, :] = total.astype(BF16)

    def send(self, turn):
        target = self.targets[turn]
        for part in range(self.parts):
            self.own_copy(target, part).wait()
            self.y_copy(target, part).wait_recv()
            for way in range(2):
                going = target > self.z if way == 0 else target < self.z

                @pl.when(going & self.has[way])
                def _(way=way, part=part):
                    self.z_copy(way, target, part).wait_recv()
                    self.add(target, part, (way,))

                @pl.when(going & jnp.logical_not(self.has[way]))
                def _(part=part):
                    self.add(target, part, ())

                @pl.when(going)
                def _(way=way, part=part):
                    self.z_copy(way, target, part).start()

    def finish(self):
        z, has = self.z, self.has
        for part in range(self.parts):
            self.own_copy(z, part).wait()
            self.y_copy(z, part).wait_recv()
            for way in range(2):
                pl.when(has[way])(lambda way=way, part=part: self.z_copy(way, z, part).wait_recv())
            for condition, ways in (
                (has[0] & has[1], (0, 1)),
                (has[0] & jnp.logical_not(has[1]), (0,)),
                (jnp.logical_not(has[0]) & has[1], (1,)),
            ):
                pl.when(condition)(
                    lambda ways=ways, part=part: self.add(z, part, ways, self.out_ref)
                )
        for target in self.targets:
            for part in range(self.parts):
                self.y_copy(target, part).wait_send()
        for target in self.targets[:-1]:
            for part in range(self.parts):
                self.z_copy(0, target, part).wait_send()


def attend_forward(bias, qkv, cots, table, swaps, nz, ny, scale, share, collective_id):
    src, _, per, block, dim = qkv.shape
    blocks = src * per
    parts = 2
    events = [blocks * 5 // 8, blocks * 7 // 8]

    count = len(swaps)

    def kernel(bias_ref, qkv_ref, cot_ref, table_ref, *refs):
        swap_in, refs = refs[:count], refs[count:]
        out_ref, out_t_ref, lse_ref, cots_ref, tables_ref, *refs = refs
        swap_out, refs = refs[:count], refs[count:]
        (
            vt_ref, cot_stage, table_stage, send_sem, recv_sem, own_sem, swap_send, swap_recv,
        ) = refs
        swap = Swap(list(zip(swap_in, swap_out)), swap_send, swap_recv)
        relay = Relay(
            [(cot_ref, cots_ref, parts), (table_ref, tables_ref, 1)], nz, ny, send_sem, recv_sem
        )
        greet(relay.peers() + swap.peers())
        relay.start()
        swap.start()
        kept = relay.keep((cot_stage, table_stage), own_sem)

        def flip(j, carry):
            vt_ref[j] = qkv_ref[j // per, 2, j % per].astype(F32).T.astype(BF16)
            return carry

        lax.fori_loop(0, blocks, flip, 0)
        own = lax.axis_index("blk") % share

        def query_block(step, carry):
            for n, event in enumerate(events):
                if n + 1 < nz:
                    pl.when(step == event)(lambda n=n: relay.pass_on_z(n + 1))

            def work():
                query = qkv_ref[step // per, 0, step % per]

                def body(j, carry):
                    top, total, acc = carry
                    scores = mm(qkv_ref[j // per, 1, j % per], query, NT) * scale
                    scores = scores + bias_ref[step * blocks + j]
                    new_top = jnp.maximum(top, jnp.max(scores, axis=0, keepdims=True))
                    weights = jnp.exp(scores - new_top)
                    shrink = jnp.exp(top - new_top)
                    total = total * shrink + jnp.sum(weights, axis=0, keepdims=True)
                    acc = acc * shrink + mm(vt_ref[j], weights.astype(BF16))
                    return new_top, total, acc

                top, total, acc = lax.fori_loop(
                    0,
                    step + 1,
                    body,
                    (
                        jnp.full((1, block), -1e30, F32),
                        jnp.zeros((1, block), F32),
                        jnp.zeros((dim, block), F32),
                    ),
                )
                result = acc / total
                out_t_ref[step] = result
                out_ref[step] = result.T.astype(BF16)
                lse_ref[step] = top + jnp.log(total)

            if share == 1:
                work()
            else:
                mine = step % share == own
                pl.when(mine)(work)

                @pl.when(jnp.logical_not(mine))
                def _():
                    out_t_ref[step] = jnp.zeros((dim, block), F32)
                    out_ref[step] = jnp.zeros((block, dim), BF16)
                    lse_ref[step] = jnp.zeros((1, block), F32)

            return carry

        lax.fori_loop(0, blocks, query_block, 0)
        for away in range(len(events) + 1, nz):
            relay.pass_on_z(away)
        for turn in range(1, ny):
            for rank in range(nz):
                relay.pass_on(nearest(relay.z, rank, nz), nearest(relay.y, turn, ny))

        def from_sibling(index, carry):
            relay.arrived(index // ny, index % ny, 1 - relay.core)
            return carry

        lax.fori_loop(0, nz * ny, from_sibling, 0)
        relay.drain()
        swap.wait()
        for copy in kept:
            copy.wait()

    anywhere = pl.BlockSpec(memory_space=pl.ANY)
    inside = pl.BlockSpec(memory_space=pltpu.VMEM)
    return pl.pallas_call(
        kernel,
        in_specs=[pl.BlockSpec(memory_space=pltpu.SMEM), inside, anywhere, anywhere]
        + [anywhere] * count,
        out_specs=[inside] * 3 + [anywhere] * (2 + count),
        out_shape=[
            jax.ShapeDtypeStruct((blocks, block, dim), BF16),
            jax.ShapeDtypeStruct((blocks, dim, block), F32),
            jax.ShapeDtypeStruct((blocks, 1, block), F32),
            jax.ShapeDtypeStruct((nz, 2, ny) + cots.shape, cots.dtype),
            jax.ShapeDtypeStruct((nz, 2, ny) + table.shape, table.dtype),
        ]
        + [jax.ShapeDtypeStruct(v.shape, v.dtype) for v in swaps],
        scratch_shapes=[
            pltpu.VMEM((blocks, dim, block), BF16),
            pltpu.VMEM(cots.shape, cots.dtype),
            pltpu.VMEM(table.shape, table.dtype),
            pltpu.SemaphoreType.DMA((5, nz * ny, parts + 1)),
            pltpu.SemaphoreType.DMA((2, nz * ny, parts + 1)),
            pltpu.SemaphoreType.DMA((2,)),
            pltpu.SemaphoreType.DMA((count,)),
            pltpu.SemaphoreType.DMA((count,)),
        ],
        compiler_params=pltpu.CompilerParams(
            collective_id=collective_id, has_side_effects=True, vmem_limit_bytes=VMEM_BYTES
        ),
        name="attend_forward",
    )(bias, qkv, cots, table, *swaps)


def attend_backward(bias, qkv, grad_out, out_t, lse, swaps, shares, scale, share, collective_id):
    src, _, per, block, dim = qkv.shape
    blocks = src * per
    count = len(swaps)
    events = [blocks * 9 // 16, blocks * 13 // 16]

    def kernel(bias_ref, qkv_ref, go_ref, out_t_ref, lse_ref, *refs):
        swap_in, refs = refs[:count], refs[count:]
        share_ref, refs = refs[: len(shares)], refs[len(shares) :]
        grad_ref, *refs = refs
        swap_out, refs = refs[:count], refs[count:]
        sum_ref, refs = refs[: len(shares)], refs[len(shares) :]
        dk_ref, dv_ref, swap_send, swap_recv, *refs = refs
        swap = Swap(list(zip(swap_in, swap_out)), swap_send, swap_recv)
        back = Return(share_ref[0], sum_ref[0], refs) if shares else None
        greet(swap.peers() + (back.peers() if back else []))
        if back:
            back.start()
        swap.start()
        dk_ref[...] = jnp.zeros_like(dk_ref)
        dv_ref[...] = jnp.zeros_like(dv_ref)
        own = lax.axis_index("blk") % share

        def query_block(step, carry):
            for n, event in enumerate(events):
                if back and n < back.nz - 1:
                    pl.when(step == event)(lambda n=n: back.send(n))

            def work():
                query = qkv_ref[step // per, 0, step % per]
                go = go_ref[step]
                delta = jnp.sum(go.astype(F32).T * out_t_ref[step], axis=0, keepdims=True)
                log_total = lse_ref[step]

                def body(j, dq):
                    key = qkv_ref[j // per, 1, j % per]
                    value = qkv_ref[j // per, 2, j % per]
                    scores = mm(key, query, NT) * scale + bias_ref[step * blocks + j]
                    probs = jnp.exp(scores - log_total)
                    grad_scores = (probs * (mm(value, go, NT) - delta)).astype(BF16)
                    dv_ref[j] += mm(probs.astype(BF16), go)
                    dk_ref[j] += mm(grad_scores, query)
                    return dq + mm(grad_scores, key, TN)

                dq = lax.fori_loop(0, step + 1, body, jnp.zeros((block, dim), F32))
                grad_ref[step // per, 0, step % per] = (dq * scale).astype(BF16)

            if share == 1:
                work()
            else:
                mine = step % share == own
                pl.when(mine)(work)

                @pl.when(jnp.logical_not(mine))
                def _():
                    grad_ref[step // per, 0, step % per] = jnp.zeros((block, dim), BF16)

            return carry

        lax.fori_loop(0, blocks, query_block, 0)
        if back:
            for turn in range(len(events), back.nz - 1):
                back.send(turn)

        def store(j, carry):
            grad_ref[j // per, 1, j % per] = (dk_ref[j] * scale).astype(BF16)
            grad_ref[j // per, 2, j % per] = dv_ref[j].astype(BF16)
            return carry

        lax.fori_loop(0, blocks, store, 0)
        if back:
            back.finish()
        swap.wait()

    anywhere = pl.BlockSpec(memory_space=pl.ANY)
    inside = pl.BlockSpec(memory_space=pltpu.VMEM)
    nz, _, tok, width = shares[0].shape if shares else (0, 0, 0, 0)
    out = pl.pallas_call(
        kernel,
        in_specs=[pl.BlockSpec(memory_space=pltpu.SMEM)] + [inside] * 4
        + [anywhere] * (count + len(shares)),
        out_specs=[inside] + [anywhere] * count + [inside] * len(shares),
        out_shape=[jax.ShapeDtypeStruct(qkv.shape, BF16)]
        + [jax.ShapeDtypeStruct(v.shape, v.dtype) for v in swaps]
        + [jax.ShapeDtypeStruct((tok, width), BF16)] * len(shares),
        scratch_shapes=[
            pltpu.VMEM((blocks, block, dim), F32),
            pltpu.VMEM((blocks, block, dim), F32),
            pltpu.SemaphoreType.DMA((count,)),
            pltpu.SemaphoreType.DMA((count,)),
        ]
        + (Return.scratch(nz, tok, width) if shares else []),
        compiler_params=pltpu.CompilerParams(
            collective_id=collective_id, has_side_effects=True, vmem_limit_bytes=VMEM_BYTES
        ),
        name="attend_backward",
    )(bias, qkv, grad_out, out_t, lse, *swaps, *shares)
    return out[0], out[1 : 1 + count], out[1 + count :]


def expert_exchange(tokens, cots, slots, gates, weights, nh, nb, rows, collective_id):
    tok, width = tokens.shape
    half = weights[0].shape[1]
    nz, ny = nb // 2, nh // 2
    steps = nz * ny
    count = 2 * rows
    parts = 2
    chunk = min(512, width)
    full = 2 * half

    def kernel(own_ref, slot_ref, gate_ref, cot_ref, *refs):
        weight_refs = refs[0:6]
        *sum_refs, xr_out, er_out, hid_out, dpre_out, all_ref = refs[6:13]
        (
            in_w, down_w, tok_buf, cot_buf, xr, er, hid, dpre, keep, give, got,
            send_sem, recv_sem, weight_sem, tok_sem, cot_sem, row_sem, sum_sem, give_sem, got_sem, free_sem,
        ) = refs[13:]
        relay = Relay([(own_ref, all_ref, parts)], nz, ny, send_sem, recv_sem)
        y, core, z, sibling = relay.y, relay.core, relay.z, relay.sibling
        weight_copies = [
            pltpu.make_async_copy(ref, place, weight_sem.at[n])
            for n, (ref, place) in enumerate(zip(
                weight_refs,
                [in_w.at[:, pl.ds(n * half, half)] for n in range(4)]
                + [down_w.at[pl.ds(n * half, half)] for n in range(2)],
            ))
        ]
        for copy in weight_copies:
            copy.start()
        greet(relay.peers())
        relay.start()

        lanes = lax.broadcasted_iota(jnp.int32, (rows, tok), 0)

        def places(step):
            return nearest(z, step // ny, nz), nearest(y, step % ny, ny)

        def row_copies(step, slot):
            return [
                pltpu.make_async_copy(buf.at[slot], out.at[step], row_sem.at[slot, n])
                for n, (buf, out) in enumerate(
                    ((xr, xr_out), (er, er_out), (hid, hid_out), (dpre, dpre_out))
                )
            ]

        def sum_copies(step, slot):
            z_at, y_at = places(step)
            return [
                pltpu.make_async_copy(keep.at[slot, n], sum_refs[n].at[z_at, y_at], sum_sem.at[slot, n])
                for n in range(2)
            ]

        def give_copies(slot):
            return [
                pltpu.make_async_remote_copy(
                    src_ref=give.at[slot, n],
                    dst_ref=got.at[slot, n],
                    send_sem=give_sem.at[slot, n],
                    recv_sem=got_sem.at[slot, n],
                    device_id=sibling,
                    device_id_type=pl.DeviceIdType.MESH,
                )
                for n in range(2)
            ]

        def finish(step, slot):
            for n, copy in enumerate(give_copies(slot)):
                copy.wait_recv()
                for r in range(0, tok, 64):
                    here = pl.ds(r, 64)
                    keep[slot, n, here, :] = (
                        keep[slot, n, here, :].astype(F32) + got[slot, n, here, :].astype(F32)
                    ).astype(BF16)
            for copy in sum_copies(step, slot):
                copy.start()
            pl.semaphore_signal(free_sem, inc=1, device_id=sibling, device_id_type=pl.DeviceIdType.MESH)

        def block_copies(step, source, buffer, sems):
            z_at, y_at = places(step)
            return [
                pltpu.make_async_copy(source.at[z_at, c, y_at], buffer.at[n], sems.at[n])
                for n, c in enumerate((core, 1 - core))
            ]

        def cot_copies(step):
            return block_copies(step, cot_ref, cot_buf, cot_sem)

        def tok_copies(step):
            return block_copies(step, all_ref, tok_buf, tok_sem)

        def load_cots(step):
            for copy in cot_copies(step):
                copy.start()

        def load_tokens(step):
            z_at, y_at = places(step)
            z_rank, y_rank = step // ny, step % ny

            @pl.when(y_rank > 0)
            def _():
                relay.pass_on(z_at, y_at)

            for away in range(1, nz):

                @pl.when((y_rank == ny - 1) & (z_rank + 1 == away))
                def _(away=away):
                    relay.pass_on_z(away)

            relay.arrived(z_at, y_at, 1 - core)
            if isinstance(step, int):
                pltpu.make_async_copy(own_ref, tok_buf.at[0], tok_sem.at[0]).start()
                pltpu.make_async_copy(all_ref.at[z, 1 - core, y], tok_buf.at[1], tok_sem.at[1]).start()
                return
            for copy in tok_copies(step):
                copy.start()

        load_cots(0)
        load_tokens(0)
        for copy in weight_copies:
            copy.wait()

        def body(step, carry):
            z_at, y_at = places(step)
            slot = step % 2
            cores = (core, 1 - core)

            @pl.when(step >= 2)
            def _():
                for copy in row_copies(step - 2, slot):
                    copy.wait()
                for copy in sum_copies(step - 2, slot):
                    copy.wait()
                for copy in give_copies(slot):
                    copy.wait_send()

            for copy in tok_copies(step):
                copy.wait()
            picks = []
            scale_by = []
            for n, c in enumerate(cores):
                hit = lanes == slot_ref[z_at, c, y_at]
                picks.append(jnp.where(hit, 1.0, 0.0).astype(BF16))
                scale_by.append(
                    jnp.sum(jnp.where(hit, gate_ref[z_at, c, y_at], 0.0), axis=1, keepdims=True)
                )
                here = slice(n * rows, (n + 1) * rows)
                for col in range(0, width, chunk):
                    cols = slice(col, col + chunk)
                    xr[slot, here, cols] = mm(picks[n], tok_buf[n, :, cols]).astype(BF16)
            for copy in cot_copies(step):
                copy.wait()
            for n in range(2):
                here = slice(n * rows, (n + 1) * rows)
                for col in range(0, width, chunk):
                    cols = slice(col, col + chunk)
                    er[slot, here, cols] = (
                        scale_by[n] * mm(picks[n], cot_buf[n, :, cols])
                    ).astype(BF16)

            @pl.when(step + 1 < steps)
            def _():
                load_cots(step + 1)

            for m in range(0, full, half):
                gate_cols, up_cols = slice(m, m + half), slice(full + m, full + m + half)
                gate_pre = mm(xr[slot], in_w[:, gate_cols])
                up_pre = mm(xr[slot], in_w[:, up_cols])
                sig = jax.nn.sigmoid(gate_pre)
                act = gate_pre * sig
                hid[slot, :, gate_cols] = (act * up_pre).astype(BF16)
                dhid = mm(er[slot], down_w[gate_cols, :], NT).astype(BF16).astype(F32)
                dpre[slot, :, gate_cols] = (
                    dhid * up_pre * sig * (1.0 + gate_pre * (1.0 - sig))
                ).astype(BF16)
                dpre[slot, :, up_cols] = (dhid * act).astype(BF16)
            for copy in row_copies(step, slot):
                copy.start()
            for col in range(0, width, chunk):
                if col == width - chunk:

                    @pl.when(step + 1 < steps)
                    def _():
                        load_tokens(step + 1)

                cols = slice(col, col + chunk)
                part_sum = mm(hid[slot], down_w[:, cols])
                drow = mm(dpre[slot], in_w[cols, :], NT).astype(BF16)
                for n, dest in enumerate((keep, give)):
                    here = slice(n * rows, (n + 1) * rows)
                    dest[slot, 0, :, cols] = mm(picks[n], drow[here], TN).astype(BF16)
                    scaled = (part_sum[here] * scale_by[n]).astype(BF16)
                    dest[slot, 1, :, cols] = mm(picks[n], scaled, TN).astype(BF16)

            @pl.when(step >= 2)
            def _():
                pl.semaphore_wait(free_sem, 1)

            for copy in give_copies(slot):
                copy.start()

            @pl.when(step >= 1)
            def _():
                finish(step - 1, 1 - slot)

            return carry

        lax.fori_loop(0, steps, body, 0)
        last = (steps - 1) % 2
        finish(steps - 1, last)
        for step in (steps - 2, steps - 1):
            slot = step % 2
            for copy in row_copies(step, slot):
                copy.wait()
            for copy in sum_copies(step, slot):
                copy.wait()
            for copy in give_copies(slot):
                copy.wait_send()
        pl.semaphore_wait(free_sem, 2)

        relay.drain()

    anywhere = pl.BlockSpec(memory_space=pl.ANY)
    inside = pl.BlockSpec(memory_space=pltpu.VMEM)
    out = pl.pallas_call(
        kernel,
        in_specs=[anywhere, inside, inside] + [anywhere] * 7,
        out_specs=[anywhere] * 7,
        out_shape=[
            jax.ShapeDtypeStruct((nz, ny, tok, width), BF16),
            jax.ShapeDtypeStruct((nz, ny, tok, width), BF16),
            jax.ShapeDtypeStruct((steps, count, width), BF16),
            jax.ShapeDtypeStruct((steps, count, width), BF16),
            jax.ShapeDtypeStruct((steps, count, full), BF16),
            jax.ShapeDtypeStruct((steps, count, 2 * full), BF16),
            jax.ShapeDtypeStruct((nz, 2, ny, tok, width), BF16),
        ],
        scratch_shapes=[
            pltpu.VMEM((width, 2 * full), BF16),
            pltpu.VMEM((full, width), BF16),
            pltpu.VMEM((2, tok, width), BF16),
            pltpu.VMEM((2, tok, width), BF16),
            pltpu.VMEM((2, count, width), BF16),
            pltpu.VMEM((2, count, width), BF16),
            pltpu.VMEM((2, count, full), BF16),
            pltpu.VMEM((2, count, 2 * full), BF16),
            pltpu.VMEM((2, 2, tok, width), BF16),
            pltpu.VMEM((2, 2, tok, width), BF16),
            pltpu.VMEM((2, 2, tok, width), BF16),
            pltpu.SemaphoreType.DMA((5, steps, parts)),
            pltpu.SemaphoreType.DMA((2, steps, parts)),
            pltpu.SemaphoreType.DMA((6,)),
            pltpu.SemaphoreType.DMA((2,)),
            pltpu.SemaphoreType.DMA((2,)),
            pltpu.SemaphoreType.DMA((2, 4)),
            pltpu.SemaphoreType.DMA((2, 2)),
            pltpu.SemaphoreType.DMA((2, 2)),
            pltpu.SemaphoreType.DMA((2, 2)),
            pltpu.SemaphoreType.REGULAR,
        ],
        compiler_params=pltpu.CompilerParams(
            collective_id=collective_id, has_side_effects=True, vmem_limit_bytes=VMEM_BYTES
        ),
        name="expert_exchange",
    )(tokens, slots, gates, cots, *weights)
    return out[:6]


def return_sum(shares, collective_id):
    nz, ny, tok, width = shares.shape
    assert ny == 2

    def kernel(share_ref, out_ref, *scratch):
        back = Return(share_ref, out_ref, scratch)
        greet(back.peers())
        back.start()
        for turn in range(nz - 1):
            back.send(turn)
        back.finish()

    return pl.pallas_call(
        kernel,
        in_specs=[pl.BlockSpec(memory_space=pl.ANY)],
        out_specs=pl.BlockSpec(memory_space=pltpu.VMEM),
        out_shape=jax.ShapeDtypeStruct((tok, width), BF16),
        scratch_shapes=Return.scratch(nz, tok, width),
        compiler_params=pltpu.CompilerParams(
            collective_id=collective_id, has_side_effects=True, vmem_limit_bytes=VMEM_BYTES
        ),
        name="return_sum",
    )(shares)


def local(
    hidden_in,
    attn_gain,
    w_query,
    w_key,
    w_value,
    query_gain,
    key_gain,
    w_out,
    ffn_gain,
    w_gate,
    w_up,
    w_down,
    routes,
    gate_weights,
    block_starts,
    cotangent,
):
    head_count = lax.axis_size("head")
    blk_count = lax.axis_size("blk")
    head_index = lax.axis_index("head")
    blk_index = lax.axis_index("blk")
    piece, seqs, width = hidden_in.shape
    span = piece * head_count
    per = span // BLOCK
    columns = w_query.shape[1]
    heads_here = columns // HEAD_DIM
    top_count = routes.shape[2]
    experts = blk_count * head_count // 2
    devices = blk_count * head_count
    tok = piece * seqs
    capacity = max(2, 5 * tok * top_count // (4 * experts))
    rows = -(-capacity // 32) * 32
    items = seqs * heads_here
    share = blk_count // items
    scale = 1.0 / math.sqrt(HEAD_DIM)
    everyone = ("blk", "head")

    def own_rows(values):
        return values.transpose(1, 0, 2).reshape(tok, values.shape[2])

    def out_rows(values):
        return values.reshape(seqs, piece, width).transpose(1, 0, 2)

    nz, ny = blk_count // 2, head_count // 2

    def flip_head(values, bit):
        return lax.ppermute(values, "head", [(h, h ^ bit) for h in range(head_count)])

    def flip_blk(values, bit):
        return lax.ppermute(values, "blk", [(b, b ^ bit) for b in range(blk_count)])

    gate_other = flip_head(w_gate[0], 1)

    table = jnp.concatenate([own_rows(routes).astype(F32).T, own_rows(gate_weights).T], axis=0)

    hidden_f = own_rows(hidden_in).astype(F32)
    grad_y_b = own_rows(cotangent)
    grad_y = grad_y_b.astype(F32)

    inv_one = inverse_rms(hidden_f)
    normed = (hidden_f * inv_one * attn_gain).astype(BF16)
    group = lax.all_gather(normed, "head", axis=0, tiled=True)
    query_cols = lax.all_gather(w_query, "blk", axis=0, tiled=True)
    key_cols = lax.all_gather(w_key, "blk", axis=0, tiled=True)
    value_cols = lax.all_gather(w_value, "blk", axis=0, tiled=True)
    out_w = lax.all_gather(w_out, "blk", axis=1, tiled=True)

    query_raw = mm(group, query_cols)
    key_raw = mm(group, key_cols)
    value_raw = mm(group, value_cols)
    square_sums = lax.psum(
        jnp.stack([jnp.sum(query_raw * query_raw, -1), jnp.sum(key_raw * key_raw, -1)]), "head"
    )
    inv_query = lax.rsqrt(square_sums[0][:, None] / width + EPSILON)
    inv_key = lax.rsqrt(square_sums[1][:, None] / width + EPSILON)
    gain_query = lax.dynamic_slice_in_dim(query_gain, head_index * columns, columns)
    gain_key = lax.dynamic_slice_in_dim(key_gain, head_index * columns, columns)
    query_n = (query_raw * inv_query * gain_query).astype(BF16)
    key_n = (key_raw * inv_key * gain_key).astype(BF16)
    value_n = value_raw.astype(BF16)

    def to_items(values):
        parts = values.reshape(head_count, seqs, piece, heads_here, HEAD_DIM)
        parts = parts.transpose(1, 3, 0, 2, 4).reshape(items, span, HEAD_DIM)
        return jnp.repeat(parts, share, axis=0) if share > 1 else parts

    def from_items(values):
        if share > 1:
            values = values.reshape(items, share, span, HEAD_DIM).astype(F32).sum(1)
        parts = values.reshape(seqs, heads_here, head_count, piece, HEAD_DIM)
        return parts.transpose(2, 0, 3, 1, 4).reshape(head_count * tok, columns)

    def swap(values):
        return lax.all_to_all(values, "blk", split_axis=0, concat_axis=0, tiled=True)

    item = blk_index // share
    starts = lax.dynamic_index_in_dim(block_starts, item // heads_here, 0, keepdims=False)
    qkv = jnp.stack([to_items(query_n), to_items(key_n), to_items(value_n)], axis=1)
    qkv, gate_other = lax.optimization_barrier((qkv, gate_other))
    qkv = swap(qkv)
    qkv = qkv.reshape(blk_count, 3, per, BLOCK, HEAD_DIM)
    total_blocks = blk_count * per
    key_block = jnp.arange(total_blocks, dtype=jnp.int32)
    bias = jnp.where(key_block[None, :] >= starts[:, None], 0.0, -1e30).astype(F32).reshape(-1)
    heads_out, heads_out_t, log_total, all_cots, tables, up_other, down_other = attend_forward(
        bias, qkv, grad_y_b, table, (w_up[0], w_down[0]), nz, ny, scale, share, 2
    )
    expert_weights = (w_gate[0], gate_other, w_up[0], up_other, w_down[0], down_other)

    expert = (blk_index * head_count + head_index) // 2
    named = tables[..., :top_count, :] == expert.astype(F32)
    hit = jnp.any(named, axis=-2)
    gates = jnp.sum(jnp.where(named, tables[..., top_count:, :], 0.0), axis=-2)[..., None, :]
    before = jnp.triu(jnp.ones((tok, tok), BF16), 1)
    ranks = jnp.dot(
        hit.reshape(-1, tok).astype(BF16), before, preferred_element_type=F32
    ).astype(jnp.int32)
    slots = jnp.where(hit, ranks.reshape(hit.shape), -1)[..., None, :]

    attended = from_items(swap(heads_out.reshape(blk_count, span, HEAD_DIM))).astype(BF16)
    branch = lax.psum_scatter(
        mm(attended, out_w).astype(BF16), "head", scatter_dimension=0, tiled=True
    ).astype(F32)
    middle = hidden_f + branch
    inv_two = inverse_rms(middle)
    normed_two = (middle * inv_two * ffn_gain).astype(BF16)

    dx_share, moe_share, xr, er, hid, dpre = expert_exchange(
        normed_two, all_cots, slots, gates, expert_weights, head_count, blk_count, rows, 0
    )

    def halvings(count):
        return [1 << i for i in reversed(range(count.bit_length() - 1))]

    def halve(values, flip, bit, mine):
        pair = values.reshape((2, values.shape[0] // 2) + values.shape[1:])
        kept = lax.dynamic_index_in_dim(pair, mine, 0, keepdims=False)
        sent = lax.dynamic_index_in_dim(pair, 1 - mine, 0, keepdims=False)
        return kept, flip(sent.astype(BF16), bit)

    y_bits = [(flip_head, 2 * b, (head_index // (2 * b)) % 2) for b in halvings(ny)]
    z_bits = [(flip_blk, 2 * b, (blk_index // (2 * b)) % 2) for b in halvings(nz)]

    def give_back(values, bits):
        for flip, bit, mine in bits:
            kept, came = halve(values, flip, bit, mine)
            values = kept.astype(F32) + came.astype(F32)
        return values[0]

    if ny == 2:
        grad_normed_two = return_sum(dx_share, 1)
    else:
        grad_normed_two = give_back(dx_share.swapaxes(0, 1), y_bits)
        grad_normed_two = give_back(grad_normed_two, z_bits).astype(BF16)
    grad_normed_two, moe_share = lax.optimization_barrier((grad_normed_two, moe_share))
    grad_normed_two = grad_normed_two.astype(F32)
    xr, er = xr.reshape(-1, width), er.reshape(-1, width)
    hid, dpre = [v.reshape(-1, v.shape[-1]) for v in (hid, dpre)]
    half = w_gate.shape[2]
    dgate, dgate_other, dup, dup_other = [dpre[:, n * half : (n + 1) * half] for n in range(4)]

    halves = [
        mm(hid[:, :half], er, TN), mm(xr, dgate, TN), mm(xr, dup, TN),
        mm(hid[:, half:], er, TN), mm(xr, dgate_other, TN), mm(xr, dup_other, TN),
    ]
    gained_two = grad_normed_two * ffn_gain
    ffn_gain_part = jnp.sum(grad_normed_two * middle * inv_two, 0)
    grad_middle = (
        grad_y
        + inv_two * gained_two
        - middle * inv_two * inv_two * inv_two * jnp.mean(gained_two * middle, -1, keepdims=True)
    )
    grad_branch = grad_middle.astype(BF16)
    grad_group = lax.all_gather(grad_branch, "head", axis=0, tiled=True)
    grad_group, *halves = lax.optimization_barrier((grad_group, *halves))
    others = [v.astype(BF16) for v in halves[3:]]
    grad_attended = mm(grad_group, out_w, NT).astype(BF16)
    out_part = mm(attended, grad_group, TN)
    grad_heads = swap(to_items(grad_attended)).reshape(blk_count * per, BLOCK, HEAD_DIM)
    own_sum = ny == 2
    grad_qkv, others[1:], sums = attend_backward(
        bias, qkv, grad_heads, heads_out_t, log_total, others[1:], [moe_share] * own_sum,
        scale, share, 3,
    )
    others[0] = flip_head(others[0], 1)
    grad_qkv = swap(grad_qkv.reshape(blk_count, 3, span, HEAD_DIM))
    grad_qkv, others[0] = lax.optimization_barrier((grad_qkv, others[0]))
    grad_down, grad_gate, grad_up = [
        (mine + other.astype(F32))[None] for mine, other in zip(halves[:3], others)
    ]
    if own_sum:
        expert_sum = sums[0].astype(F32)
    else:
        expert_sum = give_back(give_back(moe_share.swapaxes(0, 1), y_bits), z_bits)
    result = middle + expert_sum
    grad_query_n = rounded(from_items(grad_qkv[:, 0]))
    grad_key_n = rounded(from_items(grad_qkv[:, 1]))
    grad_value_b = from_items(grad_qkv[:, 2]).astype(BF16)
    gained_query = grad_query_n * gain_query
    gained_key = grad_key_n * gain_key
    row_sums = lax.psum(
        jnp.stack([jnp.sum(gained_query * query_raw, -1), jnp.sum(gained_key * key_raw, -1)]),
        "head",
    )
    grad_query_b = (
        inv_query * gained_query
        - query_raw * inv_query * inv_query * inv_query * row_sums[0][:, None] / width
    ).astype(BF16)
    grad_key_b = (
        inv_key * gained_key
        - key_raw * inv_key * inv_key * inv_key * row_sums[1][:, None] / width
    ).astype(BF16)
    query_gain_part = jnp.sum(grad_query_n * query_raw * inv_query, 0)
    key_gain_part = jnp.sum(grad_key_n * key_raw * inv_key, 0)
    total = (
        mm(grad_query_b, query_cols, NT)
        + mm(grad_key_b, key_cols, NT)
        + mm(grad_value_b, value_cols, NT)
    )
    grad_normed = rounded(
        lax.psum_scatter(total.astype(BF16), "head", scatter_dimension=0, tiled=True).astype(F32)
    )
    query_part = mm(group, grad_query_b, TN)
    key_part = mm(group, grad_key_b, TN)
    value_part = mm(group, grad_value_b, TN)
    gained_one = grad_normed * attn_gain
    attn_gain_part = jnp.sum(grad_normed * hidden_f * inv_one, 0)
    grad_hidden_in = (
        grad_middle
        + inv_one * gained_one
        - hidden_f
        * inv_one
        * inv_one
        * inv_one
        * jnp.mean(gained_one * hidden_f, -1, keepdims=True)
    )

    def over_blk(values, dim):
        return lax.psum_scatter(
            values.astype(BF16), "blk", scatter_dimension=dim, tiled=True
        ).astype(F32)

    grad_query = over_blk(query_part, 0)
    grad_key = over_blk(key_part, 0)
    grad_value = over_blk(value_part, 0)
    grad_out = over_blk(out_part, 1)
    zero_width = jnp.zeros((width,), F32)
    query_gain_full = lax.dynamic_update_slice_in_dim(
        zero_width, query_gain_part, head_index * columns, 0
    )
    key_gain_full = lax.dynamic_update_slice_in_dim(
        zero_width, key_gain_part, head_index * columns, 0
    )
    square_parts = jnp.stack(
        [jnp.sum(result * result), jnp.sum(branch * branch), jnp.sum(expert_sum * expert_sum)]
    )
    totals = lax.psum(
        (square_parts, attn_gain_part, ffn_gain_part, query_gain_full, key_gain_full),
        everyone,
    )
    entry_count = tok * width * devices
    stream_stats = jnp.sqrt(totals[0] / entry_count + EPSILON)
    return (
        out_rows(result.astype(BF16)),
        out_rows(grad_hidden_in.astype(BF16)),
        totals[1],
        grad_query,
        grad_key,
        grad_value,
        totals[3],
        totals[4],
        grad_out,
        totals[2],
        grad_gate,
        grad_up,
        grad_down,
        stream_stats,
    )


def solution(mesh):
    rows3 = P(("blk", "head"), None, None)
    placed = (
        rows3, P(), P("blk", "head"), P("blk", "head"), P("blk", "head"), P(), P(),
        P("head", "blk"), P(), rows3, rows3, rows3, rows3, rows3, P(), rows3,
    )
    return jax.shard_map(
        local,
        mesh=mesh,
        in_specs=placed,
        out_specs=(
            rows3, rows3, P(), P("blk", "head"), P("blk", "head"), P("blk", "head"), P(), P(),
            P("head", "blk"), P(), rows3, rows3, rows3, P(),
        ),
        check_vma=False,
    )
```

```python
import functools
import math

import jax
import jax.numpy as jnp
from jax import lax
from jax.experimental import pallas as pl
from jax.experimental.pallas import tpu as pltpu
from jax.sharding import PartitionSpec as P

HEAD_DIM = 128
BLOCK = 256
EPSILON = 1e-06
F32 = jnp.float32
BF16 = jnp.bfloat16
VMEM_BYTES = 58 * 1024 * 1024

NN = (((1,), (0,)), ((), ()))
NT = (((1,), (1,)), ((), ()))
TN = (((0,), (0,)), ((), ()))


def mm(left, right, dims=NN):
    return lax.dot_general(left, right, dims, preferred_element_type=F32)


def rounded(values):
    return lax.optimization_barrier(values.astype(BF16)).astype(F32)


def inverse_rms(values):
    return lax.rsqrt(jnp.mean(values * values, axis=-1, keepdims=True) + EPSILON)


def nearest(here, rank, count):
    below = here
    above = count - 1 - here
    swing = jnp.where(rank % 2 == 1, here - (rank + 1) // 2, here + rank // 2)
    far = jnp.where(below < above, rank, count - 1 - rank)
    return jnp.where(rank <= 2 * jnp.minimum(below, above), swing, far)


def greet(peers):
    barrier = pltpu.get_barrier_semaphore()
    count = 0
    for device, condition in peers:

        def signal(device=device):
            pl.semaphore_signal(
                barrier, inc=1, device_id=device, device_id_type=pl.DeviceIdType.MESH
            )

        if condition is None:
            signal()
            count = count + 1
        else:
            pl.when(condition)(signal)
            count = count + jnp.where(condition, 1, 0)
    pl.semaphore_wait(barrier, count)


class Relay:
    def __init__(self, arrays, nz, ny, send_sem, recv_sem, spread_y=True):
        self.arrays, self.nz, self.ny = arrays, nz, ny
        self.send_sem, self.recv_sem = send_sem, recv_sem
        head, blk = lax.axis_index("head"), lax.axis_index("blk")
        x, y = head % 2, head // 2 if spread_y else 0
        self.y = y
        self.core, self.z = core, z = blk % 2, blk // 2

        def device(z_at, y_at, core_at):
            return {"blk": z_at * 2 + core_at, "head": y_at * 2 + x if spread_y else head}

        self.sibling = device(z, y, 1 - core)
        self.targets = [
            self.sibling, device(z, y + 1, core), device(z, y - 1, core),
            device(z + 1, y, core), device(z - 1, y, core),
        ]
        self.present = [None, y < ny - 1, y > 0, z < nz - 1, z > 0]
        self.ways = range(5) if spread_y else (0, 3, 4)
        self.pieces = []
        for n, (own, everything, parts) in enumerate(arrays):
            rows = own.shape[0] // parts
            for part in range(parts):
                self.pieces.append((n, pl.ds(part * rows, rows)))

    @staticmethod
    def when(condition, work):
        if condition is None:
            work()
        else:
            pl.when(condition)(work)

    def peers(self):
        return list(zip(self.targets, self.present))

    def conditions(self, z_at, y_at):
        column = y_at == self.y
        there = self.present
        return [
            None, (y_at <= self.y) & there[1], (y_at >= self.y) & there[2],
            column & (z_at <= self.z) & there[3], column & (z_at >= self.z) & there[4],
        ]

    def copy(self, z_at, y_at, core_at, piece, way, own=False):
        n, here = self.pieces[piece]
        everything = self.arrays[n][1]
        place = everything.at[z_at, core_at, y_at, here]
        return pltpu.make_async_remote_copy(
            src_ref=self.arrays[n][0].at[here] if own else place,
            dst_ref=place,
            send_sem=self.send_sem.at[way, z_at * self.ny + y_at, piece],
            recv_sem=self.recv_sem.at[core_at, z_at * self.ny + y_at, piece],
            device_id=self.targets[way],
            device_id_type=pl.DeviceIdType.MESH,
        )

    def start(self):
        for piece in range(len(self.pieces)):
            for way in reversed(self.ways):
                self.when(self.present[way], lambda way=way, piece=piece: self.copy(
                    self.z, self.y, self.core, piece, way, own=True).start())

    def keep(self, stages, sems):
        loads = [
            pltpu.make_async_copy(own, stage, sems.at[n])
            for n, ((own, _, _), stage) in enumerate(zip(self.arrays, stages))
        ]
        for copy in loads:
            copy.start()
        for copy in loads:
            copy.wait()
        stores = [
            pltpu.make_async_copy(stage, everything.at[self.z, self.core, self.y], sems.at[n])
            for n, ((_, everything, _), stage) in enumerate(zip(self.arrays, stages))
        ]
        for copy in stores:
            copy.start()
        return stores

    def arrived(self, z_at, y_at, core_at):
        for piece in range(len(self.pieces)):
            self.copy(z_at, y_at, core_at, piece, 0).wait_recv()

    def pass_on(self, z_at, y_at):
        for piece in range(len(self.pieces)):
            self.copy(z_at, y_at, self.core, piece, 0).wait_recv()
            conditions = self.conditions(z_at, y_at)
            for way in self.ways:
                self.when(conditions[way], lambda way=way, piece=piece: self.copy(
                    z_at, y_at, self.core, piece, way).start())

    def pass_on_z(self, away):
        pl.when(self.z - away >= 0)(lambda: self.pass_on(self.z - away, self.y))
        pl.when(self.z + away < self.nz)(lambda: self.pass_on(self.z + away, self.y))

    def drain(self):
        def one(index, carry):
            z_at, y_at = index // self.ny, index % self.ny
            conditions = self.conditions(z_at, y_at)
            for way in self.ways:
                for piece in range(len(self.pieces)):
                    self.when(conditions[way], lambda way=way, piece=piece: self.copy(
                        z_at, y_at, self.core, piece, way).wait_send())
            return carry

        lax.fori_loop(0, self.nz * self.ny, one, 0)


class Swap:
    def __init__(self, pairs, send_sem, recv_sem):
        head, blk = lax.axis_index("head"), lax.axis_index("blk")
        self.neighbour = {"blk": blk, "head": head + 1 - 2 * (head % 2)}
        self.copies = [
            pltpu.make_async_remote_copy(
                src_ref=source,
                dst_ref=target,
                send_sem=send_sem.at[n],
                recv_sem=recv_sem.at[n],
                device_id=self.neighbour,
                device_id_type=pl.DeviceIdType.MESH,
            )
            for n, (source, target) in enumerate(pairs)
        ]

    def peers(self):
        return [(self.neighbour, None)]

    def start(self):
        for copy in self.copies:
            copy.start()

    def wait(self):
        for copy in self.copies:
            copy.wait()


class Return:
    parts = 2

    @classmethod
    def scratch(cls, nz, tok, width):
        return [
            pltpu.VMEM((nz, tok, width), BF16),
            pltpu.VMEM((nz, tok, width), BF16),
            pltpu.VMEM((2, nz, tok, width), BF16),
            pltpu.SemaphoreType.DMA((nz, cls.parts)),
            pltpu.SemaphoreType.DMA((nz, cls.parts)),
            pltpu.SemaphoreType.DMA((nz, cls.parts)),
            pltpu.SemaphoreType.DMA((nz, cls.parts)),
            pltpu.SemaphoreType.DMA((2, nz, cls.parts)),
        ]

    def __init__(self, share_ref, out_ref, scratch):
        self.share_ref, self.out_ref = share_ref, out_ref
        (
            self.mine, self.from_y, self.from_z,
            self.mine_sem, self.y_send, self.y_recv, self.z_send, self.z_recv,
        ) = scratch
        self.nz, tok = self.mine.shape[:2]
        self.piece = tok // self.parts
        self.step_rows = min(64, self.piece)
        head, blk = lax.axis_index("head"), lax.axis_index("blk")
        x, self.y, self.z = head % 2, head // 2, blk // 2
        self.beside = {"blk": blk, "head": (1 - self.y) * 2 + x}
        self.onward = [{"blk": blk + 2, "head": head}, {"blk": blk - 2, "head": head}]
        self.has = [self.z > 0, self.z < self.nz - 1]
        self.targets = [nearest(self.z, rank, self.nz) for rank in reversed(range(self.nz))]

    def peers(self):
        return [(self.beside, None), (self.onward[1], self.has[0]), (self.onward[0], self.has[1])]

    def cut(self, part):
        return pl.ds(part * self.piece, self.piece)

    def own_copy(self, target, part):
        return pltpu.make_async_copy(
            self.share_ref.at[target, self.y, self.cut(part)],
            self.mine.at[target, self.cut(part)],
            self.mine_sem.at[target, part],
        )

    def own_wait(self, target, part):
        self.own_copy(target, part).wait()

    def y_copy(self, target, part):
        return pltpu.make_async_remote_copy(
            src_ref=self.share_ref.at[target, 1 - self.y, self.cut(part)],
            dst_ref=self.from_y.at[target, self.cut(part)],
            send_sem=self.y_send.at[target, part],
            recv_sem=self.y_recv.at[target, part],
            device_id=self.beside,
            device_id_type=pl.DeviceIdType.MESH,
        )

    def z_copy(self, way, target, part):
        return pltpu.make_async_remote_copy(
            src_ref=self.mine.at[target, self.cut(part)],
            dst_ref=self.from_z.at[way, target, self.cut(part)],
            send_sem=self.z_send.at[target, part],
            recv_sem=self.z_recv.at[way, target, part],
            device_id=self.onward[way],
            device_id_type=pl.DeviceIdType.MESH,
        )

    def start(self):
        for target in self.targets:
            for part in range(self.parts):
                self.y_copy(target, part).start()
                self.own_copy(target, part).start()

    def add(self, target, part, ways, out=None):
        for r in range(part * self.piece, (part + 1) * self.piece, self.step_rows):
            here = pl.ds(r, self.step_rows)
            total = self.mine[target, here, :].astype(F32) + self.from_y[target, here, :].astype(F32)
            for way in ways:
                total = total + self.from_z[way, target, here, :].astype(F32)
            if out is None:
                self.mine[target, here, :] = total.astype(BF16)
            else:
                self.store(out, here, total)

    def store(self, out, here, total):
        out[here, :] = total.astype(out.dtype)

    def send(self, turn):
        target = self.targets[turn]
        for part in range(self.parts):
            self.own_wait(target, part)
            self.y_copy(target, part).wait_recv()
            for way in range(2):
                going = target > self.z if way == 0 else target < self.z

                @pl.when(going & self.has[way])
                def _(way=way, part=part):
                    self.z_copy(way, target, part).wait_recv()
                    self.add(target, part, (way,))

                @pl.when(going & jnp.logical_not(self.has[way]))
                def _(part=part):
                    self.add(target, part, ())

                @pl.when(going)
                def _(way=way, part=part):
                    self.z_copy(way, target, part).start()

    def finish(self):
        z, has = self.z, self.has
        for part in range(self.parts):
            self.own_wait(z, part)
            self.y_copy(z, part).wait_recv()
            for way in range(2):
                pl.when(has[way])(lambda way=way, part=part: self.z_copy(way, z, part).wait_recv())
            for condition, ways in (
                (has[0] & has[1], (0, 1)),
                (has[0] & jnp.logical_not(has[1]), (0,)),
                (jnp.logical_not(has[0]) & has[1], (1,)),
            ):
                pl.when(condition)(
                    lambda ways=ways, part=part: self.add(z, part, ways, self.out_ref)
                )
        for target in self.targets:
            for part in range(self.parts):
                self.y_copy(target, part).wait_send()
        for target in self.targets[:-1]:
            for part in range(self.parts):
                self.z_copy(0, target, part).wait_send()


class TileReturn(Return):
    def __init__(self, give_ref, out_refs, scratch):
        super().__init__(give_ref, out_refs, scratch)
        blk = lax.axis_index("blk")
        self.core = blk % 2
        self.beside = {"blk": blk + 1 - 2 * self.core, "head": lax.axis_index("head")}

    @classmethod
    def scratch(cls, nz, tok, width):
        return [pltpu.VMEM((nz, tok, width), BF16)] + super().scratch(nz, tok, width)

    def own_copy(self, target, part):
        return None

    def own_wait(self, target, part):
        pass

    def y_copy(self, target, part):
        return pltpu.make_async_remote_copy(
            src_ref=self.share_ref.at[target, self.cut(part)],
            dst_ref=self.from_y.at[target, self.cut(part)],
            send_sem=self.y_send.at[target, part],
            recv_sem=self.y_recv.at[target, part],
            device_id=self.beside,
            device_id_type=pl.DeviceIdType.MESH,
        )

    def store(self, out, here, total):
        size = total.shape[1] // len(out)
        for n, ref in enumerate(out):
            ref[here, :] = total[:, n * size : (n + 1) * size]


def attend_forward(bias, qkv, cots, table, swaps, nz, ny, scale, share, collective_id):
    src, _, per, block, dim = qkv.shape
    blocks = src * per
    parts = 2
    events = [blocks * 5 // 8, blocks * 7 // 8]

    count = len(swaps)

    def kernel(bias_ref, qkv_ref, cot_ref, table_ref, *refs):
        swap_in, refs = refs[:count], refs[count:]
        out_ref, out_t_ref, lse_ref, cots_ref, tables_ref, *refs = refs
        swap_out, refs = refs[:count], refs[count:]
        (
            vt_ref, cot_stage, table_stage, send_sem, recv_sem, own_sem, swap_send, swap_recv,
        ) = refs
        swap = Swap(list(zip(swap_in, swap_out)), swap_send, swap_recv)
        relay = Relay(
            [(cot_ref, cots_ref, parts), (table_ref, tables_ref, 1)], nz, ny, send_sem, recv_sem
        )
        greet(relay.peers() + swap.peers())
        relay.start()
        swap.start()
        kept = relay.keep((cot_stage, table_stage), own_sem)

        def flip(j, carry):
            vt_ref[j] = qkv_ref[j // per, 2, j % per].astype(F32).T.astype(BF16)
            return carry

        lax.fori_loop(0, blocks, flip, 0)
        own = lax.axis_index("blk") % share

        def query_block(step, carry):
            for n, event in enumerate(events):
                if n + 1 < nz:
                    pl.when(step == event)(lambda n=n: relay.pass_on_z(n + 1))

            def work():
                query = qkv_ref[step // per, 0, step % per]

                def body(j, carry):
                    top, total, acc = carry
                    scores = mm(qkv_ref[j // per, 1, j % per], query, NT) * scale
                    scores = scores + bias_ref[step * blocks + j]
                    new_top = jnp.maximum(top, jnp.max(scores, axis=0, keepdims=True))
                    weights = jnp.exp(scores - new_top)
                    shrink = jnp.exp(top - new_top)
                    total = total * shrink + jnp.sum(weights, axis=0, keepdims=True)
                    acc = acc * shrink + mm(vt_ref[j], weights.astype(BF16))
                    return new_top, total, acc

                top, total, acc = lax.fori_loop(
                    0,
                    step + 1,
                    body,
                    (
                        jnp.full((1, block), -1e30, F32),
                        jnp.zeros((1, block), F32),
                        jnp.zeros((dim, block), F32),
                    ),
                )
                result = acc / total
                out_t_ref[step] = result
                out_ref[step] = result.T.astype(BF16)
                lse_ref[step] = top + jnp.log(total)

            if share == 1:
                work()
            else:
                mine = step % share == own
                pl.when(mine)(work)

                @pl.when(jnp.logical_not(mine))
                def _():
                    out_t_ref[step] = jnp.zeros((dim, block), F32)
                    out_ref[step] = jnp.zeros((block, dim), BF16)
                    lse_ref[step] = jnp.zeros((1, block), F32)

            return carry

        lax.fori_loop(0, blocks, query_block, 0)
        for away in range(len(events) + 1, nz):
            relay.pass_on_z(away)
        for turn in range(1, ny):
            for rank in range(nz):
                relay.pass_on(nearest(relay.z, rank, nz), nearest(relay.y, turn, ny))

        def from_sibling(index, carry):
            relay.arrived(index // ny, index % ny, 1 - relay.core)
            return carry

        lax.fori_loop(0, nz * ny, from_sibling, 0)
        relay.drain()
        swap.wait()
        for copy in kept:
            copy.wait()

    anywhere = pl.BlockSpec(memory_space=pl.ANY)
    inside = pl.BlockSpec(memory_space=pltpu.VMEM)
    return pl.pallas_call(
        kernel,
        in_specs=[pl.BlockSpec(memory_space=pltpu.SMEM), inside, anywhere, anywhere]
        + [anywhere] * count,
        out_specs=[inside] * 3 + [anywhere] * (2 + count),
        out_shape=[
            jax.ShapeDtypeStruct((blocks, block, dim), BF16),
            jax.ShapeDtypeStruct((blocks, dim, block), F32),
            jax.ShapeDtypeStruct((blocks, 1, block), F32),
            jax.ShapeDtypeStruct((nz, 2, ny) + cots.shape, cots.dtype),
            jax.ShapeDtypeStruct((nz, 2, ny) + table.shape, table.dtype),
        ]
        + [jax.ShapeDtypeStruct(v.shape, v.dtype) for v in swaps],
        scratch_shapes=[
            pltpu.VMEM((blocks, dim, block), BF16),
            pltpu.VMEM(cots.shape, cots.dtype),
            pltpu.VMEM(table.shape, table.dtype),
            pltpu.SemaphoreType.DMA((5, nz * ny, parts + 1)),
            pltpu.SemaphoreType.DMA((2, nz * ny, parts + 1)),
            pltpu.SemaphoreType.DMA((2,)),
            pltpu.SemaphoreType.DMA((count,)),
            pltpu.SemaphoreType.DMA((count,)),
        ],
        compiler_params=pltpu.CompilerParams(
            collective_id=collective_id, has_side_effects=True, vmem_limit_bytes=VMEM_BYTES
        ),
        name="attend_forward",
    )(bias, qkv, cots, table, *swaps)


def attend_backward(bias, qkv, grad_out, out_t, lse, swaps, shares, scale, share, collective_id):
    src, _, per, block, dim = qkv.shape
    blocks = src * per
    count = len(swaps)
    events = [blocks * 9 // 16, blocks * 13 // 16]

    def kernel(bias_ref, qkv_ref, go_ref, out_t_ref, lse_ref, *refs):
        swap_in, refs = refs[:count], refs[count:]
        share_ref, refs = refs[: len(shares)], refs[len(shares) :]
        grad_ref, *refs = refs
        swap_out, refs = refs[:count], refs[count:]
        sum_ref, refs = refs[: len(shares)], refs[len(shares) :]
        dk_ref, dv_ref, swap_send, swap_recv, *refs = refs
        swap = Swap(list(zip(swap_in, swap_out)), swap_send, swap_recv)
        back = Return(share_ref[0], sum_ref[0], refs) if shares else None
        greet(swap.peers() + (back.peers() if back else []))
        if back:
            back.start()
        swap.start()
        dk_ref[...] = jnp.zeros_like(dk_ref)
        dv_ref[...] = jnp.zeros_like(dv_ref)
        own = lax.axis_index("blk") % share

        def query_block(step, carry):
            for n, event in enumerate(events):
                if back and n < back.nz - 1:
                    pl.when(step == event)(lambda n=n: back.send(n))

            def work():
                query = qkv_ref[step // per, 0, step % per]
                go = go_ref[step]
                delta = jnp.sum(go.astype(F32).T * out_t_ref[step], axis=0, keepdims=True)
                log_total = lse_ref[step]

                def body(j, dq):
                    key = qkv_ref[j // per, 1, j % per]
                    value = qkv_ref[j // per, 2, j % per]
                    scores = mm(key, query, NT) * scale + bias_ref[step * blocks + j]
                    probs = jnp.exp(scores - log_total)
                    grad_scores = (probs * (mm(value, go, NT) - delta)).astype(BF16)
                    dv_ref[j] += mm(probs.astype(BF16), go)
                    dk_ref[j] += mm(grad_scores, query)
                    return dq + mm(grad_scores, key, TN)

                dq = lax.fori_loop(0, step + 1, body, jnp.zeros((block, dim), F32))
                grad_ref[step // per, 0, step % per] = (dq * scale).astype(BF16)

            if share == 1:
                work()
            else:
                mine = step % share == own
                pl.when(mine)(work)

                @pl.when(jnp.logical_not(mine))
                def _():
                    grad_ref[step // per, 0, step % per] = jnp.zeros((block, dim), BF16)

            return carry

        lax.fori_loop(0, blocks, query_block, 0)
        if back:
            for turn in range(len(events), back.nz - 1):
                back.send(turn)

        def store(j, carry):
            grad_ref[j // per, 1, j % per] = (dk_ref[j] * scale).astype(BF16)
            grad_ref[j // per, 2, j % per] = dv_ref[j].astype(BF16)
            return carry

        lax.fori_loop(0, blocks, store, 0)
        if back:
            back.finish()
        swap.wait()

    anywhere = pl.BlockSpec(memory_space=pl.ANY)
    inside = pl.BlockSpec(memory_space=pltpu.VMEM)
    nz, _, tok, width = shares[0].shape if shares else (0, 0, 0, 0)
    out = pl.pallas_call(
        kernel,
        in_specs=[pl.BlockSpec(memory_space=pltpu.SMEM)] + [inside] * 4
        + [anywhere] * (count + len(shares)),
        out_specs=[inside] + [anywhere] * count + [inside] * len(shares),
        out_shape=[jax.ShapeDtypeStruct(qkv.shape, BF16)]
        + [jax.ShapeDtypeStruct(v.shape, v.dtype) for v in swaps]
        + [jax.ShapeDtypeStruct((tok, width), BF16)] * len(shares),
        scratch_shapes=[
            pltpu.VMEM((blocks, block, dim), F32),
            pltpu.VMEM((blocks, block, dim), F32),
            pltpu.SemaphoreType.DMA((count,)),
            pltpu.SemaphoreType.DMA((count,)),
        ]
        + (Return.scratch(nz, tok, width) if shares else []),
        compiler_params=pltpu.CompilerParams(
            collective_id=collective_id, has_side_effects=True, vmem_limit_bytes=VMEM_BYTES
        ),
        name="attend_backward",
    )(bias, qkv, grad_out, out_t, lse, *swaps, *shares)
    return out[0], out[1 : 1 + count], out[1 + count :]


def expert_exchange(tokens, cots, slots, gates, weights, nh, nb, rows, collective_id):
    tok, width = tokens.shape
    half = weights[0].shape[1]
    nz, ny = nb // 2, nh // 2
    steps = nz * ny
    count = 2 * rows
    parts = 2
    chunk = min(512, width)
    full = 2 * half

    def kernel(own_ref, slot_ref, gate_ref, cot_ref, *refs):
        weight_refs = refs[0:6]
        *sum_refs, xr_out, er_out, hid_out, dpre_out, all_ref = refs[6:13]
        (
            in_w, down_w, tok_buf, cot_buf, xr, er, hid, dpre, keep, give, got,
            send_sem, recv_sem, weight_sem, tok_sem, cot_sem, row_sem, sum_sem, give_sem, got_sem, free_sem,
        ) = refs[13:]
        relay = Relay([(own_ref, all_ref, parts)], nz, ny, send_sem, recv_sem)
        y, core, z, sibling = relay.y, relay.core, relay.z, relay.sibling
        weight_copies = [
            pltpu.make_async_copy(ref, place, weight_sem.at[n])
            for n, (ref, place) in enumerate(zip(
                weight_refs,
                [in_w.at[:, pl.ds(n * half, half)] for n in range(4)]
                + [down_w.at[pl.ds(n * half, half)] for n in range(2)],
            ))
        ]
        for copy in weight_copies:
            copy.start()
        greet(relay.peers())
        relay.start()

        lanes = lax.broadcasted_iota(jnp.int32, (rows, tok), 0)

        def places(step):
            return nearest(z, step // ny, nz), nearest(y, step % ny, ny)

        def row_copies(step, slot):
            return [
                pltpu.make_async_copy(buf.at[slot], out.at[step], row_sem.at[slot, n])
                for n, (buf, out) in enumerate(
                    ((xr, xr_out), (er, er_out), (hid, hid_out), (dpre, dpre_out))
                )
            ]

        def sum_copies(step, slot):
            z_at, y_at = places(step)
            return [
                pltpu.make_async_copy(keep.at[slot, n], sum_refs[n].at[z_at, y_at], sum_sem.at[slot, n])
                for n in range(2)
            ]

        def give_copies(slot):
            return [
                pltpu.make_async_remote_copy(
                    src_ref=give.at[slot, n],
                    dst_ref=got.at[slot, n],
                    send_sem=give_sem.at[slot, n],
                    recv_sem=got_sem.at[slot, n],
                    device_id=sibling,
                    device_id_type=pl.DeviceIdType.MESH,
                )
                for n in range(2)
            ]

        def finish(step, slot):
            for n, copy in enumerate(give_copies(slot)):
                copy.wait_recv()
                for r in range(0, tok, 64):
                    here = pl.ds(r, 64)
                    keep[slot, n, here, :] = (
                        keep[slot, n, here, :].astype(F32) + got[slot, n, here, :].astype(F32)
                    ).astype(BF16)
            for copy in sum_copies(step, slot):
                copy.start()
            pl.semaphore_signal(free_sem, inc=1, device_id=sibling, device_id_type=pl.DeviceIdType.MESH)

        def block_copies(step, source, buffer, sems):
            z_at, y_at = places(step)
            return [
                pltpu.make_async_copy(source.at[z_at, c, y_at], buffer.at[n], sems.at[n])
                for n, c in enumerate((core, 1 - core))
            ]

        def cot_copies(step):
            return block_copies(step, cot_ref, cot_buf, cot_sem)

        def tok_copies(step):
            return block_copies(step, all_ref, tok_buf, tok_sem)

        def load_cots(step):
            for copy in cot_copies(step):
                copy.start()

        def load_tokens(step):
            z_at, y_at = places(step)
            z_rank, y_rank = step // ny, step % ny

            @pl.when(y_rank > 0)
            def _():
                relay.pass_on(z_at, y_at)

            for away in range(1, nz):

                @pl.when((y_rank == ny - 1) & (z_rank + 1 == away))
                def _(away=away):
                    relay.pass_on_z(away)

            relay.arrived(z_at, y_at, 1 - core)
            if isinstance(step, int):
                pltpu.make_async_copy(own_ref, tok_buf.at[0], tok_sem.at[0]).start()
                pltpu.make_async_copy(all_ref.at[z, 1 - core, y], tok_buf.at[1], tok_sem.at[1]).start()
                return
            for copy in tok_copies(step):
                copy.start()

        load_cots(0)
        load_tokens(0)
        for copy in weight_copies:
            copy.wait()

        def body(step, carry):
            z_at, y_at = places(step)
            slot = step % 2
            cores = (core, 1 - core)

            @pl.when(step >= 2)
            def _():
                for copy in row_copies(step - 2, slot):
                    copy.wait()
                for copy in sum_copies(step - 2, slot):
                    copy.wait()
                for copy in give_copies(slot):
                    copy.wait_send()

            for copy in tok_copies(step):
                copy.wait()
            picks = []
            scale_by = []
            for n, c in enumerate(cores):
                hit = lanes == slot_ref[z_at, c, y_at]
                picks.append(jnp.where(hit, 1.0, 0.0).astype(BF16))
                scale_by.append(
                    jnp.sum(jnp.where(hit, gate_ref[z_at, c, y_at], 0.0), axis=1, keepdims=True)
                )
                here = slice(n * rows, (n + 1) * rows)
                for col in range(0, width, chunk):
                    cols = slice(col, col + chunk)
                    xr[slot, here, cols] = mm(picks[n], tok_buf[n, :, cols]).astype(BF16)
            for copy in cot_copies(step):
                copy.wait()
            for n in range(2):
                here = slice(n * rows, (n + 1) * rows)
                for col in range(0, width, chunk):
                    cols = slice(col, col + chunk)
                    er[slot, here, cols] = (
                        scale_by[n] * mm(picks[n], cot_buf[n, :, cols])
                    ).astype(BF16)

            @pl.when(step + 1 < steps)
            def _():
                load_cots(step + 1)

            for m in range(0, full, half):
                gate_cols, up_cols = slice(m, m + half), slice(full + m, full + m + half)
                gate_pre = mm(xr[slot], in_w[:, gate_cols])
                up_pre = mm(xr[slot], in_w[:, up_cols])
                sig = jax.nn.sigmoid(gate_pre)
                act = gate_pre * sig
                hid[slot, :, gate_cols] = (act * up_pre).astype(BF16)
                dhid = mm(er[slot], down_w[gate_cols, :], NT).astype(BF16).astype(F32)
                dpre[slot, :, gate_cols] = (
                    dhid * up_pre * sig * (1.0 + gate_pre * (1.0 - sig))
                ).astype(BF16)
                dpre[slot, :, up_cols] = (dhid * act).astype(BF16)
            for copy in row_copies(step, slot):
                copy.start()
            for col in range(0, width, chunk):
                if col == width - chunk:

                    @pl.when(step + 1 < steps)
                    def _():
                        load_tokens(step + 1)

                cols = slice(col, col + chunk)
                part_sum = mm(hid[slot], down_w[:, cols])
                drow = mm(dpre[slot], in_w[cols, :], NT).astype(BF16)
                for n, dest in enumerate((keep, give)):
                    here = slice(n * rows, (n + 1) * rows)
                    dest[slot, 0, :, cols] = mm(picks[n], drow[here], TN).astype(BF16)
                    scaled = (part_sum[here] * scale_by[n]).astype(BF16)
                    dest[slot, 1, :, cols] = mm(picks[n], scaled, TN).astype(BF16)

            @pl.when(step >= 2)
            def _():
                pl.semaphore_wait(free_sem, 1)

            for copy in give_copies(slot):
                copy.start()

            @pl.when(step >= 1)
            def _():
                finish(step - 1, 1 - slot)

            return carry

        lax.fori_loop(0, steps, body, 0)
        last = (steps - 1) % 2
        finish(steps - 1, last)
        for step in (steps - 2, steps - 1):
            slot = step % 2
            for copy in row_copies(step, slot):
                copy.wait()
            for copy in sum_copies(step, slot):
                copy.wait()
            for copy in give_copies(slot):
                copy.wait_send()
        pl.semaphore_wait(free_sem, 2)

        relay.drain()

    anywhere = pl.BlockSpec(memory_space=pl.ANY)
    inside = pl.BlockSpec(memory_space=pltpu.VMEM)
    out = pl.pallas_call(
        kernel,
        in_specs=[anywhere, inside, inside] + [anywhere] * 7,
        out_specs=[anywhere] * 7,
        out_shape=[
            jax.ShapeDtypeStruct((nz, ny, tok, width), BF16),
            jax.ShapeDtypeStruct((nz, ny, tok, width), BF16),
            jax.ShapeDtypeStruct((steps, count, width), BF16),
            jax.ShapeDtypeStruct((steps, count, width), BF16),
            jax.ShapeDtypeStruct((steps, count, full), BF16),
            jax.ShapeDtypeStruct((steps, count, 2 * full), BF16),
            jax.ShapeDtypeStruct((nz, 2, ny, tok, width), BF16),
        ],
        scratch_shapes=[
            pltpu.VMEM((width, 2 * full), BF16),
            pltpu.VMEM((full, width), BF16),
            pltpu.VMEM((2, tok, width), BF16),
            pltpu.VMEM((2, tok, width), BF16),
            pltpu.VMEM((2, count, width), BF16),
            pltpu.VMEM((2, count, width), BF16),
            pltpu.VMEM((2, count, full), BF16),
            pltpu.VMEM((2, count, 2 * full), BF16),
            pltpu.VMEM((2, 2, tok, width), BF16),
            pltpu.VMEM((2, 2, tok, width), BF16),
            pltpu.VMEM((2, 2, tok, width), BF16),
            pltpu.SemaphoreType.DMA((5, steps, parts)),
            pltpu.SemaphoreType.DMA((2, steps, parts)),
            pltpu.SemaphoreType.DMA((6,)),
            pltpu.SemaphoreType.DMA((2,)),
            pltpu.SemaphoreType.DMA((2,)),
            pltpu.SemaphoreType.DMA((2, 4)),
            pltpu.SemaphoreType.DMA((2, 2)),
            pltpu.SemaphoreType.DMA((2, 2)),
            pltpu.SemaphoreType.DMA((2, 2)),
            pltpu.SemaphoreType.REGULAR,
        ],
        compiler_params=pltpu.CompilerParams(
            collective_id=collective_id, has_side_effects=True, vmem_limit_bytes=VMEM_BYTES
        ),
        name="expert_exchange",
    )(tokens, slots, gates, cots, *weights)
    return out[:6]


def return_sum(shares, collective_id):
    nz, ny, tok, width = shares.shape
    assert ny == 2

    def kernel(share_ref, out_ref, *scratch):
        back = Return(share_ref, out_ref, scratch)
        greet(back.peers())
        back.start()
        for turn in range(nz - 1):
            back.send(turn)
        back.finish()

    return pl.pallas_call(
        kernel,
        in_specs=[pl.BlockSpec(memory_space=pl.ANY)],
        out_specs=pl.BlockSpec(memory_space=pltpu.VMEM),
        out_shape=jax.ShapeDtypeStruct((tok, width), BF16),
        scratch_shapes=Return.scratch(nz, tok, width),
        compiler_params=pltpu.CompilerParams(
            collective_id=collective_id, has_side_effects=True, vmem_limit_bytes=VMEM_BYTES
        ),
        name="return_sum",
    )(shares)


def project_forward(normed, weights, gains, swaps, nh, nb, seqs, share, collective_id):
    tok, width = normed.shape
    tile, columns = weights[0].shape
    heads = columns // HEAD_DIM
    items = seqs * heads
    piece = tok // seqs
    span = nh * piece
    rows = nh * tok
    nz = nb // 2
    lots = nh * seqs
    count = len(swaps)

    def kernel(normed_ref, wq_ref, wk_ref, wv_ref, gain_ref, *refs):
        swap_in, refs = refs[:count], refs[count:]
        out_ref, qraw_ref, kraw_ref, inv_ref, group_ref, *refs = refs
        all_refs, refs = refs[:3], refs[3:]
        swap_out, refs = refs[:count], refs[count:]
        (
            vraw_ref, give_ref, sum_ref, norm_send, norm_recv, relay_send, relay_recv,
            sum_send, sum_recv, give_send, give_recv, swap_send, swap_recv,
        ) = refs
        head, blk = lax.axis_index("head"), lax.axis_index("blk")
        own_refs = (wq_ref, wk_ref, wv_ref)
        relay = Relay(
            [(own, everything, 1) for own, everything in zip(own_refs, all_refs)],
            nz, 1, relay_send, relay_recv, spread_y=False,
        )
        z, core = relay.z, relay.core
        swap = Swap(list(zip(swap_in, swap_out)), swap_send, swap_recv)
        others = [lax.rem(head + k, nh) for k in range(1, nh)]
        devices = [{"blk": blk, "head": other} for other in others]
        blks = [lax.rem(blk + k, nb) for k in range(1, nb)]
        greet(
            [(device, None) for device in devices]
            + [({"blk": other, "head": head}, None) for other in blks]
        )
        relay.start()

        def lines(slot):
            return pl.ds(pl.multiple_of(slot * tok, tok), tok)

        def norm_copy(k, slot):
            return pltpu.make_async_remote_copy(
                src_ref=normed_ref,
                dst_ref=group_ref.at[lines(slot)],
                send_sem=norm_send.at[k],
                recv_sem=norm_recv.at[slot],
                device_id=devices[k],
                device_id_type=pl.DeviceIdType.MESH,
            )

        def sum_copy(k, slot):
            return pltpu.make_async_remote_copy(
                src_ref=sum_ref.at[slot],
                dst_ref=sum_ref.at[slot],
                send_sem=sum_send.at[k],
                recv_sem=sum_recv.at[slot],
                device_id=devices[k],
                device_id_type=pl.DeviceIdType.MESH,
            )

        def give_copy(k, n, slot):
            return pltpu.make_async_remote_copy(
                src_ref=give_ref.at[blks[k] // share, n],
                dst_ref=out_ref.at[slot, n],
                send_sem=give_send.at[k, n],
                recv_sem=give_recv.at[slot, n],
                device_id={"blk": blks[k], "head": head},
                device_id_type=pl.DeviceIdType.MESH,
            )

        for k in range(nh - 1):
            norm_copy(k, head).start()
        swap.start()
        group_ref[lines(head), :] = normed_ref[...]
        for own, everything in zip(own_refs, all_refs):
            everything[z, core, 0] = own[...]

        raws = (qraw_ref, kraw_ref, vraw_ref)

        def multiply(rank):
            at = nearest(z, rank, nz)
            relay.arrived(at, 0, 1 - core)
            cols = pl.ds(pl.multiple_of(at * 2 * tile, 2 * tile), 2 * tile)
            for n in (2, 0, 1):
                product = mm(group_ref[:, cols], all_refs[n][at].reshape(2 * tile, columns))
                if rank == 0:
                    raws[n][...] = product
                else:
                    raws[n][...] += product

        for away in range(1, nz - 1):
            relay.pass_on_z(away)
        for k in range(nh - 1):
            norm_copy(k, others[k]).wait_recv()
        for rank in range(nz - 1):
            multiply(rank)
        relay.pass_on_z(nz - 1)
        multiply(nz - 1)

        def place(n, lot, hl):
            at, s = lot // seqs, lot % seqs
            return give_ref.at[s * heads + hl, n, pl.ds(at * piece, piece)]

        for lot in range(lots):
            here = slice(lot * piece, (lot + 1) * piece)
            for hl in range(heads):
                cols = slice(hl * HEAD_DIM, (hl + 1) * HEAD_DIM)
                place(2, lot, hl)[...] = vraw_ref[here, cols].astype(BF16)
            for n in range(2):
                total = jnp.zeros((piece, HEAD_DIM), F32)
                for hl in range(heads):
                    raw = raws[n][here, hl * HEAD_DIM : (hl + 1) * HEAD_DIM]
                    total = total + raw * raw
                sum_ref[head, n * lots + lot : n * lots + lot + 1, :] = jnp.sum(
                    total.T, axis=0, keepdims=True
                )
        for k in range(nh - 1):
            sum_copy(k, head).start()
        for k in range(nb - 1):
            give_copy(k, 2, blk).start()
        for k in range(nh - 1):
            sum_copy(k, others[k]).wait_recv()
        total_sums = sum_ref[0]
        for slot in range(1, nh):
            total_sums = total_sums + sum_ref[slot]
        inv_ref[...] = lax.rsqrt(total_sums / width + EPSILON)
        for n in range(2):
            for lot in range(lots):
                here = slice(lot * piece, (lot + 1) * piece)
                row = inv_ref[n * lots + lot : n * lots + lot + 1, :]
                inv = jnp.broadcast_to(row, (HEAD_DIM, piece)).T
                for hl in range(heads):
                    cols = slice(hl * HEAD_DIM, (hl + 1) * HEAD_DIM)
                    place(n, lot, hl)[...] = (
                        raws[n][here, cols] * inv * gain_ref[n : n + 1, cols]
                    ).astype(BF16)
            for k in range(nb - 1):
                give_copy(k, n, blk).start()
        for n in range(3):
            out_ref[blk, n] = give_ref[blk // share, n]
        for n in (2, 0, 1):
            for k in range(nb - 1):
                give_copy(k, n, blks[k]).wait_recv()
                give_copy(k, n, blk).wait_send()
        for k in range(nh - 1):
            norm_copy(k, head).wait_send()
            sum_copy(k, head).wait_send()
        swap.wait()
        relay.drain()

    anywhere = pl.BlockSpec(memory_space=pl.ANY)
    inside = pl.BlockSpec(memory_space=pltpu.VMEM)
    out = pl.pallas_call(
        kernel,
        in_specs=[inside] * 5 + [anywhere] * count,
        out_specs=[inside] * 8 + [anywhere] * count,
        out_shape=[
            jax.ShapeDtypeStruct((nb, 3, span, HEAD_DIM), BF16),
            jax.ShapeDtypeStruct((rows, columns), F32),
            jax.ShapeDtypeStruct((rows, columns), F32),
            jax.ShapeDtypeStruct((2 * lots, piece), F32),
            jax.ShapeDtypeStruct((rows, width), BF16),
        ]
        + [jax.ShapeDtypeStruct((nz, 2, 1, tile, columns), BF16)] * 3
        + [jax.ShapeDtypeStruct(v.shape, v.dtype) for v in swaps],
        scratch_shapes=[
            pltpu.VMEM((rows, columns), F32),
            pltpu.VMEM((items, 3, span, HEAD_DIM), BF16),
            pltpu.VMEM((nh, 2 * lots, piece), F32),
            pltpu.SemaphoreType.DMA((nh - 1,)),
            pltpu.SemaphoreType.DMA((nh,)),
            pltpu.SemaphoreType.DMA((5, nz, 3)),
            pltpu.SemaphoreType.DMA((2, nz, 3)),
            pltpu.SemaphoreType.DMA((nh - 1,)),
            pltpu.SemaphoreType.DMA((nh,)),
            pltpu.SemaphoreType.DMA((nb - 1, 3)),
            pltpu.SemaphoreType.DMA((nb, 3)),
            pltpu.SemaphoreType.DMA((count,)),
            pltpu.SemaphoreType.DMA((count,)),
        ],
        compiler_params=pltpu.CompilerParams(
            collective_id=collective_id, has_side_effects=True, vmem_limit_bytes=VMEM_BYTES
        ),
        name="project_forward",
    )(normed, *weights, gains, *swaps)
    gathered = [v.reshape(width, columns) for v in out[5:8]]
    return out[0], out[1:3], out[3], out[4], gathered, out[8:]


def project_backward(grads, raws, invs, gains, group, weights, nh, nb, collective_id):
    rows, width = group.shape
    columns = raws[0].shape[1]
    items = grads.shape[0]
    heads = columns // HEAD_DIM
    seqs = items // heads
    tok = rows // nh
    piece = tok // seqs
    nz = nb // 2
    tile = width // nb
    lots = nh * seqs
    chunk = min(512, width)

    def kernel(grad_ref, qraw_ref, kraw_ref, inv_ref, gain_ref, group_ref, wq_ref, wk_ref, wv_ref, *refs):
        out_ref, *refs = refs
        tile_refs, refs = refs[:3], refs[3:]
        qk_ref, product_ref, *refs = refs
        d_ref, sum_ref, part_ref, got_ref, sum_send, sum_recv, part_send, part_recv, *refs = refs
        give = refs[0]
        back = TileReturn(give, tile_refs, refs[1:])
        head, blk = lax.axis_index("head"), lax.axis_index("blk")
        core, z = back.core, back.z
        others = [lax.rem(head + k, nh) for k in range(1, nh)]
        devices = [{"blk": blk, "head": other} for other in others]

        def sum_copy(k, slot):
            return pltpu.make_async_remote_copy(
                src_ref=sum_ref.at[slot],
                dst_ref=sum_ref.at[slot],
                send_sem=sum_send.at[k],
                recv_sem=sum_recv.at[slot],
                device_id=devices[k],
                device_id_type=pl.DeviceIdType.MESH,
            )

        def part_copy(k, slot):
            return pltpu.make_async_remote_copy(
                src_ref=part_ref.at[k],
                dst_ref=got_ref.at[slot],
                send_sem=part_send.at[k],
                recv_sem=part_recv.at[slot],
                device_id=devices[k],
                device_id_type=pl.DeviceIdType.MESH,
            )

        def grad_tile(n, lot, hl):
            at, s = lot // seqs, lot % seqs
            return grad_ref[s * heads + hl, n, at * piece : (at + 1) * piece, :]

        def upright(row):
            return jnp.broadcast_to(row, (HEAD_DIM, piece)).T

        for lot in range(lots):
            here = slice(lot * piece, (lot + 1) * piece)
            for n, raw_ref in enumerate((qraw_ref, kraw_ref)):
                total = jnp.zeros((piece, HEAD_DIM), F32)
                for hl in range(heads):
                    cols = slice(hl * HEAD_DIM, (hl + 1) * HEAD_DIM)
                    gained = grad_tile(n, lot, hl).astype(F32) * gain_ref[n : n + 1, cols]
                    total = total + gained * raw_ref[here, cols]
                sum_ref[head, n * lots + lot : n * lots + lot + 1, :] = jnp.sum(
                    total.T, axis=0, keepdims=True
                )
        greet([(device, None) for device in devices] + back.peers())
        for k in range(nh - 1):
            sum_copy(k, head).start()
        for lot in range(lots):
            here = slice(lot * piece, (lot + 1) * piece)
            for hl in range(heads):
                cols = slice(2 * columns + hl * HEAD_DIM, 2 * columns + (hl + 1) * HEAD_DIM)
                d_ref[here, cols] = grad_tile(2, lot, hl)
        for k in range(nh - 1):
            sum_copy(k, others[k]).wait_recv()
        total_sums = sum_ref[0]
        for slot in range(1, nh):
            total_sums = total_sums + sum_ref[slot]
        for n, raw_ref in enumerate((qraw_ref, kraw_ref)):
            gain_total = [jnp.zeros((1, HEAD_DIM), F32) for _ in range(heads)]
            for lot in range(lots):
                here = slice(lot * piece, (lot + 1) * piece)
                index = slice(n * lots + lot, n * lots + lot + 1)
                inv = upright(inv_ref[index, :])
                lean = inv * inv * inv * (upright(total_sums[index, :]) / width)
                for hl in range(heads):
                    cols = slice(hl * HEAD_DIM, (hl + 1) * HEAD_DIM)
                    grad = grad_tile(n, lot, hl).astype(F32)
                    raw = raw_ref[here, cols]
                    gain_total[hl] = gain_total[hl] + jnp.sum(grad * raw * inv, axis=0, keepdims=True)
                    d_ref[here, n * columns + hl * HEAD_DIM : n * columns + (hl + 1) * HEAD_DIM] = (
                        inv * (grad * gain_ref[n : n + 1, cols]) - raw * lean
                    ).astype(BF16)
            for hl in range(heads):
                qk_ref[n : n + 1, hl * HEAD_DIM : (hl + 1) * HEAD_DIM] = gain_total[hl]

        edge = jnp.logical_or(z == 0, z == nz - 1)
        inner = jnp.logical_not(edge)
        for turn, target in enumerate(back.targets):
            for at, dest in ((1 - core, give), (core, back.mine)):
                cols = pl.ds(pl.multiple_of((target * 2 + at) * tile, tile), tile)
                dest[target] = mm(group_ref[:, cols], d_ref[...], TN).astype(BF16)
            for part in range(back.parts):
                back.y_copy(target, part).start()
            if turn < nz - 1:
                pl.when(edge)(lambda turn=turn: back.send(turn))

        product_ref[...] = jnp.zeros_like(product_ref)

        def partial(at, store):
            lines = pl.ds(pl.multiple_of(at * tok, tok), tok)
            for col in range(0, width, chunk):
                cols = slice(col, col + chunk)
                total = mm(d_ref[lines, 0:columns], wq_ref[cols, :], NT)
                total = total + mm(d_ref[lines, columns : 2 * columns], wk_ref[cols, :], NT)
                total = total + mm(d_ref[lines, 2 * columns : 3 * columns], wv_ref[cols, :], NT)
                product_ref[:, cols] += jnp.sum(
                    total * group_ref[lines, cols].astype(F32), axis=0, keepdims=True
                )
                store(cols, total)

        sent = 0
        for k in range(nh - 1):

            def keep(cols, total, k=k):
                part_ref[k, :, cols] = total.astype(BF16)

            partial(others[k], keep)
            part_copy(k, head).start()
            while sent < nz - 1 and (k + 1) * (nz - 1) >= (sent + 2) * (nh - 1):
                pl.when(inner)(lambda turn=sent: back.send(turn))
                sent += 1

        def keep_own(cols, total):
            out_ref[:, cols] = total

        partial(head, keep_own)
        for turn in range(sent, nz - 1):
            pl.when(inner)(lambda turn=turn: back.send(turn))
        for k in range(nh - 1):
            part_copy(k, others[k]).wait_recv()
            for r in range(0, tok, 64):
                here = pl.ds(r, 64)
                out_ref[here, :] += got_ref[others[k], here, :].astype(F32)
        back.finish()
        for k in range(nh - 1):
            sum_copy(k, head).wait_send()
            part_copy(k, head).wait_send()

    inside = pl.BlockSpec(memory_space=pltpu.VMEM)
    out = pl.pallas_call(
        kernel,
        in_specs=[inside] * 9,
        out_specs=[inside] * 6,
        out_shape=[jax.ShapeDtypeStruct((tok, width), F32)]
        + [jax.ShapeDtypeStruct((tile, columns), F32)] * 3
        + [jax.ShapeDtypeStruct((2, columns), F32), jax.ShapeDtypeStruct((1, width), F32)],
        scratch_shapes=[
            pltpu.VMEM((rows, 3 * columns), BF16),
            pltpu.VMEM((nh, 2 * lots, piece), F32),
            pltpu.VMEM((nh - 1, tok, width), BF16),
            pltpu.VMEM((nh, tok, width), BF16),
            pltpu.SemaphoreType.DMA((nh - 1,)),
            pltpu.SemaphoreType.DMA((nh,)),
            pltpu.SemaphoreType.DMA((nh - 1,)),
            pltpu.SemaphoreType.DMA((nh,)),
        ]
        + TileReturn.scratch(nz, tile, 3 * columns),
        compiler_params=pltpu.CompilerParams(
            collective_id=collective_id, has_side_effects=True, vmem_limit_bytes=VMEM_BYTES
        ),
        name="project_backward",
    )(grads, *raws, invs, gains, group, *weights)
    return out[0], out[1:4], out[4], out[5]


def local(
    hidden_in,
    attn_gain,
    w_query,
    w_key,
    w_value,
    query_gain,
    key_gain,
    w_out,
    ffn_gain,
    w_gate,
    w_up,
    w_down,
    routes,
    gate_weights,
    block_starts,
    cotangent,
):
    head_count = lax.axis_size("head")
    blk_count = lax.axis_size("blk")
    head_index = lax.axis_index("head")
    blk_index = lax.axis_index("blk")
    piece, seqs, width = hidden_in.shape
    span = piece * head_count
    per = span // BLOCK
    columns = w_query.shape[1]
    heads_here = columns // HEAD_DIM
    top_count = routes.shape[2]
    experts = blk_count * head_count // 2
    devices = blk_count * head_count
    tok = piece * seqs
    capacity = max(2, 5 * tok * top_count // (4 * experts))
    rows = -(-capacity // 32) * 32
    items = seqs * heads_here
    share = blk_count // items
    scale = 1.0 / math.sqrt(HEAD_DIM)
    everyone = ("blk", "head")

    def own_rows(values):
        return values.transpose(1, 0, 2).reshape(tok, values.shape[2])

    def out_rows(values):
        return values.reshape(seqs, piece, width).transpose(1, 0, 2)

    nz, ny = blk_count // 2, head_count // 2

    def flip_head(values, bit):
        return lax.ppermute(values, "head", [(h, h ^ bit) for h in range(head_count)])

    def flip_blk(values, bit):
        return lax.ppermute(values, "blk", [(b, b ^ bit) for b in range(blk_count)])


    table = jnp.concatenate([own_rows(routes).astype(F32).T, own_rows(gate_weights).T], axis=0)

    hidden_f = own_rows(hidden_in).astype(F32)
    grad_y_b = own_rows(cotangent)
    grad_y = grad_y_b.astype(F32)

    inv_one = inverse_rms(hidden_f)
    normed = (hidden_f * inv_one * attn_gain).astype(BF16)
    gain_query = lax.dynamic_slice_in_dim(query_gain, head_index * columns, columns)
    gain_key = lax.dynamic_slice_in_dim(key_gain, head_index * columns, columns)
    qk_gains = jnp.stack([gain_query, gain_key])
    out_w = lax.all_gather(w_out, "blk", axis=1, tiled=True)
    qkv, raws, invs, group, qkv_cols, (gate_other,) = project_forward(
        normed, (w_query, w_key, w_value), qk_gains, (w_gate[0],), head_count, blk_count, seqs,
        share, 5,
    )

    def to_items(values):
        parts = values.reshape(head_count, seqs, piece, heads_here, HEAD_DIM)
        parts = parts.transpose(1, 3, 0, 2, 4).reshape(items, span, HEAD_DIM)
        return jnp.repeat(parts, share, axis=0) if share > 1 else parts

    def from_items(values):
        if share > 1:
            values = values.reshape(items, share, span, HEAD_DIM).astype(F32).sum(1)
        parts = values.reshape(seqs, heads_here, head_count, piece, HEAD_DIM)
        return parts.transpose(2, 0, 3, 1, 4).reshape(head_count * tok, columns)

    def swap(values):
        return lax.all_to_all(values, "blk", split_axis=0, concat_axis=0, tiled=True)

    item = blk_index // share
    starts = lax.dynamic_index_in_dim(block_starts, item // heads_here, 0, keepdims=False)
    qkv = qkv.reshape(blk_count, 3, per, BLOCK, HEAD_DIM)
    total_blocks = blk_count * per
    key_block = jnp.arange(total_blocks, dtype=jnp.int32)
    bias = jnp.where(key_block[None, :] >= starts[:, None], 0.0, -1e30).astype(F32).reshape(-1)
    heads_out, heads_out_t, log_total, all_cots, tables, up_other, down_other = attend_forward(
        bias, qkv, grad_y_b, table, (w_up[0], w_down[0]), nz, ny, scale, share, 2
    )
    expert_weights = (w_gate[0], gate_other, w_up[0], up_other, w_down[0], down_other)

    expert = (blk_index * head_count + head_index) // 2
    named = tables[..., :top_count, :] == expert.astype(F32)
    hit = jnp.any(named, axis=-2)
    gates = jnp.sum(jnp.where(named, tables[..., top_count:, :], 0.0), axis=-2)[..., None, :]
    before = jnp.triu(jnp.ones((tok, tok), BF16), 1)
    ranks = jnp.dot(
        hit.reshape(-1, tok).astype(BF16), before, preferred_element_type=F32
    ).astype(jnp.int32)
    slots = jnp.where(hit, ranks.reshape(hit.shape), -1)[..., None, :]

    attended = from_items(swap(heads_out.reshape(blk_count, span, HEAD_DIM))).astype(BF16)
    branch = lax.psum_scatter(
        mm(attended, out_w).astype(BF16), "head", scatter_dimension=0, tiled=True
    ).astype(F32)
    middle = hidden_f + branch
    inv_two = inverse_rms(middle)
    normed_two = (middle * inv_two * ffn_gain).astype(BF16)

    dx_share, moe_share, xr, er, hid, dpre = expert_exchange(
        normed_two, all_cots, slots, gates, expert_weights, head_count, blk_count, rows, 0
    )

    def halvings(count):
        return [1 << i for i in reversed(range(count.bit_length() - 1))]

    def halve(values, flip, bit, mine):
        pair = values.reshape((2, values.shape[0] // 2) + values.shape[1:])
        kept = lax.dynamic_index_in_dim(pair, mine, 0, keepdims=False)
        sent = lax.dynamic_index_in_dim(pair, 1 - mine, 0, keepdims=False)
        return kept, flip(sent.astype(BF16), bit)

    y_bits = [(flip_head, 2 * b, (head_index // (2 * b)) % 2) for b in halvings(ny)]
    z_bits = [(flip_blk, 2 * b, (blk_index // (2 * b)) % 2) for b in halvings(nz)]

    def give_back(values, bits):
        for flip, bit, mine in bits:
            kept, came = halve(values, flip, bit, mine)
            values = kept.astype(F32) + came.astype(F32)
        return values[0]

    if ny == 2:
        grad_normed_two = return_sum(dx_share, 1)
    else:
        grad_normed_two = give_back(dx_share.swapaxes(0, 1), y_bits)
        grad_normed_two = give_back(grad_normed_two, z_bits).astype(BF16)
    grad_normed_two, moe_share = lax.optimization_barrier((grad_normed_two, moe_share))
    grad_normed_two = grad_normed_two.astype(F32)
    xr, er = xr.reshape(-1, width), er.reshape(-1, width)
    hid, dpre = [v.reshape(-1, v.shape[-1]) for v in (hid, dpre)]
    half = w_gate.shape[2]
    dgate, dgate_other, dup, dup_other = [dpre[:, n * half : (n + 1) * half] for n in range(4)]

    halves = [
        mm(hid[:, :half], er, TN), mm(xr, dgate, TN), mm(xr, dup, TN),
        mm(hid[:, half:], er, TN), mm(xr, dgate_other, TN), mm(xr, dup_other, TN),
    ]
    gained_two = grad_normed_two * ffn_gain
    ffn_gain_part = jnp.sum(grad_normed_two * middle * inv_two, 0)
    grad_middle = (
        grad_y
        + inv_two * gained_two
        - middle * inv_two * inv_two * inv_two * jnp.mean(gained_two * middle, -1, keepdims=True)
    )
    grad_branch = grad_middle.astype(BF16)
    grad_group = lax.all_gather(grad_branch, "head", axis=0, tiled=True)
    grad_group, *halves = lax.optimization_barrier((grad_group, *halves))
    others = [v.astype(BF16) for v in halves[3:]]
    grad_attended = mm(grad_group, out_w, NT).astype(BF16)
    out_part = mm(attended, grad_group, TN)
    grad_heads = swap(to_items(grad_attended)).reshape(blk_count * per, BLOCK, HEAD_DIM)
    own_sum = ny == 2
    grad_qkv, others[1:], sums = attend_backward(
        bias, qkv, grad_heads, heads_out_t, log_total, others[1:], [moe_share] * own_sum,
        scale, share, 3,
    )
    others[0] = flip_head(others[0], 1)
    grad_qkv = swap(grad_qkv.reshape(blk_count, 3, span, HEAD_DIM))
    grad_qkv, others[0] = lax.optimization_barrier((grad_qkv, others[0]))
    grad_down, grad_gate, grad_up = [
        (mine + other.astype(F32))[None] for mine, other in zip(halves[:3], others)
    ]
    if own_sum:
        expert_sum = sums[0].astype(F32)
    else:
        expert_sum = give_back(give_back(moe_share.swapaxes(0, 1), y_bits), z_bits)
    result = middle + expert_sum
    if share > 1:
        grad_qkv = grad_qkv.reshape(items, share, 3, span, HEAD_DIM).astype(F32).sum(1).astype(BF16)
    grad_normed, (grad_query, grad_key, grad_value), qk_parts, product = project_backward(
        grad_qkv, raws, invs, qk_gains, group, qkv_cols, head_count, blk_count, 4
    )
    grad_normed = rounded(grad_normed)
    query_gain_part, key_gain_part = qk_parts[0], qk_parts[1]
    gained_one = grad_normed * attn_gain
    attn_gain_part = product[0] / attn_gain
    grad_hidden_in = (
        grad_middle
        + inv_one * gained_one
        - hidden_f
        * inv_one
        * inv_one
        * inv_one
        * jnp.mean(gained_one * hidden_f, -1, keepdims=True)
    )

    def over_blk(values, dim):
        return lax.psum_scatter(
            values.astype(BF16), "blk", scatter_dimension=dim, tiled=True
        ).astype(F32)

    grad_out = over_blk(out_part, 1)
    zero_width = jnp.zeros((width,), F32)
    query_gain_full = lax.dynamic_update_slice_in_dim(
        zero_width, query_gain_part, head_index * columns, 0
    )
    key_gain_full = lax.dynamic_update_slice_in_dim(
        zero_width, key_gain_part, head_index * columns, 0
    )
    square_parts = jnp.stack(
        [jnp.sum(result * result), jnp.sum(branch * branch), jnp.sum(expert_sum * expert_sum)]
    )
    stacked = jnp.concatenate(
        [attn_gain_part, ffn_gain_part, query_gain_full, key_gain_full, jnp.pad(square_parts, (0, 125))]
    ).reshape(-1, 128)
    for axis in ("head", "blk"):
        stacked = jnp.sum(lax.all_gather(stacked, axis, axis=0, tiled=False), 0)
    stacked = stacked.reshape(-1)
    totals = [stacked[4 * width : 4 * width + 3]] + [
        stacked[n * width : (n + 1) * width] for n in range(4)
    ]
    entry_count = tok * width * devices
    stream_stats = jnp.sqrt(totals[0] / entry_count + EPSILON)
    return (
        out_rows(result.astype(BF16)),
        out_rows(grad_hidden_in.astype(BF16)),
        totals[1],
        grad_query,
        grad_key,
        grad_value,
        totals[3],
        totals[4],
        grad_out,
        totals[2],
        grad_gate,
        grad_up,
        grad_down,
        stream_stats,
    )


def solution(mesh):
    rows3 = P(("blk", "head"), None, None)
    placed = (
        rows3, P(), P("blk", "head"), P("blk", "head"), P("blk", "head"), P(), P(),
        P("head", "blk"), P(), rows3, rows3, rows3, rows3, rows3, P(), rows3,
    )
    return jax.shard_map(
        local,
        mesh=mesh,
        in_specs=placed,
        out_specs=(
            rows3, rows3, P(), P("blk", "head"), P("blk", "head"), P("blk", "head"), P(), P(),
            P("head", "blk"), P(), rows3, rows3, rows3, P(),
        ),
        check_vma=False,
    )
```

```python
import functools
import math

import jax
import jax.numpy as jnp
from jax import lax
from jax.experimental import pallas as pl
from jax.experimental.pallas import tpu as pltpu
from jax.sharding import PartitionSpec as P

HEAD_DIM = 128
BLOCK = 256
EPSILON = 1e-06
F32 = jnp.float32
BF16 = jnp.bfloat16
VMEM_BYTES = 58 * 1024 * 1024

NN = (((1,), (0,)), ((), ()))
NT = (((1,), (1,)), ((), ()))
TN = (((0,), (0,)), ((), ()))


def mm(left, right, dims=NN):
    return lax.dot_general(left, right, dims, preferred_element_type=F32)


def rounded(values):
    return lax.optimization_barrier(values.astype(BF16)).astype(F32)


def inverse_rms(values):
    return lax.rsqrt(jnp.mean(values * values, axis=-1, keepdims=True) + EPSILON)


def nearest(here, rank, count):
    below = here
    above = count - 1 - here
    swing = jnp.where(rank % 2 == 1, here - (rank + 1) // 2, here + rank // 2)
    far = jnp.where(below < above, rank, count - 1 - rank)
    return jnp.where(rank <= 2 * jnp.minimum(below, above), swing, far)


def greet(peers):
    barrier = pltpu.get_barrier_semaphore()
    count = 0
    for device, condition in peers:

        def signal(device=device):
            pl.semaphore_signal(
                barrier, inc=1, device_id=device, device_id_type=pl.DeviceIdType.MESH
            )

        if condition is None:
            signal()
            count = count + 1
        else:
            pl.when(condition)(signal)
            count = count + jnp.where(condition, 1, 0)
    pl.semaphore_wait(barrier, count)


class Relay:
    def __init__(self, arrays, nz, ny, send_sem, recv_sem, spread_y=True):
        self.arrays, self.nz, self.ny = arrays, nz, ny
        self.send_sem, self.recv_sem = send_sem, recv_sem
        head, blk = lax.axis_index("head"), lax.axis_index("blk")
        x, y = head % 2, head // 2 if spread_y else 0
        self.y = y
        self.core, self.z = core, z = blk % 2, blk // 2

        def device(z_at, y_at, core_at):
            return {"blk": z_at * 2 + core_at, "head": y_at * 2 + x if spread_y else head}

        self.sibling = device(z, y, 1 - core)
        self.targets = [
            self.sibling, device(z, y + 1, core), device(z, y - 1, core),
            device(z + 1, y, core), device(z - 1, y, core),
        ]
        self.present = [None, y < ny - 1, y > 0, z < nz - 1, z > 0]
        self.ways = range(5) if spread_y else (0, 3, 4)
        self.pieces = []
        for n, (own, everything, parts) in enumerate(arrays):
            rows = own.shape[0] // parts
            for part in range(parts):
                self.pieces.append((n, pl.ds(part * rows, rows)))

    @staticmethod
    def when(condition, work):
        if condition is None:
            work()
        else:
            pl.when(condition)(work)

    def peers(self):
        return list(zip(self.targets, self.present))

    def conditions(self, z_at, y_at):
        column = y_at == self.y
        there = self.present
        return [
            None, (y_at <= self.y) & there[1], (y_at >= self.y) & there[2],
            column & (z_at <= self.z) & there[3], column & (z_at >= self.z) & there[4],
        ]

    def copy(self, z_at, y_at, core_at, piece, way, own=False):
        n, here = self.pieces[piece]
        everything = self.arrays[n][1]
        place = everything.at[z_at, core_at, y_at, here]
        return pltpu.make_async_remote_copy(
            src_ref=self.arrays[n][0].at[here] if own else place,
            dst_ref=place,
            send_sem=self.send_sem.at[way, z_at * self.ny + y_at, piece],
            recv_sem=self.recv_sem.at[core_at, z_at * self.ny + y_at, piece],
            device_id=self.targets[way],
            device_id_type=pl.DeviceIdType.MESH,
        )

    def start(self):
        for piece in range(len(self.pieces)):
            for way in reversed(self.ways):
                self.when(self.present[way], lambda way=way, piece=piece: self.copy(
                    self.z, self.y, self.core, piece, way, own=True).start())

    def keep(self, stages, sems):
        loads = [
            pltpu.make_async_copy(own, stage, sems.at[n])
            for n, ((own, _, _), stage) in enumerate(zip(self.arrays, stages))
        ]
        for copy in loads:
            copy.start()
        for copy in loads:
            copy.wait()
        stores = [
            pltpu.make_async_copy(stage, everything.at[self.z, self.core, self.y], sems.at[n])
            for n, ((_, everything, _), stage) in enumerate(zip(self.arrays, stages))
        ]
        for copy in stores:
            copy.start()
        return stores

    def arrived(self, z_at, y_at, core_at):
        for piece in range(len(self.pieces)):
            self.copy(z_at, y_at, core_at, piece, 0).wait_recv()

    def pass_on(self, z_at, y_at):
        for piece in range(len(self.pieces)):
            self.copy(z_at, y_at, self.core, piece, 0).wait_recv()
            conditions = self.conditions(z_at, y_at)
            for way in self.ways:
                self.when(conditions[way], lambda way=way, piece=piece: self.copy(
                    z_at, y_at, self.core, piece, way).start())

    def pass_on_z(self, away):
        pl.when(self.z - away >= 0)(lambda: self.pass_on(self.z - away, self.y))
        pl.when(self.z + away < self.nz)(lambda: self.pass_on(self.z + away, self.y))

    def drain(self):
        def one(index, carry):
            z_at, y_at = index // self.ny, index % self.ny
            conditions = self.conditions(z_at, y_at)
            for way in self.ways:
                for piece in range(len(self.pieces)):
                    self.when(conditions[way], lambda way=way, piece=piece: self.copy(
                        z_at, y_at, self.core, piece, way).wait_send())
            return carry

        lax.fori_loop(0, self.nz * self.ny, one, 0)


class Swap:
    def __init__(self, pairs, send_sem, recv_sem):
        head, blk = lax.axis_index("head"), lax.axis_index("blk")
        self.neighbour = {"blk": blk, "head": head + 1 - 2 * (head % 2)}
        self.copies = [
            pltpu.make_async_remote_copy(
                src_ref=source,
                dst_ref=target,
                send_sem=send_sem.at[n],
                recv_sem=recv_sem.at[n],
                device_id=self.neighbour,
                device_id_type=pl.DeviceIdType.MESH,
            )
            for n, (source, target) in enumerate(pairs)
        ]

    def peers(self):
        return [(self.neighbour, None)]

    def start(self):
        for copy in self.copies:
            copy.start()

    def wait(self):
        for copy in self.copies:
            copy.wait()


class Deliver:
    def __init__(self, stage, out_ref, send_sem, recv_sem):
        self.stage, self.out_ref = stage, out_ref
        self.send_sem, self.recv_sem = send_sem, recv_sem
        self.count, self.per = out_ref.shape[:2]
        self.blk, self.head = lax.axis_index("blk"), lax.axis_index("head")
        self.others = [lax.rem(self.blk + k, self.count) for k in range(1, self.count)]

    def device(self, blk):
        return {"blk": blk, "head": self.head}

    def peers(self):
        return [(self.device(other), None) for other in self.others]

    def copy(self, block, source, owner):
        at = lax.rem(block, self.per)
        return pltpu.make_async_remote_copy(
            src_ref=self.stage.at[block],
            dst_ref=self.out_ref.at[source, at],
            send_sem=self.send_sem.at[block],
            recv_sem=self.recv_sem.at[source, at],
            device_id=self.device(owner),
            device_id_type=pl.DeviceIdType.MESH,
        )

    def send(self, block):
        owner = block // self.per
        pl.when(owner != self.blk)(lambda: self.copy(block, self.blk, owner).start())

        @pl.when(owner == self.blk)
        def _():
            self.out_ref[self.blk, lax.rem(block, self.per)] = self.stage[block]

    def wait(self):
        for other in self.others:
            for at in range(self.per):
                self.copy(self.blk * self.per + at, other, other).wait_recv()

        def sent(block, carry):
            owner = block // self.per
            pl.when(owner != self.blk)(lambda: self.copy(block, self.blk, owner).wait_send())
            return carry

        lax.fori_loop(0, self.count * self.per, sent, 0)


class Return:
    parts = 2

    @classmethod
    def scratch(cls, nz, tok, width):
        return [
            pltpu.VMEM((nz, tok, width), BF16),
            pltpu.VMEM((nz, tok, width), BF16),
            pltpu.VMEM((nz + 1, tok, width), BF16),
            pltpu.SemaphoreType.DMA((nz, cls.parts)),
            pltpu.SemaphoreType.DMA((nz, cls.parts)),
            pltpu.SemaphoreType.DMA((nz, cls.parts)),
            pltpu.SemaphoreType.DMA((nz, cls.parts)),
            pltpu.SemaphoreType.DMA((nz + 1, cls.parts)),
        ]

    def __init__(self, share_ref, out_ref, scratch):
        self.share_ref, self.out_ref = share_ref, out_ref
        (
            self.mine, self.from_y, self.from_z,
            self.mine_sem, self.y_send, self.y_recv, self.z_send, self.z_recv,
        ) = scratch
        self.nz, tok = self.mine.shape[:2]
        self.piece = tok // self.parts
        self.step_rows = min(64, self.piece)
        head, blk = lax.axis_index("head"), lax.axis_index("blk")
        x, self.y, self.z = head % 2, head // 2, blk // 2
        self.beside = {"blk": blk, "head": (1 - self.y) * 2 + x}
        self.onward = [{"blk": blk + 2, "head": head}, {"blk": blk - 2, "head": head}]
        self.has = [self.z > 0, self.z < self.nz - 1]
        self.targets = [nearest(self.z, rank, self.nz) for rank in reversed(range(self.nz))]

    def peers(self):
        return [(self.beside, None), (self.onward[1], self.has[0]), (self.onward[0], self.has[1])]

    def cut(self, part):
        return pl.ds(part * self.piece, self.piece)

    def own_copy(self, target, part):
        return pltpu.make_async_copy(
            self.share_ref.at[target, self.y, self.cut(part)],
            self.mine.at[target, self.cut(part)],
            self.mine_sem.at[target, part],
        )

    def own_wait(self, target, part):
        self.own_copy(target, part).wait()

    def y_wait(self, target, part):
        self.y_copy(target, part).wait_recv()

    def y_drain(self):
        for target in self.targets:
            for part in range(self.parts):
                self.y_copy(target, part).wait_send()

    def y_copy(self, target, part):
        return pltpu.make_async_remote_copy(
            src_ref=self.share_ref.at[target, 1 - self.y, self.cut(part)],
            dst_ref=self.from_y.at[target, self.cut(part)],
            send_sem=self.y_send.at[target, part],
            recv_sem=self.y_recv.at[target, part],
            device_id=self.beside,
            device_id_type=pl.DeviceIdType.MESH,
        )

    def slot(self, way, target, at):
        return target if way == 0 else jnp.where(target == at, self.nz, target)

    def z_copy(self, way, target, part, at=None):
        at = (self.z + 1, self.z - 1)[way] if at is None else at
        slot = self.slot(way, target, at)
        return pltpu.make_async_remote_copy(
            src_ref=self.mine.at[target, self.cut(part)],
            dst_ref=self.from_z.at[slot, self.cut(part)],
            send_sem=self.z_send.at[target, part],
            recv_sem=self.z_recv.at[slot, part],
            device_id=self.onward[way],
            device_id_type=pl.DeviceIdType.MESH,
        )

    def start(self):
        for target in self.targets:
            for part in range(self.parts):
                self.y_copy(target, part).start()
                self.own_copy(target, part).start()

    def add(self, target, part, ways, out=None, beside=True):
        for r in range(part * self.piece, (part + 1) * self.piece, self.step_rows):
            here = pl.ds(r, self.step_rows)
            total = self.mine[target, here, :].astype(F32)
            if beside and self.from_y is not None:
                total = total + self.from_y[target, here, :].astype(F32)
            for way in ways:
                total = total + self.from_z[self.slot(way, target, self.z), here, :].astype(F32)
            if out is None:
                self.mine[target, here, :] = total.astype(BF16)
            else:
                self.store(out, here, total)

    def store(self, out, here, total):
        out[here, :] = total.astype(out.dtype)

    def send(self, turn, part=None):
        target = self.targets[turn]
        for part in range(self.parts) if part is None else (part,):
            self.own_wait(target, part)
            self.y_wait(target, part)
            for way in range(2):
                going = target > self.z if way == 0 else target < self.z

                @pl.when(going & self.has[way])
                def _(way=way, part=part):
                    self.z_copy(way, target, part, self.z).wait_recv()
                    self.add(target, part, (way,))

                @pl.when(going & jnp.logical_not(self.has[way]))
                def _(part=part):
                    self.add(target, part, ())

                @pl.when(going)
                def _(way=way, part=part):
                    self.z_copy(way, target, part).start()

    def pair(self, turn):
        target = self.targets[turn]
        for part in range(self.parts):
            self.own_wait(target, part)
            self.y_wait(target, part)
            self.add(target, part, ())
            for way in range(2):
                first = (target > self.z if way == 0 else target < self.z) & jnp.logical_not(
                    self.has[way]
                )
                pl.when(first)(lambda way=way, part=part: self.z_copy(way, target, part).start())

    def link(self, turn):
        target = self.targets[turn]
        for part in range(self.parts):
            for way in range(2):
                later = (target > self.z if way == 0 else target < self.z) & self.has[way]

                @pl.when(later)
                def _(way=way, part=part):
                    self.z_copy(way, target, part, self.z).wait_recv()
                    self.add(target, part, (way,), beside=False)
                    self.z_copy(way, target, part).start()

    def finish(self, paired=False):
        z, has = self.z, self.has
        for part in range(self.parts):
            if not paired:
                self.own_wait(z, part)
                self.y_wait(z, part)
            for way in range(2):
                pl.when(has[way])(lambda way=way, part=part: self.z_copy(way, z, part, z).wait_recv())
            for condition, ways in (
                (has[0] & has[1], (0, 1)),
                (has[0] & jnp.logical_not(has[1]), (0,)),
                (jnp.logical_not(has[0]) & has[1], (1,)),
            ):
                pl.when(condition)(
                    lambda ways=ways, part=part: self.add(z, part, ways, self.out_ref, not paired)
                )
        self.y_drain()
        for target in self.targets[:-1]:
            for part in range(self.parts):
                self.z_copy(0, target, part).wait_send()


class ZReturn(Return):
    @classmethod
    def scratch(cls, nz, tok, width):
        return [
            pltpu.VMEM((nz + 1, tok, width), BF16),
            pltpu.SemaphoreType.DMA((nz, cls.parts)),
            pltpu.SemaphoreType.DMA((nz, cls.parts)),
            pltpu.SemaphoreType.DMA((nz + 1, cls.parts)),
        ]

    def __init__(self, mine, share_ref, out_ref, scratch):
        from_z, mine_sem, z_send, z_recv = scratch
        super().__init__(
            share_ref, out_ref, (mine, None, from_z, mine_sem, None, None, z_send, z_recv)
        )

    def own_copy(self, target, part):
        return pltpu.make_async_copy(
            self.share_ref.at[target, self.cut(part)],
            self.mine.at[target, self.cut(part)],
            self.mine_sem.at[target, part],
        )

    def y_wait(self, target, part):
        pass

    def y_drain(self):
        pass

    def start(self):
        for target in self.targets:
            for part in range(self.parts):
                self.own_copy(target, part).start()


class TileReturn(Return):
    def __init__(self, give_ref, out_refs, scratch):
        super().__init__(give_ref, out_refs, scratch)
        blk = lax.axis_index("blk")
        self.core = blk % 2
        self.beside = {"blk": blk + 1 - 2 * self.core, "head": lax.axis_index("head")}

    @classmethod
    def scratch(cls, nz, tok, width):
        return [pltpu.VMEM((nz, tok, width), BF16)] + super().scratch(nz, tok, width)

    def own_copy(self, target, part):
        return None

    def own_wait(self, target, part):
        pass

    def y_copy(self, target, part):
        return pltpu.make_async_remote_copy(
            src_ref=self.share_ref.at[target, self.cut(part)],
            dst_ref=self.from_y.at[target, self.cut(part)],
            send_sem=self.y_send.at[target, part],
            recv_sem=self.y_recv.at[target, part],
            device_id=self.beside,
            device_id_type=pl.DeviceIdType.MESH,
        )

    def store(self, out, here, total):
        size = total.shape[1] // len(out)
        for n, ref in enumerate(out):
            ref[here, :] = total[:, n * size : (n + 1) * size]


def attend_forward(bias, qkv, cots, table, swaps, nz, ny, scale, share, collective_id):
    src, _, per, block, dim = qkv.shape
    blocks = src * per
    parts = 2
    events = [blocks * 5 // 8, blocks * 7 // 8]

    count = len(swaps)

    def kernel(bias_ref, qkv_ref, cot_ref, table_ref, *refs):
        swap_in, refs = refs[:count], refs[count:]
        out_ref, out_t_ref, lse_ref, cots_ref, tables_ref, *refs = refs
        swap_out, refs = refs[:count], refs[count:]
        (
            vt_ref, cot_stage, table_stage, send_sem, recv_sem, own_sem, swap_send, swap_recv,
            out_stage, out_send, out_recv,
        ) = refs
        swap = Swap(list(zip(swap_in, swap_out)), swap_send, swap_recv)
        deliver = Deliver(out_stage, out_ref, out_send, out_recv)
        relay = Relay(
            [(cot_ref, cots_ref, parts), (table_ref, tables_ref, 1)], nz, ny, send_sem, recv_sem
        )
        greet(deliver.peers() + relay.peers()[1:3] + swap.peers())
        relay.start()
        swap.start()
        kept = relay.keep((cot_stage, table_stage), own_sem)

        def flip(j, carry):
            vt_ref[j] = qkv_ref[j // per, 2, j % per].astype(F32).T.astype(BF16)
            return carry

        lax.fori_loop(0, blocks, flip, 0)
        own = lax.axis_index("blk") % share

        def query_block(step, carry):
            for n, event in enumerate(events):
                if n + 1 < nz:
                    pl.when(step == event)(lambda n=n: relay.pass_on_z(n + 1))

            def work():
                query = qkv_ref[step // per, 0, step % per]

                def body(j, carry):
                    top, total, acc = carry
                    scores = mm(qkv_ref[j // per, 1, j % per], query, NT) * scale
                    scores = scores + bias_ref[step * blocks + j]
                    new_top = jnp.maximum(top, jnp.max(scores, axis=0, keepdims=True))
                    weights = jnp.exp(scores - new_top)
                    shrink = jnp.exp(top - new_top)
                    total = total * shrink + jnp.sum(weights, axis=0, keepdims=True)
                    acc = acc * shrink + mm(vt_ref[j], weights.astype(BF16))
                    return new_top, total, acc

                top, total, acc = lax.fori_loop(
                    0,
                    step + 1,
                    body,
                    (
                        jnp.full((1, block), -1e30, F32),
                        jnp.zeros((1, block), F32),
                        jnp.zeros((dim, block), F32),
                    ),
                )
                result = acc / total
                out_t_ref[step] = result
                out_stage[step] = result.T.astype(BF16)
                lse_ref[step] = top + jnp.log(total)

            if share == 1:
                work()
            else:
                mine = step % share == own
                pl.when(mine)(work)

                @pl.when(jnp.logical_not(mine))
                def _():
                    out_t_ref[step] = jnp.zeros((dim, block), F32)
                    out_stage[step] = jnp.zeros((block, dim), BF16)
                    lse_ref[step] = jnp.zeros((1, block), F32)

            deliver.send(step)
            return carry

        lax.fori_loop(0, blocks, query_block, 0)
        for away in range(len(events) + 1, nz):
            relay.pass_on_z(away)
        for turn in range(1, ny):
            for rank in range(nz):
                relay.pass_on(nearest(relay.z, rank, nz), nearest(relay.y, turn, ny))

        def from_sibling(index, carry):
            relay.arrived(index // ny, index % ny, 1 - relay.core)
            return carry

        lax.fori_loop(0, nz * ny, from_sibling, 0)
        relay.drain()
        deliver.wait()
        swap.wait()
        for copy in kept:
            copy.wait()

    anywhere = pl.BlockSpec(memory_space=pl.ANY)
    inside = pl.BlockSpec(memory_space=pltpu.VMEM)
    return pl.pallas_call(
        kernel,
        in_specs=[pl.BlockSpec(memory_space=pltpu.SMEM), inside, anywhere, anywhere]
        + [anywhere] * count,
        out_specs=[inside] * 3 + [anywhere] * (2 + count),
        out_shape=[
            jax.ShapeDtypeStruct((src, per, block, dim), BF16),
            jax.ShapeDtypeStruct((blocks, dim, block), F32),
            jax.ShapeDtypeStruct((blocks, 1, block), F32),
            jax.ShapeDtypeStruct((nz, 2, ny) + cots.shape, cots.dtype),
            jax.ShapeDtypeStruct((nz, 2, ny) + table.shape, table.dtype),
        ]
        + [jax.ShapeDtypeStruct(v.shape, v.dtype) for v in swaps],
        scratch_shapes=[
            pltpu.VMEM((blocks, dim, block), BF16),
            pltpu.VMEM(cots.shape, cots.dtype),
            pltpu.VMEM(table.shape, table.dtype),
            pltpu.SemaphoreType.DMA((5, nz * ny, parts + 1)),
            pltpu.SemaphoreType.DMA((2, nz * ny, parts + 1)),
            pltpu.SemaphoreType.DMA((2,)),
            pltpu.SemaphoreType.DMA((count,)),
            pltpu.SemaphoreType.DMA((count,)),
            pltpu.VMEM((blocks, block, dim), BF16),
            pltpu.SemaphoreType.DMA((blocks,)),
            pltpu.SemaphoreType.DMA((src, per)),
        ],
        compiler_params=pltpu.CompilerParams(
            collective_id=collective_id, has_side_effects=True, vmem_limit_bytes=VMEM_BYTES
        ),
        name="attend_forward",
    )(bias, qkv, cots, table, *swaps)


def attend_backward(bias, qkv, grad_out, out_t, lse, swaps, shares, scale, share, collective_id):
    src, _, per, block, dim = qkv.shape
    blocks = src * per
    count = len(swaps)
    events = [blocks * n // 16 for n in (3, 7, 13)]

    def kernel(bias_ref, qkv_ref, go_ref, out_t_ref, lse_ref, *refs):
        swap_in, refs = refs[:count], refs[count:]
        share_ref, refs = refs[: len(shares)], refs[len(shares) :]
        grad_ref, *refs = refs
        swap_out, refs = refs[:count], refs[count:]
        sum_ref, refs = refs[: len(shares)], refs[len(shares) :]
        dk_ref, dv_ref, delta_ref, swap_send, swap_recv, stage, out_send, out_recv, *refs = refs
        deliver = Deliver(stage, grad_ref, out_send, out_recv)
        swap = Swap(list(zip(swap_in, swap_out)), swap_send, swap_recv)
        back = Return(share_ref[0], sum_ref[0], refs) if shares else None
        greet(deliver.peers() + swap.peers() + (back.peers()[:1] if back else []))
        if back:
            back.start()
        swap.start()
        dk_ref[...] = jnp.zeros_like(dk_ref)
        dv_ref[...] = jnp.zeros_like(dv_ref)
        own = lax.axis_index("blk") % share
        core = lax.axis_index("blk") % 2

        def block_delta(i, carry):
            delta_ref[i] = jnp.sum(go_ref[i].astype(F32).T * out_t_ref[i], axis=0, keepdims=True)
            return carry

        lax.fori_loop(0, blocks, block_delta, 0)

        def pair(i, j):
            scores = mm(qkv_ref[j // per, 1, j % per], qkv_ref[i // per, 0, i % per], NT) * scale
            probs = jnp.exp(scores + bias_ref[i * blocks + j] - lse_ref[i])
            grad_probs = mm(qkv_ref[j // per, 2, j % per], go_ref[i], NT)
            return probs.astype(BF16), (probs * (grad_probs - delta_ref[i])).astype(BF16)

        def down(turn):
            i = blocks - 1 - turn

            def work():
                query, go = qkv_ref[i // per, 0, i % per], go_ref[i]

                def body(j, dq):
                    probs, grad_scores = pair(i, j)
                    dv_ref[j] += mm(probs, go)
                    dk_ref[j] += mm(grad_scores, query)
                    return dq + mm(grad_scores, qkv_ref[j // per, 1, j % per], TN)

                dq = lax.fori_loop(0, i + 1, body, jnp.zeros((block, dim), F32))
                stage[i, 0] = (dq * scale).astype(BF16)

            if share == 1:
                work()
            else:
                mine = i % share == own
                pl.when(mine)(work)

                @pl.when(jnp.logical_not(mine))
                def _():
                    stage[i, 0] = jnp.zeros((block, dim), BF16)

            stage[i, 1] = (dk_ref[i] * scale).astype(BF16)
            stage[i, 2] = dv_ref[i].astype(BF16)
            deliver.send(i)

        def up(j):
            key = qkv_ref[j // per, 1, j % per]

            def body(turn, carry):
                dk, dv = carry
                i = own + share * turn
                probs, grad_scores = pair(i, j)
                dk_ref[i] += mm(grad_scores, key, TN)
                query = qkv_ref[i // per, 0, i % per]
                return dk + mm(grad_scores, query), dv + mm(probs, go_ref[i])

            zero = jnp.zeros((block, dim), F32)
            first = jnp.maximum(j - own + share - 1, 0) // share
            dk, dv = lax.fori_loop(first, blocks // share, body, (zero, zero))
            stage[j, 0] = (dk_ref[j] * scale).astype(BF16)
            stage[j, 1] = (dk * scale).astype(BF16)
            stage[j, 2] = dv.astype(BF16)
            deliver.send(j)

        def rounds(work):
            def one(turn, carry):
                for n, event in enumerate(events):
                    if back and n < back.nz:
                        pl.when(turn == event)(lambda n=n: back.pair(n))
                if back:
                    pl.when(turn == events[-1])(lambda: back.link(0))
                work(turn)
                return carry

            lax.fori_loop(0, blocks, one, 0)

        pl.when(core == 0)(lambda: rounds(down))
        pl.when(core == 1)(lambda: rounds(up))
        if back:
            for n in range(min(len(events), back.nz), back.nz):
                back.pair(n)
            for n in range(1, back.nz - 1):
                back.link(n)
            back.finish(True)
        deliver.wait()
        swap.wait()

    anywhere = pl.BlockSpec(memory_space=pl.ANY)
    inside = pl.BlockSpec(memory_space=pltpu.VMEM)
    nz, _, tok, width = shares[0].shape if shares else (0, 0, 0, 0)
    out = pl.pallas_call(
        kernel,
        in_specs=[pl.BlockSpec(memory_space=pltpu.SMEM)] + [inside] * 4
        + [anywhere] * (count + len(shares)),
        out_specs=[inside] + [anywhere] * count + [inside] * len(shares),
        out_shape=[jax.ShapeDtypeStruct((src, per, 3, block, dim), BF16)]
        + [jax.ShapeDtypeStruct(v.shape, v.dtype) for v in swaps]
        + [jax.ShapeDtypeStruct((tok, width), BF16)] * len(shares),
        scratch_shapes=[
            pltpu.VMEM((blocks, block, dim), F32),
            pltpu.VMEM((blocks, block, dim), F32),
            pltpu.VMEM((blocks, 1, block), F32),
            pltpu.SemaphoreType.DMA((count,)),
            pltpu.SemaphoreType.DMA((count,)),
            pltpu.VMEM((blocks, 3, block, dim), BF16),
            pltpu.SemaphoreType.DMA((blocks,)),
            pltpu.SemaphoreType.DMA((src, per)),
        ]
        + (Return.scratch(nz, tok, width) if shares else []),
        compiler_params=pltpu.CompilerParams(
            collective_id=collective_id, has_side_effects=True, vmem_limit_bytes=VMEM_BYTES
        ),
        name="attend_backward",
    )(bias, qkv, grad_out, out_t, lse, *swaps, *shares)
    return out[0], out[1 : 1 + count], out[1 + count :]


def expert_exchange(tokens, cots, slots, gates, weights, nh, nb, rows, collective_id):
    tok, width = tokens.shape
    half = weights[0].shape[1]
    nz, ny = nb // 2, nh // 2
    steps = nz * ny
    count = 2 * rows
    parts = 2
    chunk = min(512, width)
    full = 2 * half

    def kernel(own_ref, slot_ref, gate_ref, cot_ref, *refs):
        weight_refs = refs[0:6]
        *sum_refs, xr_out, er_out, hid_out, dpre_out, all_ref = refs[6:13]
        (
            in_w, down_w, tok_buf, cot_buf, xr, er, hid, dpre, keep, give, got,
            send_sem, recv_sem, weight_sem, tok_sem, cot_sem, row_sem, sum_sem, give_sem, got_sem, free_sem,
        ) = refs[13:]
        relay = Relay([(own_ref, all_ref, parts)], nz, ny, send_sem, recv_sem)
        y, core, z, sibling = relay.y, relay.core, relay.z, relay.sibling
        weight_copies = [
            pltpu.make_async_copy(ref, place, weight_sem.at[n])
            for n, (ref, place) in enumerate(zip(
                weight_refs,
                [in_w.at[:, pl.ds(n * half, half)] for n in range(4)]
                + [down_w.at[pl.ds(n * half, half)] for n in range(2)],
            ))
        ]
        for copy in weight_copies:
            copy.start()
        greet(relay.peers())
        relay.start()

        lanes = lax.broadcasted_iota(jnp.int32, (rows, tok), 0)

        def places(step):
            return nearest(z, step // ny, nz), nearest(y, step % ny, ny)

        def row_copies(step, slot):
            return [
                pltpu.make_async_copy(buf.at[slot], out.at[step], row_sem.at[slot, n])
                for n, (buf, out) in enumerate(
                    ((xr, xr_out), (er, er_out), (hid, hid_out), (dpre, dpre_out))
                )
            ]

        def sum_copies(step, slot):
            z_at, y_at = places(step)
            return [
                pltpu.make_async_copy(keep.at[slot, n], sum_refs[n].at[z_at, y_at], sum_sem.at[slot, n])
                for n in range(2)
            ]

        def give_copies(slot):
            return [
                pltpu.make_async_remote_copy(
                    src_ref=give.at[slot, n],
                    dst_ref=got.at[slot, n],
                    send_sem=give_sem.at[slot, n],
                    recv_sem=got_sem.at[slot, n],
                    device_id=sibling,
                    device_id_type=pl.DeviceIdType.MESH,
                )
                for n in range(2)
            ]

        def finish(step, slot):
            for n, copy in enumerate(give_copies(slot)):
                copy.wait_recv()
                for r in range(0, tok, 64):
                    here = pl.ds(r, 64)
                    keep[slot, n, here, :] = (
                        keep[slot, n, here, :].astype(F32) + got[slot, n, here, :].astype(F32)
                    ).astype(BF16)
            for copy in sum_copies(step, slot):
                copy.start()
            pl.semaphore_signal(free_sem, inc=1, device_id=sibling, device_id_type=pl.DeviceIdType.MESH)

        def block_copies(step, source, buffer, sems):
            z_at, y_at = places(step)
            return [
                pltpu.make_async_copy(source.at[z_at, c, y_at], buffer.at[n], sems.at[n])
                for n, c in enumerate((core, 1 - core))
            ]

        def cot_copies(step):
            return block_copies(step, cot_ref, cot_buf, cot_sem)

        def tok_copies(step):
            return block_copies(step, all_ref, tok_buf, tok_sem)

        def load_cots(step):
            for copy in cot_copies(step):
                copy.start()

        def load_tokens(step):
            z_at, y_at = places(step)
            z_rank, y_rank = step // ny, step % ny

            @pl.when(y_rank > 0)
            def _():
                relay.pass_on(z_at, y_at)

            for away in range(1, nz):

                @pl.when((y_rank == ny - 1) & (z_rank + 1 == away))
                def _(away=away):
                    relay.pass_on_z(away)

            relay.arrived(z_at, y_at, 1 - core)
            if isinstance(step, int):
                pltpu.make_async_copy(own_ref, tok_buf.at[0], tok_sem.at[0]).start()
                pltpu.make_async_copy(all_ref.at[z, 1 - core, y], tok_buf.at[1], tok_sem.at[1]).start()
                return
            for copy in tok_copies(step):
                copy.start()

        load_cots(0)
        load_tokens(0)
        for copy in weight_copies:
            copy.wait()

        def body(step, carry):
            z_at, y_at = places(step)
            slot = step % 2
            cores = (core, 1 - core)

            @pl.when(step >= 2)
            def _():
                for copy in row_copies(step - 2, slot):
                    copy.wait()
                for copy in sum_copies(step - 2, slot):
                    copy.wait()
                for copy in give_copies(slot):
                    copy.wait_send()

            for copy in tok_copies(step):
                copy.wait()
            picks = []
            scale_by = []
            for n, c in enumerate(cores):
                hit = lanes == slot_ref[z_at, c, y_at]
                picks.append(jnp.where(hit, 1.0, 0.0).astype(BF16))
                scale_by.append(
                    jnp.sum(jnp.where(hit, gate_ref[z_at, c, y_at], 0.0), axis=1, keepdims=True)
                )
                here = slice(n * rows, (n + 1) * rows)
                for col in range(0, width, chunk):
                    cols = slice(col, col + chunk)
                    xr[slot, here, cols] = mm(picks[n], tok_buf[n, :, cols]).astype(BF16)
            for copy in cot_copies(step):
                copy.wait()
            for n in range(2):
                here = slice(n * rows, (n + 1) * rows)
                for col in range(0, width, chunk):
                    cols = slice(col, col + chunk)
                    er[slot, here, cols] = (
                        scale_by[n] * mm(picks[n], cot_buf[n, :, cols])
                    ).astype(BF16)

            @pl.when(step + 1 < steps)
            def _():
                load_cots(step + 1)

            for m in range(0, full, half):
                gate_cols, up_cols = slice(m, m + half), slice(full + m, full + m + half)
                gate_pre = mm(xr[slot], in_w[:, gate_cols])
                up_pre = mm(xr[slot], in_w[:, up_cols])
                sig = jax.nn.sigmoid(gate_pre)
                act = gate_pre * sig
                hid[slot, :, gate_cols] = (act * up_pre).astype(BF16)
                dhid = mm(er[slot], down_w[gate_cols, :], NT).astype(BF16).astype(F32)
                dpre[slot, :, gate_cols] = (
                    dhid * up_pre * sig * (1.0 + gate_pre * (1.0 - sig))
                ).astype(BF16)
                dpre[slot, :, up_cols] = (dhid * act).astype(BF16)
            for copy in row_copies(step, slot):
                copy.start()
            for col in range(0, width, chunk):
                if col == width - chunk:

                    @pl.when(step + 1 < steps)
                    def _():
                        load_tokens(step + 1)

                cols = slice(col, col + chunk)
                part_sum = mm(hid[slot], down_w[:, cols])
                drow = mm(dpre[slot], in_w[cols, :], NT).astype(BF16)
                for n, dest in enumerate((keep, give)):
                    here = slice(n * rows, (n + 1) * rows)
                    dest[slot, 0, :, cols] = mm(picks[n], drow[here], TN).astype(BF16)
                    scaled = (part_sum[here] * scale_by[n]).astype(BF16)
                    dest[slot, 1, :, cols] = mm(picks[n], scaled, TN).astype(BF16)

            @pl.when(step >= 2)
            def _():
                pl.semaphore_wait(free_sem, 1)

            for copy in give_copies(slot):
                copy.start()

            @pl.when(step >= 1)
            def _():
                finish(step - 1, 1 - slot)

            return carry

        lax.fori_loop(0, steps, body, 0)
        last = (steps - 1) % 2
        finish(steps - 1, last)
        for step in (steps - 2, steps - 1):
            slot = step % 2
            for copy in row_copies(step, slot):
                copy.wait()
            for copy in sum_copies(step, slot):
                copy.wait()
            for copy in give_copies(slot):
                copy.wait_send()
        pl.semaphore_wait(free_sem, 2)

        relay.drain()

    anywhere = pl.BlockSpec(memory_space=pl.ANY)
    inside = pl.BlockSpec(memory_space=pltpu.VMEM)
    out = pl.pallas_call(
        kernel,
        in_specs=[anywhere, inside, inside] + [anywhere] * 7,
        out_specs=[anywhere] * 7,
        out_shape=[
            jax.ShapeDtypeStruct((nz, ny, tok, width), BF16),
            jax.ShapeDtypeStruct((nz, ny, tok, width), BF16),
            jax.ShapeDtypeStruct((steps, count, width), BF16),
            jax.ShapeDtypeStruct((steps, count, width), BF16),
            jax.ShapeDtypeStruct((steps, count, full), BF16),
            jax.ShapeDtypeStruct((steps, count, 2 * full), BF16),
            jax.ShapeDtypeStruct((nz, 2, ny, tok, width), BF16),
        ],
        scratch_shapes=[
            pltpu.VMEM((width, 2 * full), BF16),
            pltpu.VMEM((full, width), BF16),
            pltpu.VMEM((2, tok, width), BF16),
            pltpu.VMEM((2, tok, width), BF16),
            pltpu.VMEM((2, count, width), BF16),
            pltpu.VMEM((2, count, width), BF16),
            pltpu.VMEM((2, count, full), BF16),
            pltpu.VMEM((2, count, 2 * full), BF16),
            pltpu.VMEM((2, 2, tok, width), BF16),
            pltpu.VMEM((2, 2, tok, width), BF16),
            pltpu.VMEM((2, 2, tok, width), BF16),
            pltpu.SemaphoreType.DMA((5, steps, parts)),
            pltpu.SemaphoreType.DMA((2, steps, parts)),
            pltpu.SemaphoreType.DMA((6,)),
            pltpu.SemaphoreType.DMA((2,)),
            pltpu.SemaphoreType.DMA((2,)),
            pltpu.SemaphoreType.DMA((2, 4)),
            pltpu.SemaphoreType.DMA((2, 2)),
            pltpu.SemaphoreType.DMA((2, 2)),
            pltpu.SemaphoreType.DMA((2, 2)),
            pltpu.SemaphoreType.REGULAR,
        ],
        compiler_params=pltpu.CompilerParams(
            collective_id=collective_id, has_side_effects=True, vmem_limit_bytes=VMEM_BYTES
        ),
        name="expert_exchange",
    )(tokens, slots, gates, cots, *weights)
    return out[:6]


def return_sum(shares, collective_id):
    nz, ny, tok, width = shares.shape
    assert ny == 2

    def kernel(share_ref, out_ref, *scratch):
        back = Return(share_ref, out_ref, scratch)
        greet(back.peers())
        back.start()
        for turn in range(nz - 1):
            back.send(turn)
        back.finish()

    return pl.pallas_call(
        kernel,
        in_specs=[pl.BlockSpec(memory_space=pl.ANY)],
        out_specs=pl.BlockSpec(memory_space=pltpu.VMEM),
        out_shape=jax.ShapeDtypeStruct((tok, width), BF16),
        scratch_shapes=Return.scratch(nz, tok, width),
        compiler_params=pltpu.CompilerParams(
            collective_id=collective_id, has_side_effects=True, vmem_limit_bytes=VMEM_BYTES
        ),
        name="return_sum",
    )(shares)


def project_forward(normed, weights, gains, swaps, nh, nb, seqs, share, collective_id):
    tok, width = normed.shape
    tile, columns = weights[0].shape
    heads = columns // HEAD_DIM
    items = seqs * heads
    piece = tok // seqs
    span = nh * piece
    rows = nh * tok
    nz = nb // 2
    lots = nh * seqs
    count = len(swaps)

    def kernel(normed_ref, wq_ref, wk_ref, wv_ref, gain_ref, *refs):
        swap_in, refs = refs[:count], refs[count:]
        out_ref, qraw_ref, kraw_ref, inv_ref, group_ref, *refs = refs
        all_refs, refs = refs[:3], refs[3:]
        swap_out, refs = refs[:count], refs[count:]
        (
            vraw_ref, give_ref, sum_ref, norm_send, norm_recv, relay_send, relay_recv,
            sum_send, sum_recv, give_send, give_recv, swap_send, swap_recv,
        ) = refs
        head, blk = lax.axis_index("head"), lax.axis_index("blk")
        own_refs = (wq_ref, wk_ref, wv_ref)
        relay = Relay(
            [(own, everything, 1) for own, everything in zip(own_refs, all_refs)],
            nz, 1, relay_send, relay_recv, spread_y=False,
        )
        z, core = relay.z, relay.core
        swap = Swap(list(zip(swap_in, swap_out)), swap_send, swap_recv)
        others = [lax.rem(head + k, nh) for k in range(1, nh)]
        devices = [{"blk": blk, "head": other} for other in others]
        blks = [lax.rem(blk + k, nb) for k in range(1, nb)]
        greet(
            [(device, None) for device in devices]
            + [({"blk": other, "head": head}, None) for other in blks]
        )
        relay.start()

        def lines(slot):
            return pl.ds(pl.multiple_of(slot * tok, tok), tok)

        def norm_copy(k, slot):
            return pltpu.make_async_remote_copy(
                src_ref=normed_ref,
                dst_ref=group_ref.at[lines(slot)],
                send_sem=norm_send.at[k],
                recv_sem=norm_recv.at[slot],
                device_id=devices[k],
                device_id_type=pl.DeviceIdType.MESH,
            )

        def sum_copy(k, slot):
            return pltpu.make_async_remote_copy(
                src_ref=sum_ref.at[slot],
                dst_ref=sum_ref.at[slot],
                send_sem=sum_send.at[k],
                recv_sem=sum_recv.at[slot],
                device_id=devices[k],
                device_id_type=pl.DeviceIdType.MESH,
            )

        def give_copy(k, n, slot):
            return pltpu.make_async_remote_copy(
                src_ref=give_ref.at[blks[k] // share, n],
                dst_ref=out_ref.at[slot, n],
                send_sem=give_send.at[k, n],
                recv_sem=give_recv.at[slot, n],
                device_id={"blk": blks[k], "head": head},
                device_id_type=pl.DeviceIdType.MESH,
            )

        for k in range(nh - 1):
            norm_copy(k, head).start()
        swap.start()
        group_ref[lines(head), :] = normed_ref[...]
        for own, everything in zip(own_refs, all_refs):
            everything[z, core, 0] = own[...]

        raws = (qraw_ref, kraw_ref, vraw_ref)

        def multiply(rank):
            at = nearest(z, rank, nz)
            relay.arrived(at, 0, 1 - core)
            cols = pl.ds(pl.multiple_of(at * 2 * tile, 2 * tile), 2 * tile)
            for n in (2, 0, 1):
                product = mm(group_ref[:, cols], all_refs[n][at].reshape(2 * tile, columns))
                if rank == 0:
                    raws[n][...] = product
                else:
                    raws[n][...] += product

        for away in range(1, nz - 1):
            relay.pass_on_z(away)
        for k in range(nh - 1):
            norm_copy(k, others[k]).wait_recv()
        for rank in range(nz - 1):
            multiply(rank)
        relay.pass_on_z(nz - 1)
        multiply(nz - 1)

        def place(n, lot, hl):
            at, s = lot // seqs, lot % seqs
            return give_ref.at[s * heads + hl, n, pl.ds(at * piece, piece)]

        for lot in range(lots):
            here = slice(lot * piece, (lot + 1) * piece)
            for hl in range(heads):
                cols = slice(hl * HEAD_DIM, (hl + 1) * HEAD_DIM)
                place(2, lot, hl)[...] = vraw_ref[here, cols].astype(BF16)
            for n in range(2):
                total = jnp.zeros((piece, HEAD_DIM), F32)
                for hl in range(heads):
                    raw = raws[n][here, hl * HEAD_DIM : (hl + 1) * HEAD_DIM]
                    total = total + raw * raw
                sum_ref[head, n * lots + lot : n * lots + lot + 1, :] = jnp.sum(
                    total.T, axis=0, keepdims=True
                )
        for k in range(nh - 1):
            sum_copy(k, head).start()
        for k in range(nb - 1):
            give_copy(k, 2, blk).start()
        for k in range(nh - 1):
            sum_copy(k, others[k]).wait_recv()
        total_sums = sum_ref[0]
        for slot in range(1, nh):
            total_sums = total_sums + sum_ref[slot]
        inv_ref[...] = lax.rsqrt(total_sums / width + EPSILON)
        for n in range(2):
            for lot in range(lots):
                here = slice(lot * piece, (lot + 1) * piece)
                row = inv_ref[n * lots + lot : n * lots + lot + 1, :]
                inv = jnp.broadcast_to(row, (HEAD_DIM, piece)).T
                for hl in range(heads):
                    cols = slice(hl * HEAD_DIM, (hl + 1) * HEAD_DIM)
                    place(n, lot, hl)[...] = (
                        raws[n][here, cols] * inv * gain_ref[n : n + 1, cols]
                    ).astype(BF16)
            for k in range(nb - 1):
                give_copy(k, n, blk).start()
        for n in range(3):
            out_ref[blk, n] = give_ref[blk // share, n]
        for n in (2, 0, 1):
            for k in range(nb - 1):
                give_copy(k, n, blks[k]).wait_recv()
                give_copy(k, n, blk).wait_send()
        for k in range(nh - 1):
            norm_copy(k, head).wait_send()
            sum_copy(k, head).wait_send()
        swap.wait()
        relay.drain()

    anywhere = pl.BlockSpec(memory_space=pl.ANY)
    inside = pl.BlockSpec(memory_space=pltpu.VMEM)
    out = pl.pallas_call(
        kernel,
        in_specs=[inside] * 5 + [anywhere] * count,
        out_specs=[inside] * 8 + [anywhere] * count,
        out_shape=[
            jax.ShapeDtypeStruct((nb, 3, span, HEAD_DIM), BF16),
            jax.ShapeDtypeStruct((rows, columns), F32),
            jax.ShapeDtypeStruct((rows, columns), F32),
            jax.ShapeDtypeStruct((2 * lots, piece), F32),
            jax.ShapeDtypeStruct((rows, width), BF16),
        ]
        + [jax.ShapeDtypeStruct((nz, 2, 1, tile, columns), BF16)] * 3
        + [jax.ShapeDtypeStruct(v.shape, v.dtype) for v in swaps],
        scratch_shapes=[
            pltpu.VMEM((rows, columns), F32),
            pltpu.VMEM((items, 3, span, HEAD_DIM), BF16),
            pltpu.VMEM((nh, 2 * lots, piece), F32),
            pltpu.SemaphoreType.DMA((nh - 1,)),
            pltpu.SemaphoreType.DMA((nh,)),
            pltpu.SemaphoreType.DMA((5, nz, 3)),
            pltpu.SemaphoreType.DMA((2, nz, 3)),
            pltpu.SemaphoreType.DMA((nh - 1,)),
            pltpu.SemaphoreType.DMA((nh,)),
            pltpu.SemaphoreType.DMA((nb - 1, 3)),
            pltpu.SemaphoreType.DMA((nb, 3)),
            pltpu.SemaphoreType.DMA((count,)),
            pltpu.SemaphoreType.DMA((count,)),
        ],
        compiler_params=pltpu.CompilerParams(
            collective_id=collective_id, has_side_effects=True, vmem_limit_bytes=VMEM_BYTES
        ),
        name="project_forward",
    )(normed, *weights, gains, *swaps)
    gathered = [v.reshape(width, columns) for v in out[5:8]]
    return out[0], out[1:3], out[3], out[4], gathered, out[8:]


def project_backward(
    grads, raws, invs, gains, group, weights, swaps, sums, nh, nb, collective_id
):
    rows, width = group.shape
    columns = raws[0].shape[1]
    items = grads.shape[0]
    heads = columns // HEAD_DIM
    seqs = items // heads
    tok = rows // nh
    piece = tok // seqs
    nz = nb // 2
    tile = width // nb
    lots = nh * seqs
    chunk = min(512, width)
    count = len(swaps)

    def kernel(grad_ref, qraw_ref, kraw_ref, inv_ref, gain_ref, group_ref, wq_ref, wk_ref, wv_ref, *refs):
        swap_in, refs = refs[:count], refs[count:]
        share_ref, refs = refs[: len(sums)], refs[len(sums) :]
        out_ref, *refs = refs
        tile_refs, refs = refs[:3], refs[3:]
        qk_ref, product_ref, *refs = refs
        swap_out, refs = refs[:count], refs[count:]
        total_ref, refs = refs[: len(sums)], refs[len(sums) :]
        swap_send, swap_recv, *refs = refs
        chain = None
        if sums:
            chain, refs = ZReturn(refs[0], share_ref[0], total_ref[0], refs[1:5]), refs[5:]
        swap = Swap(list(zip(swap_in, swap_out)), swap_send, swap_recv)
        d_ref, sum_ref, part_ref, got_ref, sum_send, sum_recv, part_send, part_recv, *refs = refs
        give = refs[0]
        back = TileReturn(give, tile_refs, refs[1:])
        head, blk = lax.axis_index("head"), lax.axis_index("blk")
        core, z = back.core, back.z
        others = [lax.rem(head + k, nh) for k in range(1, nh)]
        devices = [{"blk": blk, "head": other} for other in others]

        def sum_copy(k, slot):
            return pltpu.make_async_remote_copy(
                src_ref=sum_ref.at[slot],
                dst_ref=sum_ref.at[slot],
                send_sem=sum_send.at[k],
                recv_sem=sum_recv.at[slot],
                device_id=devices[k],
                device_id_type=pl.DeviceIdType.MESH,
            )

        def part_copy(k):
            return pltpu.make_async_remote_copy(
                src_ref=part_ref.at[k],
                dst_ref=got_ref.at[nh - 2 - k],
                send_sem=part_send.at[k],
                recv_sem=part_recv.at[nh - 2 - k],
                device_id=devices[k],
                device_id_type=pl.DeviceIdType.MESH,
            )

        def grad_tile(n, lot, hl):
            at, s = lot // seqs, lot % seqs
            block, offset = divmod(at * piece, BLOCK)
            return grad_ref[s * heads + hl, block, n, offset : offset + piece, :]

        def upright(row):
            return jnp.broadcast_to(row, (HEAD_DIM, piece)).T

        for lot in range(lots):
            here = slice(lot * piece, (lot + 1) * piece)
            for n, raw_ref in enumerate((qraw_ref, kraw_ref)):
                total = jnp.zeros((piece, HEAD_DIM), F32)
                for hl in range(heads):
                    cols = slice(hl * HEAD_DIM, (hl + 1) * HEAD_DIM)
                    gained = grad_tile(n, lot, hl).astype(F32) * gain_ref[n : n + 1, cols]
                    total = total + gained * raw_ref[here, cols]
                sum_ref[head, n * lots + lot : n * lots + lot + 1, :] = jnp.sum(
                    total.T, axis=0, keepdims=True
                )
        greet([(device, None) for device in devices] + back.peers())
        for k in range(nh - 1):
            sum_copy(k, head).start()
        swap.start()
        edge = jnp.logical_or(z == 0, z == nz - 1)
        inner = jnp.logical_not(edge)
        if chain:
            chain.start()
            for turn in range(nz - 1):
                pl.when(edge)(lambda turn=turn: chain.send(turn))
        for lot in range(lots):
            here = slice(lot * piece, (lot + 1) * piece)
            for hl in range(heads):
                cols = slice(2 * columns + hl * HEAD_DIM, 2 * columns + (hl + 1) * HEAD_DIM)
                d_ref[here, cols] = grad_tile(2, lot, hl)
        for k in range(nh - 1):
            sum_copy(k, others[k]).wait_recv()
        total_sums = sum_ref[0]
        for slot in range(1, nh):
            total_sums = total_sums + sum_ref[slot]
        for n, raw_ref in enumerate((qraw_ref, kraw_ref)):
            gain_total = [jnp.zeros((1, HEAD_DIM), F32) for _ in range(heads)]
            for lot in range(lots):
                here = slice(lot * piece, (lot + 1) * piece)
                index = slice(n * lots + lot, n * lots + lot + 1)
                inv = upright(inv_ref[index, :])
                lean = inv * inv * inv * (upright(total_sums[index, :]) / width)
                for hl in range(heads):
                    cols = slice(hl * HEAD_DIM, (hl + 1) * HEAD_DIM)
                    grad = grad_tile(n, lot, hl).astype(F32)
                    raw = raw_ref[here, cols]
                    gain_total[hl] = gain_total[hl] + jnp.sum(grad * raw * inv, axis=0, keepdims=True)
                    d_ref[here, n * columns + hl * HEAD_DIM : n * columns + (hl + 1) * HEAD_DIM] = (
                        inv * (grad * gain_ref[n : n + 1, cols]) - raw * lean
                    ).astype(BF16)
            for hl in range(heads):
                qk_ref[n : n + 1, hl * HEAD_DIM : (hl + 1) * HEAD_DIM] = gain_total[hl]

        for turn, target in enumerate(back.targets):
            for at, dest in ((1 - core, give), (core, back.mine)):
                cols = pl.ds(pl.multiple_of((target * 2 + at) * tile, tile), tile)
                dest[target] = mm(group_ref[:, cols], d_ref[...], TN).astype(BF16)
            for part in range(back.parts):
                back.y_copy(target, part).start()
            if turn < nz - 1:
                pl.when(edge)(lambda turn=turn: back.send(turn))

        product_ref[...] = jnp.zeros_like(product_ref)

        def partial(at, store):
            lines = pl.ds(pl.multiple_of(at * tok, tok), tok)
            for col in range(0, width, chunk):
                cols = slice(col, col + chunk)
                total = mm(d_ref[lines, 0:columns], wq_ref[cols, :], NT)
                total = total + mm(d_ref[lines, columns : 2 * columns], wk_ref[cols, :], NT)
                total = total + mm(d_ref[lines, 2 * columns : 3 * columns], wv_ref[cols, :], NT)
                product_ref[:, cols] += jnp.sum(
                    total * group_ref[lines, cols].astype(F32), axis=0, keepdims=True
                )
                store(cols, total)

        sent = 0
        for k in range(nh - 1):

            def keep(cols, total, k=k):
                part_ref[k, :, cols] = total.astype(BF16)

            partial(others[k], keep)
            part_copy(k).start()
            while sent < nz - 1 and (k + 1) * (nz - 1) >= (sent + 2) * (nh - 1):
                if chain:
                    pl.when(inner)(lambda turn=sent: chain.send(turn))
                pl.when(inner)(lambda turn=sent: back.send(turn))
                sent += 1

        def keep_own(cols, total):
            out_ref[:, cols] = total

        partial(head, keep_own)
        for turn in range(sent, nz - 1):
            if chain:
                pl.when(inner)(lambda turn=turn: chain.send(turn))
            pl.when(inner)(lambda turn=turn: back.send(turn))
        for k in range(nh - 1):
            part_copy(nh - 2 - k).wait_recv()
            for r in range(0, tok, 64):
                here = pl.ds(r, 64)
                out_ref[here, :] += got_ref[k, here, :].astype(F32)
        back.finish()
        if chain:
            chain.finish()
        for k in range(nh - 1):
            sum_copy(k, head).wait_send()
            part_copy(k).wait_send()
        swap.wait()

    anywhere = pl.BlockSpec(memory_space=pl.ANY)
    inside = pl.BlockSpec(memory_space=pltpu.VMEM)
    out = pl.pallas_call(
        kernel,
        in_specs=[inside] * 9 + [anywhere] * (count + len(sums)),
        out_specs=[inside] * 6 + [anywhere] * count + [inside] * len(sums),
        out_shape=[jax.ShapeDtypeStruct((tok, width), F32)]
        + [jax.ShapeDtypeStruct((tile, columns), F32)] * 3
        + [jax.ShapeDtypeStruct((2, columns), F32), jax.ShapeDtypeStruct((1, width), F32)]
        + [jax.ShapeDtypeStruct(v.shape, v.dtype) for v in swaps]
        + [jax.ShapeDtypeStruct((tok, width), BF16)] * len(sums),
        scratch_shapes=[
            pltpu.SemaphoreType.DMA((count,)),
            pltpu.SemaphoreType.DMA((count,)),
        ]
        + ([pltpu.VMEM((nz, tok, width), BF16)] + ZReturn.scratch(nz, tok, width)) * len(sums)
        + [
            pltpu.VMEM((rows, 3 * columns), BF16),
            pltpu.VMEM((nh, 2 * lots, piece), F32),
            pltpu.VMEM((nh - 1, tok, width), BF16),
            pltpu.VMEM((nh - 1, tok, width), BF16),
            pltpu.SemaphoreType.DMA((nh - 1,)),
            pltpu.SemaphoreType.DMA((nh,)),
            pltpu.SemaphoreType.DMA((nh - 1,)),
            pltpu.SemaphoreType.DMA((nh - 1,)),
        ]
        + TileReturn.scratch(nz, tile, 3 * columns),
        compiler_params=pltpu.CompilerParams(
            collective_id=collective_id, has_side_effects=True, vmem_limit_bytes=VMEM_BYTES
        ),
        name="project_backward",
    )(grads, *raws, invs, gains, group, *weights, *swaps, *sums)
    return out[0], out[1:4], out[4], out[5], out[6 : 6 + count], out[6 + count :]


def local(
    hidden_in,
    attn_gain,
    w_query,
    w_key,
    w_value,
    query_gain,
    key_gain,
    w_out,
    ffn_gain,
    w_gate,
    w_up,
    w_down,
    routes,
    gate_weights,
    block_starts,
    cotangent,
):
    head_count = lax.axis_size("head")
    blk_count = lax.axis_size("blk")
    head_index = lax.axis_index("head")
    blk_index = lax.axis_index("blk")
    piece, seqs, width = hidden_in.shape
    span = piece * head_count
    per = span // BLOCK
    columns = w_query.shape[1]
    heads_here = columns // HEAD_DIM
    top_count = routes.shape[2]
    experts = blk_count * head_count // 2
    devices = blk_count * head_count
    tok = piece * seqs
    capacity = max(2, 5 * tok * top_count // (4 * experts))
    rows = -(-capacity // 32) * 32
    items = seqs * heads_here
    share = blk_count // items
    scale = 1.0 / math.sqrt(HEAD_DIM)
    everyone = ("blk", "head")

    def own_rows(values):
        return values.transpose(1, 0, 2).reshape(tok, values.shape[2])

    def out_rows(values):
        return values.reshape(seqs, piece, width).transpose(1, 0, 2)

    nz, ny = blk_count // 2, head_count // 2

    def flip_head(values, bit):
        return lax.ppermute(values, "head", [(h, h ^ bit) for h in range(head_count)])

    def flip_blk(values, bit):
        return lax.ppermute(values, "blk", [(b, b ^ bit) for b in range(blk_count)])


    table = jnp.concatenate([own_rows(routes).astype(F32).T, own_rows(gate_weights).T], axis=0)

    hidden_f = own_rows(hidden_in).astype(F32)
    grad_y_b = own_rows(cotangent)
    grad_y = grad_y_b.astype(F32)

    inv_one = inverse_rms(hidden_f)
    normed = (hidden_f * inv_one * attn_gain).astype(BF16)
    gain_query = lax.dynamic_slice_in_dim(query_gain, head_index * columns, columns)
    gain_key = lax.dynamic_slice_in_dim(key_gain, head_index * columns, columns)
    qk_gains = jnp.stack([gain_query, gain_key])
    out_w = lax.all_gather(w_out, "blk", axis=1, tiled=True)
    qkv, raws, invs, group, qkv_cols, (gate_other,) = project_forward(
        normed, (w_query, w_key, w_value), qk_gains, (w_gate[0],), head_count, blk_count, seqs,
        share, 5,
    )

    def to_items(values):
        parts = values.reshape(head_count, seqs, piece, heads_here, HEAD_DIM)
        parts = parts.transpose(1, 3, 0, 2, 4).reshape(items, span, HEAD_DIM)
        return jnp.repeat(parts, share, axis=0) if share > 1 else parts

    def from_items(values):
        if share > 1:
            values = values.reshape(items, share, span, HEAD_DIM).astype(F32).sum(1)
        parts = values.reshape(seqs, heads_here, head_count, piece, HEAD_DIM)
        return parts.transpose(2, 0, 3, 1, 4).reshape(head_count * tok, columns)

    def swap(values):
        return lax.all_to_all(values, "blk", split_axis=0, concat_axis=0, tiled=True)

    item = blk_index // share
    starts = lax.dynamic_index_in_dim(block_starts, item // heads_here, 0, keepdims=False)
    qkv = qkv.reshape(blk_count, 3, per, BLOCK, HEAD_DIM)
    total_blocks = blk_count * per
    key_block = jnp.arange(total_blocks, dtype=jnp.int32)
    bias = jnp.where(key_block[None, :] >= starts[:, None], 0.0, -1e30).astype(F32).reshape(-1)
    heads_out, heads_out_t, log_total, all_cots, tables, up_other, down_other = attend_forward(
        bias, qkv, grad_y_b, table, (w_up[0], w_down[0]), nz, ny, scale, share, 2
    )
    expert_weights = (w_gate[0], gate_other, w_up[0], up_other, w_down[0], down_other)

    expert = (blk_index * head_count + head_index) // 2
    named = tables[..., :top_count, :] == expert.astype(F32)
    hit = jnp.any(named, axis=-2)
    gates = jnp.sum(jnp.where(named, tables[..., top_count:, :], 0.0), axis=-2)[..., None, :]
    before = jnp.triu(jnp.ones((tok, tok), BF16), 1)
    ranks = jnp.dot(
        hit.reshape(-1, tok).astype(BF16), before, preferred_element_type=F32
    ).astype(jnp.int32)
    slots = jnp.where(hit, ranks.reshape(hit.shape), -1)[..., None, :]

    attended = from_items(heads_out.reshape(blk_count, span, HEAD_DIM)).astype(BF16)
    branch = lax.psum_scatter(
        mm(attended, out_w).astype(BF16), "head", scatter_dimension=0, tiled=True
    ).astype(F32)
    middle = hidden_f + branch
    inv_two = inverse_rms(middle)
    normed_two = (middle * inv_two * ffn_gain).astype(BF16)

    dx_share, moe_share, xr, er, hid, dpre = expert_exchange(
        normed_two, all_cots, slots, gates, expert_weights, head_count, blk_count, rows, 0
    )

    def halvings(count):
        return [1 << i for i in reversed(range(count.bit_length() - 1))]

    def halve(values, flip, bit, mine):
        pair = values.reshape((2, values.shape[0] // 2) + values.shape[1:])
        kept = lax.dynamic_index_in_dim(pair, mine, 0, keepdims=False)
        sent = lax.dynamic_index_in_dim(pair, 1 - mine, 0, keepdims=False)
        return kept, flip(sent.astype(BF16), bit)

    y_bits = [(flip_head, 2 * b, (head_index // (2 * b)) % 2) for b in halvings(ny)]
    z_bits = [(flip_blk, 2 * b, (blk_index // (2 * b)) % 2) for b in halvings(nz)]

    def give_back(values, bits):
        for flip, bit, mine in bits:
            kept, came = halve(values, flip, bit, mine)
            values = kept.astype(F32) + came.astype(F32)
        return values[0]

    if ny == 2:
        grad_normed_two = return_sum(dx_share, 1)
    else:
        grad_normed_two = give_back(dx_share.swapaxes(0, 1), y_bits)
        grad_normed_two = give_back(grad_normed_two, z_bits).astype(BF16)
    grad_normed_two, moe_share = lax.optimization_barrier((grad_normed_two, moe_share))
    grad_normed_two = grad_normed_two.astype(F32)
    xr, er = xr.reshape(-1, width), er.reshape(-1, width)
    hid, dpre = [v.reshape(-1, v.shape[-1]) for v in (hid, dpre)]
    half = w_gate.shape[2]
    dgate, dgate_other, dup, dup_other = [dpre[:, n * half : (n + 1) * half] for n in range(4)]

    halves = [
        mm(hid[:, :half], er, TN), mm(xr, dgate, TN), mm(xr, dup, TN),
        mm(hid[:, half:], er, TN), mm(xr, dgate_other, TN), mm(xr, dup_other, TN),
    ]
    gained_two = grad_normed_two * ffn_gain
    ffn_gain_part = jnp.sum(grad_normed_two * middle * inv_two, 0)
    grad_middle = (
        grad_y
        + inv_two * gained_two
        - middle * inv_two * inv_two * inv_two * jnp.mean(gained_two * middle, -1, keepdims=True)
    )
    grad_branch = grad_middle.astype(BF16)
    grad_group = lax.all_gather(grad_branch, "head", axis=0, tiled=True)
    grad_group, *halves = lax.optimization_barrier((grad_group, *halves))
    others = [v.astype(BF16) for v in halves[3:]]
    grad_attended = mm(grad_group, out_w, NT).astype(BF16)
    out_part = mm(attended, grad_group, TN)
    grad_heads = swap(to_items(grad_attended)).reshape(blk_count * per, BLOCK, HEAD_DIM)
    own_sum = ny == 2
    middle_row = half // 2
    grad_qkv, (down_first, gate_part, up_part), sums = attend_backward(
        bias, qkv, grad_heads, heads_out_t, log_total,
        (others[0][:middle_row], others[1], others[2]), [moe_share] * own_sum, scale, share, 3,
    )
    if share > 1:
        grad_qkv = grad_qkv.reshape((items, share) + grad_qkv.shape[1:])
        grad_qkv = grad_qkv.astype(F32).sum(1).astype(BF16)
    grad_normed, (grad_query, grad_key, grad_value), qk_parts, product, (down_last,), _ = (
        project_backward(
            grad_qkv, raws, invs, qk_gains, group, qkv_cols, (others[0][middle_row:],), (),
            head_count, blk_count, 4,
        )
    )
    if own_sum:
        expert_sum = sums[0].astype(F32)
    else:
        expert_sum = give_back(give_back(moe_share.swapaxes(0, 1), y_bits), z_bits)
    result = middle + expert_sum
    grad_down, grad_gate, grad_up = [
        (mine + other.astype(F32))[None]
        for mine, other in zip(
            halves[:3], (jnp.concatenate([down_first, down_last]), gate_part, up_part)
        )
    ]
    grad_normed = rounded(grad_normed)
    query_gain_part, key_gain_part = qk_parts[0], qk_parts[1]
    gained_one = grad_normed * attn_gain
    attn_gain_part = product[0] / attn_gain
    grad_hidden_in = (
        grad_middle
        + inv_one * gained_one
        - hidden_f
        * inv_one
        * inv_one
        * inv_one
        * jnp.mean(gained_one * hidden_f, -1, keepdims=True)
    )

    def over_blk(values, dim):
        return lax.psum_scatter(
            values.astype(BF16), "blk", scatter_dimension=dim, tiled=True
        ).astype(F32)

    grad_out = over_blk(out_part, 1)
    zero_width = jnp.zeros((width,), F32)
    query_gain_full = lax.dynamic_update_slice_in_dim(
        zero_width, query_gain_part, head_index * columns, 0
    )
    key_gain_full = lax.dynamic_update_slice_in_dim(
        zero_width, key_gain_part, head_index * columns, 0
    )
    square_parts = jnp.stack(
        [jnp.sum(result * result), jnp.sum(branch * branch), jnp.sum(expert_sum * expert_sum)]
    )
    stacked = jnp.concatenate(
        [attn_gain_part, ffn_gain_part, query_gain_full, key_gain_full, jnp.pad(square_parts, (0, 125))]
    ).reshape(-1, 128)
    for axis in ("head", "blk"):
        stacked = jnp.sum(lax.all_gather(stacked, axis, axis=0, tiled=False), 0)
    stacked = stacked.reshape(-1)
    totals = [stacked[4 * width : 4 * width + 3]] + [
        stacked[n * width : (n + 1) * width] for n in range(4)
    ]
    entry_count = tok * width * devices
    stream_stats = jnp.sqrt(totals[0] / entry_count + EPSILON)
    return (
        out_rows(result.astype(BF16)),
        out_rows(grad_hidden_in.astype(BF16)),
        totals[1],
        grad_query,
        grad_key,
        grad_value,
        totals[3],
        totals[4],
        grad_out,
        totals[2],
        grad_gate,
        grad_up,
        grad_down,
        stream_stats,
    )


def solution(mesh):
    rows3 = P(("blk", "head"), None, None)
    placed = (
        rows3, P(), P("blk", "head"), P("blk", "head"), P("blk", "head"), P(), P(),
        P("head", "blk"), P(), rows3, rows3, rows3, rows3, rows3, P(), rows3,
    )
    return jax.shard_map(
        local,
        mesh=mesh,
        in_specs=placed,
        out_specs=(
            rows3, rows3, P(), P("blk", "head"), P("blk", "head"), P("blk", "head"), P(), P(),
            P("head", "blk"), P(), rows3, rows3, rows3, P(),
        ),
        check_vma=False,
    )
```

```python
import functools
import math

import jax
import jax.numpy as jnp
from jax import lax
from jax.experimental import pallas as pl
from jax.experimental.pallas import tpu as pltpu
from jax.sharding import PartitionSpec as P

HEAD_DIM = 128
BLOCK = 256
EPSILON = 1e-06
F32 = jnp.float32
BF16 = jnp.bfloat16
VMEM_BYTES = 58 * 1024 * 1024

NN = (((1,), (0,)), ((), ()))
NT = (((1,), (1,)), ((), ()))
TN = (((0,), (0,)), ((), ()))


def mm(left, right, dims=NN):
    return lax.dot_general(left, right, dims, preferred_element_type=F32)


def rounded(values):
    return lax.optimization_barrier(values.astype(BF16)).astype(F32)


def inverse_rms(values):
    return lax.rsqrt(jnp.mean(values * values, axis=-1, keepdims=True) + EPSILON)


def nearest(here, rank, count):
    below = here
    above = count - 1 - here
    swing = jnp.where(rank % 2 == 1, here - (rank + 1) // 2, here + rank // 2)
    far = jnp.where(below < above, rank, count - 1 - rank)
    return jnp.where(rank <= 2 * jnp.minimum(below, above), swing, far)


def greet(peers):
    barrier = pltpu.get_barrier_semaphore()
    count = 0
    for device, condition in peers:

        def signal(device=device):
            pl.semaphore_signal(
                barrier, inc=1, device_id=device, device_id_type=pl.DeviceIdType.MESH
            )

        if condition is None:
            signal()
            count = count + 1
        else:
            pl.when(condition)(signal)
            count = count + jnp.where(condition, 1, 0)
    pl.semaphore_wait(barrier, count)


class Relay:
    def __init__(self, arrays, nz, ny, send_sem, recv_sem, spread_y=True):
        self.arrays, self.nz, self.ny = arrays, nz, ny
        self.send_sem, self.recv_sem = send_sem, recv_sem
        head, blk = lax.axis_index("head"), lax.axis_index("blk")
        x, y = head % 2, head // 2 if spread_y else 0
        self.y = y
        self.core, self.z = core, z = blk % 2, blk // 2

        def device(z_at, y_at, core_at):
            return {"blk": z_at * 2 + core_at, "head": y_at * 2 + x if spread_y else head}

        self.sibling = device(z, y, 1 - core)
        self.targets = [
            self.sibling, device(z, y + 1, core), device(z, y - 1, core),
            device(z + 1, y, core), device(z - 1, y, core),
        ]
        self.present = [None, y < ny - 1, y > 0, z < nz - 1, z > 0]
        self.ways = range(5) if spread_y else (0, 3, 4)
        self.pieces = []
        for n, (own, everything, parts) in enumerate(arrays):
            rows = own.shape[0] // parts
            for part in range(parts):
                self.pieces.append((n, pl.ds(part * rows, rows)))

    @staticmethod
    def when(condition, work):
        if condition is None:
            work()
        else:
            pl.when(condition)(work)

    def peers(self):
        return list(zip(self.targets, self.present))

    def conditions(self, z_at, y_at):
        column = y_at == self.y
        there = self.present
        return [
            None, (y_at <= self.y) & there[1], (y_at >= self.y) & there[2],
            column & (z_at <= self.z) & there[3], column & (z_at >= self.z) & there[4],
        ]

    def copy(self, z_at, y_at, core_at, piece, way, own=False):
        n, here = self.pieces[piece]
        everything = self.arrays[n][1]
        place = everything.at[z_at, core_at, y_at, here]
        return pltpu.make_async_remote_copy(
            src_ref=self.arrays[n][0].at[here] if own else place,
            dst_ref=place,
            send_sem=self.send_sem.at[way, z_at * self.ny + y_at, piece],
            recv_sem=self.recv_sem.at[core_at, z_at * self.ny + y_at, piece],
            device_id=self.targets[way],
            device_id_type=pl.DeviceIdType.MESH,
        )

    def start(self):
        for piece in range(len(self.pieces)):
            for way in reversed(self.ways):
                self.when(self.present[way], lambda way=way, piece=piece: self.copy(
                    self.z, self.y, self.core, piece, way, own=True).start())

    def keep(self, stages, sems):
        loads = [
            pltpu.make_async_copy(own, stage, sems.at[n])
            for n, ((own, _, _), stage) in enumerate(zip(self.arrays, stages))
        ]
        for copy in loads:
            copy.start()
        for copy in loads:
            copy.wait()
        stores = [
            pltpu.make_async_copy(stage, everything.at[self.z, self.core, self.y], sems.at[n])
            for n, ((_, everything, _), stage) in enumerate(zip(self.arrays, stages))
        ]
        for copy in stores:
            copy.start()
        return stores

    def arrived(self, z_at, y_at, core_at):
        for piece in range(len(self.pieces)):
            self.copy(z_at, y_at, core_at, piece, 0).wait_recv()

    def pass_on(self, z_at, y_at):
        for piece in range(len(self.pieces)):
            self.copy(z_at, y_at, self.core, piece, 0).wait_recv()
            conditions = self.conditions(z_at, y_at)
            for way in self.ways:
                self.when(conditions[way], lambda way=way, piece=piece: self.copy(
                    z_at, y_at, self.core, piece, way).start())

    def pass_on_z(self, away):
        pl.when(self.z - away >= 0)(lambda: self.pass_on(self.z - away, self.y))
        pl.when(self.z + away < self.nz)(lambda: self.pass_on(self.z + away, self.y))

    def drain(self):
        def one(index, carry):
            z_at, y_at = index // self.ny, index % self.ny
            conditions = self.conditions(z_at, y_at)
            for way in self.ways:
                for piece in range(len(self.pieces)):
                    self.when(conditions[way], lambda way=way, piece=piece: self.copy(
                        z_at, y_at, self.core, piece, way).wait_send())
            return carry

        lax.fori_loop(0, self.nz * self.ny, one, 0)


class Swap:
    def __init__(self, pairs, send_sem, recv_sem):
        head, blk = lax.axis_index("head"), lax.axis_index("blk")
        self.neighbour = {"blk": blk, "head": head + 1 - 2 * (head % 2)}
        self.copies = [
            pltpu.make_async_remote_copy(
                src_ref=source,
                dst_ref=target,
                send_sem=send_sem.at[n],
                recv_sem=recv_sem.at[n],
                device_id=self.neighbour,
                device_id_type=pl.DeviceIdType.MESH,
            )
            for n, (source, target) in enumerate(pairs)
        ]

    def peers(self):
        return [(self.neighbour, None)]

    def start(self):
        for copy in self.copies:
            copy.start()

    def wait(self):
        for copy in self.copies:
            copy.wait()


class Deliver:
    def __init__(self, stage, out_ref, send_sem, recv_sem):
        self.stage, self.out_ref = stage, out_ref
        self.send_sem, self.recv_sem = send_sem, recv_sem
        self.count, self.per = out_ref.shape[:2]
        self.blk, self.head = lax.axis_index("blk"), lax.axis_index("head")
        self.others = [lax.rem(self.blk + k, self.count) for k in range(1, self.count)]

    def device(self, blk):
        return {"blk": blk, "head": self.head}

    def peers(self):
        return [(self.device(other), None) for other in self.others]

    def copy(self, block, source, owner):
        at = lax.rem(block, self.per)
        return pltpu.make_async_remote_copy(
            src_ref=self.stage.at[block],
            dst_ref=self.out_ref.at[source, at],
            send_sem=self.send_sem.at[block],
            recv_sem=self.recv_sem.at[source, at],
            device_id=self.device(owner),
            device_id_type=pl.DeviceIdType.MESH,
        )

    def send(self, block):
        owner = block // self.per
        pl.when(owner != self.blk)(lambda: self.copy(block, self.blk, owner).start())

        @pl.when(owner == self.blk)
        def _():
            self.out_ref[self.blk, lax.rem(block, self.per)] = self.stage[block]

    def wait(self):
        for other in self.others:
            for at in range(self.per):
                self.copy(self.blk * self.per + at, other, other).wait_recv()

        def sent(block, carry):
            owner = block // self.per
            pl.when(owner != self.blk)(lambda: self.copy(block, self.blk, owner).wait_send())
            return carry

        lax.fori_loop(0, self.count * self.per, sent, 0)


class Return:
    parts = 2

    @classmethod
    def scratch(cls, nz, tok, width):
        return [
            pltpu.VMEM((nz, tok, width), BF16),
            pltpu.VMEM((nz, tok, width), BF16),
            pltpu.VMEM((nz + 1, tok, width), BF16),
            pltpu.SemaphoreType.DMA((nz, cls.parts)),
            pltpu.SemaphoreType.DMA((nz, cls.parts)),
            pltpu.SemaphoreType.DMA((nz, cls.parts)),
            pltpu.SemaphoreType.DMA((nz, cls.parts)),
            pltpu.SemaphoreType.DMA((nz + 1, cls.parts)),
        ]

    def __init__(self, share_ref, out_ref, scratch):
        self.share_ref, self.out_ref = share_ref, out_ref
        (
            self.mine, self.from_y, self.from_z,
            self.mine_sem, self.y_send, self.y_recv, self.z_send, self.z_recv,
        ) = scratch
        self.nz, tok = self.mine.shape[:2]
        self.piece = tok // self.parts
        self.step_rows = min(64, self.piece)
        head, blk = lax.axis_index("head"), lax.axis_index("blk")
        x, self.y, self.z = head % 2, head // 2, blk // 2
        self.beside = {"blk": blk, "head": (1 - self.y) * 2 + x}
        self.onward = [{"blk": blk + 2, "head": head}, {"blk": blk - 2, "head": head}]
        self.has = [self.z > 0, self.z < self.nz - 1]
        self.targets = [nearest(self.z, rank, self.nz) for rank in reversed(range(self.nz))]

    def peers(self):
        return [(self.beside, None), (self.onward[1], self.has[0]), (self.onward[0], self.has[1])]

    def cut(self, part):
        return pl.ds(part * self.piece, self.piece)

    def own_copy(self, target, part):
        return pltpu.make_async_copy(
            self.share_ref.at[target, self.y, self.cut(part)],
            self.mine.at[target, self.cut(part)],
            self.mine_sem.at[target, part],
        )

    def own_wait(self, target, part):
        self.own_copy(target, part).wait()

    def y_wait(self, target, part):
        self.y_copy(target, part).wait_recv()

    def y_drain(self):
        for target in self.targets:
            for part in range(self.parts):
                self.y_copy(target, part).wait_send()

    def y_copy(self, target, part):
        return pltpu.make_async_remote_copy(
            src_ref=self.share_ref.at[target, 1 - self.y, self.cut(part)],
            dst_ref=self.from_y.at[target, self.cut(part)],
            send_sem=self.y_send.at[target, part],
            recv_sem=self.y_recv.at[target, part],
            device_id=self.beside,
            device_id_type=pl.DeviceIdType.MESH,
        )

    def slot(self, way, target, at):
        return target if way == 0 else jnp.where(target == at, self.nz, target)

    def z_copy(self, way, target, part, at=None):
        at = (self.z + 1, self.z - 1)[way] if at is None else at
        slot = self.slot(way, target, at)
        return pltpu.make_async_remote_copy(
            src_ref=self.mine.at[target, self.cut(part)],
            dst_ref=self.from_z.at[slot, self.cut(part)],
            send_sem=self.z_send.at[target, part],
            recv_sem=self.z_recv.at[slot, part],
            device_id=self.onward[way],
            device_id_type=pl.DeviceIdType.MESH,
        )

    def start(self):
        for target in self.targets:
            for part in range(self.parts):
                self.y_copy(target, part).start()
                self.own_copy(target, part).start()

    def add(self, target, part, ways, out=None, beside=True):
        for r in range(part * self.piece, (part + 1) * self.piece, self.step_rows):
            here = pl.ds(r, self.step_rows)
            total = self.mine[target, here, :].astype(F32)
            if beside and self.from_y is not None:
                total = total + self.from_y[target, here, :].astype(F32)
            for way in ways:
                total = total + self.from_z[self.slot(way, target, self.z), here, :].astype(F32)
            if out is None:
                self.mine[target, here, :] = total.astype(BF16)
            else:
                self.store(out, here, total)

    def store(self, out, here, total):
        out[here, :] = total.astype(out.dtype)

    def send(self, turn, part=None):
        target = self.targets[turn]
        for part in range(self.parts) if part is None else (part,):
            self.own_wait(target, part)
            self.y_wait(target, part)
            for way in range(2):
                going = target > self.z if way == 0 else target < self.z

                @pl.when(going & self.has[way])
                def _(way=way, part=part):
                    self.z_copy(way, target, part, self.z).wait_recv()
                    self.add(target, part, (way,))

                @pl.when(going & jnp.logical_not(self.has[way]))
                def _(part=part):
                    self.add(target, part, ())

                @pl.when(going)
                def _(way=way, part=part):
                    self.z_copy(way, target, part).start()

    def pair(self, turn):
        target = self.targets[turn]
        for part in range(self.parts):
            self.own_wait(target, part)
            self.y_wait(target, part)
            self.add(target, part, ())
            for way in range(2):
                first = (target > self.z if way == 0 else target < self.z) & jnp.logical_not(
                    self.has[way]
                )
                pl.when(first)(lambda way=way, part=part: self.z_copy(way, target, part).start())

    def link(self, turn):
        target = self.targets[turn]
        for part in range(self.parts):
            for way in range(2):
                later = (target > self.z if way == 0 else target < self.z) & self.has[way]

                @pl.when(later)
                def _(way=way, part=part):
                    self.z_copy(way, target, part, self.z).wait_recv()
                    self.add(target, part, (way,), beside=False)
                    self.z_copy(way, target, part).start()

    def finish(self, paired=False):
        z, has = self.z, self.has
        for part in range(self.parts):
            if not paired:
                self.own_wait(z, part)
                self.y_wait(z, part)
            for way in range(2):
                pl.when(has[way])(lambda way=way, part=part: self.z_copy(way, z, part, z).wait_recv())
            for condition, ways in (
                (has[0] & has[1], (0, 1)),
                (has[0] & jnp.logical_not(has[1]), (0,)),
                (jnp.logical_not(has[0]) & has[1], (1,)),
            ):
                pl.when(condition)(
                    lambda ways=ways, part=part: self.add(z, part, ways, self.out_ref, not paired)
                )
        self.y_drain()
        for target in self.targets[:-1]:
            for part in range(self.parts):
                self.z_copy(0, target, part).wait_send()


class ZReturn(Return):
    @classmethod
    def scratch(cls, nz, tok, width):
        return [
            pltpu.VMEM((nz + 1, tok, width), BF16),
            pltpu.SemaphoreType.DMA((nz, cls.parts)),
            pltpu.SemaphoreType.DMA((nz, cls.parts)),
            pltpu.SemaphoreType.DMA((nz + 1, cls.parts)),
        ]

    def __init__(self, mine, share_ref, out_ref, scratch):
        from_z, mine_sem, z_send, z_recv = scratch
        super().__init__(
            share_ref, out_ref, (mine, None, from_z, mine_sem, None, None, z_send, z_recv)
        )

    def own_copy(self, target, part):
        return pltpu.make_async_copy(
            self.share_ref.at[target, self.cut(part)],
            self.mine.at[target, self.cut(part)],
            self.mine_sem.at[target, part],
        )

    def y_wait(self, target, part):
        pass

    def y_drain(self):
        pass

    def start(self):
        for target in self.targets:
            for part in range(self.parts):
                self.own_copy(target, part).start()


class TileReturn(Return):
    def __init__(self, give_ref, out_refs, scratch):
        super().__init__(give_ref, out_refs, scratch)
        blk = lax.axis_index("blk")
        self.core = blk % 2
        self.beside = {"blk": blk + 1 - 2 * self.core, "head": lax.axis_index("head")}

    @classmethod
    def scratch(cls, nz, tok, width):
        return [pltpu.VMEM((nz, tok, width), BF16)] + super().scratch(nz, tok, width)

    def own_copy(self, target, part):
        return None

    def own_wait(self, target, part):
        pass

    def y_copy(self, target, part):
        return pltpu.make_async_remote_copy(
            src_ref=self.share_ref.at[target, self.cut(part)],
            dst_ref=self.from_y.at[target, self.cut(part)],
            send_sem=self.y_send.at[target, part],
            recv_sem=self.y_recv.at[target, part],
            device_id=self.beside,
            device_id_type=pl.DeviceIdType.MESH,
        )

    def store(self, out, here, total):
        size = total.shape[1] // len(out)
        for n, ref in enumerate(out):
            ref[here, :] = total[:, n * size : (n + 1) * size]


def attend_forward(bias, qkv, cots, table, swaps, nz, ny, scale, share, collective_id):
    src, _, per, block, dim = qkv.shape
    blocks = src * per
    parts = 2
    events = [(blocks * 10 // 16, blocks * 3 // 16), (blocks * 14 // 16, blocks * 7 // 16)]

    count = len(swaps)

    def kernel(bias_ref, qkv_ref, cot_ref, table_ref, *refs):
        swap_in, refs = refs[:count], refs[count:]
        out_ref, out_t_ref, lse_ref, cots_ref, tables_ref, *refs = refs
        swap_out, refs = refs[:count], refs[count:]
        (
            vt_ref, cot_stage, table_stage, send_sem, recv_sem, own_sem, swap_send, swap_recv,
            out_stage, out_send, out_recv,
        ) = refs
        swap = Swap(list(zip(swap_in, swap_out)), swap_send, swap_recv)
        deliver = Deliver(out_stage, out_ref, out_send, out_recv)
        relay = Relay(
            [(cot_ref, cots_ref, parts), (table_ref, tables_ref, 1)], nz, ny, send_sem, recv_sem
        )
        greet(deliver.peers() + relay.peers()[1:3] + swap.peers())
        relay.start()
        swap.start()
        kept = relay.keep((cot_stage, table_stage), own_sem)

        def flip(j, carry):
            vt_ref[j] = qkv_ref[j // per, 2, j % per].astype(F32).T.astype(BF16)
            return carry

        lax.fori_loop(0, blocks, flip, 0)
        own = lax.axis_index("blk") % share

        def query_block(turn, carry):
            step = jnp.where(relay.core == 0, turn, blocks - 1 - turn)
            for n, event in enumerate(events):
                if n + 1 < nz:
                    pl.when(turn == jnp.where(relay.core == 0, *event))(
                        lambda n=n: relay.pass_on_z(n + 1)
                    )

            def work():
                query = qkv_ref[step // per, 0, step % per]

                def body(j, carry):
                    top, total, acc = carry
                    scores = mm(qkv_ref[j // per, 1, j % per], query, NT) * scale
                    scores = scores + bias_ref[step * blocks + j]
                    new_top = jnp.maximum(top, jnp.max(scores, axis=0, keepdims=True))
                    weights = jnp.exp(scores - new_top)
                    shrink = jnp.exp(top - new_top)
                    total = total * shrink + jnp.sum(weights, axis=0, keepdims=True)
                    acc = acc * shrink + mm(vt_ref[j], weights.astype(BF16))
                    return new_top, total, acc

                top, total, acc = lax.fori_loop(
                    0,
                    step + 1,
                    body,
                    (
                        jnp.full((1, block), -1e30, F32),
                        jnp.zeros((1, block), F32),
                        jnp.zeros((dim, block), F32),
                    ),
                )
                result = acc / total
                out_t_ref[step] = result
                out_stage[step] = result.T.astype(BF16)
                lse_ref[step] = top + jnp.log(total)

            if share == 1:
                work()
            else:
                mine = step % share == own
                pl.when(mine)(work)

                @pl.when(jnp.logical_not(mine))
                def _():
                    out_t_ref[step] = jnp.zeros((dim, block), F32)
                    out_stage[step] = jnp.zeros((block, dim), BF16)
                    lse_ref[step] = jnp.zeros((1, block), F32)

            deliver.send(step)
            return carry

        lax.fori_loop(0, blocks, query_block, 0)
        for away in range(len(events) + 1, nz):
            relay.pass_on_z(away)
        for turn in range(1, ny):
            for rank in range(nz):
                relay.pass_on(nearest(relay.z, rank, nz), nearest(relay.y, turn, ny))

        def from_sibling(index, carry):
            relay.arrived(index // ny, index % ny, 1 - relay.core)
            return carry

        lax.fori_loop(0, nz * ny, from_sibling, 0)
        relay.drain()
        deliver.wait()
        swap.wait()
        for copy in kept:
            copy.wait()

    anywhere = pl.BlockSpec(memory_space=pl.ANY)
    inside = pl.BlockSpec(memory_space=pltpu.VMEM)
    return pl.pallas_call(
        kernel,
        in_specs=[pl.BlockSpec(memory_space=pltpu.SMEM), inside, anywhere, anywhere]
        + [anywhere] * count,
        out_specs=[inside] * 3 + [anywhere] * (2 + count),
        out_shape=[
            jax.ShapeDtypeStruct((src, per, block, dim), BF16),
            jax.ShapeDtypeStruct((blocks, dim, block), F32),
            jax.ShapeDtypeStruct((blocks, 1, block), F32),
            jax.ShapeDtypeStruct((nz, 2, ny) + cots.shape, cots.dtype),
            jax.ShapeDtypeStruct((nz, 2, ny) + table.shape, table.dtype),
        ]
        + [jax.ShapeDtypeStruct(v.shape, v.dtype) for v in swaps],
        scratch_shapes=[
            pltpu.VMEM((blocks, dim, block), BF16),
            pltpu.VMEM(cots.shape, cots.dtype),
            pltpu.VMEM(table.shape, table.dtype),
            pltpu.SemaphoreType.DMA((5, nz * ny, parts + 1)),
            pltpu.SemaphoreType.DMA((2, nz * ny, parts + 1)),
            pltpu.SemaphoreType.DMA((2,)),
            pltpu.SemaphoreType.DMA((count,)),
            pltpu.SemaphoreType.DMA((count,)),
            pltpu.VMEM((blocks, block, dim), BF16),
            pltpu.SemaphoreType.DMA((blocks,)),
            pltpu.SemaphoreType.DMA((src, per)),
        ],
        compiler_params=pltpu.CompilerParams(
            collective_id=collective_id, has_side_effects=True, vmem_limit_bytes=VMEM_BYTES
        ),
        name="attend_forward",
    )(bias, qkv, cots, table, *swaps)


def attend_backward(bias, qkv, grad_out, out_t, lse, swaps, shares, scale, share, collective_id):
    src, _, per, block, dim = qkv.shape
    blocks = src * per
    count = len(swaps)
    events = [blocks * n // 16 for n in (3, 7, 13)]

    def kernel(bias_ref, qkv_ref, go_ref, out_t_ref, lse_ref, *refs):
        swap_in, refs = refs[:count], refs[count:]
        share_ref, refs = refs[: len(shares)], refs[len(shares) :]
        grad_ref, *refs = refs
        swap_out, refs = refs[:count], refs[count:]
        sum_ref, refs = refs[: len(shares)], refs[len(shares) :]
        dk_ref, dv_ref, delta_ref, swap_send, swap_recv, stage, out_send, out_recv, *refs = refs
        deliver = Deliver(stage, grad_ref, out_send, out_recv)
        swap = Swap(list(zip(swap_in, swap_out)), swap_send, swap_recv)
        back = Return(share_ref[0], sum_ref[0], refs) if shares else None
        greet(deliver.peers() + swap.peers() + (back.peers()[:1] if back else []))
        if back:
            back.start()
        swap.start()
        dk_ref[...] = jnp.zeros_like(dk_ref)
        dv_ref[...] = jnp.zeros_like(dv_ref)
        own = lax.axis_index("blk") % share
        core = lax.axis_index("blk") % 2

        def block_delta(i, carry):
            delta_ref[i] = jnp.sum(go_ref[i].astype(F32).T * out_t_ref[i], axis=0, keepdims=True)
            return carry

        lax.fori_loop(0, blocks, block_delta, 0)

        def pair(i, j):
            scores = mm(qkv_ref[j // per, 1, j % per], qkv_ref[i // per, 0, i % per], NT) * scale
            probs = jnp.exp(scores + bias_ref[i * blocks + j] - lse_ref[i])
            grad_probs = mm(qkv_ref[j // per, 2, j % per], go_ref[i], NT)
            return probs.astype(BF16), (probs * (grad_probs - delta_ref[i])).astype(BF16)

        def down(turn):
            i = blocks - 1 - turn

            def work():
                query, go = qkv_ref[i // per, 0, i % per], go_ref[i]

                def body(j, dq):
                    probs, grad_scores = pair(i, j)
                    dv_ref[j] += mm(probs, go)
                    dk_ref[j] += mm(grad_scores, query)
                    return dq + mm(grad_scores, qkv_ref[j // per, 1, j % per], TN)

                dq = lax.fori_loop(0, i + 1, body, jnp.zeros((block, dim), F32))
                stage[i, 0] = (dq * scale).astype(BF16)

            if share == 1:
                work()
            else:
                mine = i % share == own
                pl.when(mine)(work)

                @pl.when(jnp.logical_not(mine))
                def _():
                    stage[i, 0] = jnp.zeros((block, dim), BF16)

            stage[i, 1] = (dk_ref[i] * scale).astype(BF16)
            stage[i, 2] = dv_ref[i].astype(BF16)
            deliver.send(i)

        def up(j):
            key = qkv_ref[j // per, 1, j % per]

            def body(turn, carry):
                dk, dv = carry
                i = own + share * turn
                probs, grad_scores = pair(i, j)
                dk_ref[i] += mm(grad_scores, key, TN)
                query = qkv_ref[i // per, 0, i % per]
                return dk + mm(grad_scores, query), dv + mm(probs, go_ref[i])

            zero = jnp.zeros((block, dim), F32)
            first = jnp.maximum(j - own + share - 1, 0) // share
            dk, dv = lax.fori_loop(first, blocks // share, body, (zero, zero))
            stage[j, 0] = (dk_ref[j] * scale).astype(BF16)
            stage[j, 1] = (dk * scale).astype(BF16)
            stage[j, 2] = dv.astype(BF16)
            deliver.send(j)

        def rounds(work):
            def one(turn, carry):
                for n, event in enumerate(events):
                    if back and n < back.nz:
                        pl.when(turn == event)(lambda n=n: back.pair(n))
                if back:
                    pl.when(turn == events[-1])(lambda: back.link(0))
                work(turn)
                return carry

            lax.fori_loop(0, blocks, one, 0)

        pl.when(core == 0)(lambda: rounds(down))
        pl.when(core == 1)(lambda: rounds(up))
        if back:
            for n in range(min(len(events), back.nz), back.nz):
                back.pair(n)
            for n in range(1, back.nz - 1):
                back.link(n)
            back.finish(True)
        deliver.wait()
        swap.wait()

    anywhere = pl.BlockSpec(memory_space=pl.ANY)
    inside = pl.BlockSpec(memory_space=pltpu.VMEM)
    nz, _, tok, width = shares[0].shape if shares else (0, 0, 0, 0)
    out = pl.pallas_call(
        kernel,
        in_specs=[pl.BlockSpec(memory_space=pltpu.SMEM)] + [inside] * 4
        + [anywhere] * (count + len(shares)),
        out_specs=[inside] + [anywhere] * count + [inside] * len(shares),
        out_shape=[jax.ShapeDtypeStruct((src, per, 3, block, dim), BF16)]
        + [jax.ShapeDtypeStruct(v.shape, v.dtype) for v in swaps]
        + [jax.ShapeDtypeStruct((tok, width), BF16)] * len(shares),
        scratch_shapes=[
            pltpu.VMEM((blocks, block, dim), F32),
            pltpu.VMEM((blocks, block, dim), F32),
            pltpu.VMEM((blocks, 1, block), F32),
            pltpu.SemaphoreType.DMA((count,)),
            pltpu.SemaphoreType.DMA((count,)),
            pltpu.VMEM((blocks, 3, block, dim), BF16),
            pltpu.SemaphoreType.DMA((blocks,)),
            pltpu.SemaphoreType.DMA((src, per)),
        ]
        + (Return.scratch(nz, tok, width) if shares else []),
        compiler_params=pltpu.CompilerParams(
            collective_id=collective_id, has_side_effects=True, vmem_limit_bytes=VMEM_BYTES
        ),
        name="attend_backward",
    )(bias, qkv, grad_out, out_t, lse, *swaps, *shares)
    return out[0], out[1 : 1 + count], out[1 + count :]


def expert_exchange(tokens, cots, slots, gates, weights, nh, nb, rows, collective_id):
    tok, width = tokens.shape
    half = weights[0].shape[1]
    nz, ny = nb // 2, nh // 2
    steps = nz * ny
    count = 2 * rows
    parts = 2
    chunk = min(512, width)
    full = 2 * half

    def kernel(own_ref, slot_ref, gate_ref, cot_ref, *refs):
        weight_refs = refs[0:6]
        *sum_refs, xr_out, er_out, hid_out, dpre_out, all_ref = refs[6:13]
        (
            in_w, down_w, tok_buf, cot_buf, xr, er, hid, dpre, keep, give, got,
            send_sem, recv_sem, weight_sem, tok_sem, cot_sem, row_sem, sum_sem, give_sem, got_sem, free_sem,
        ) = refs[13:]
        relay = Relay([(own_ref, all_ref, parts)], nz, ny, send_sem, recv_sem)
        y, core, z, sibling = relay.y, relay.core, relay.z, relay.sibling
        weight_copies = [
            pltpu.make_async_copy(ref, place, weight_sem.at[n])
            for n, (ref, place) in enumerate(zip(
                weight_refs,
                [in_w.at[:, pl.ds(n * half, half)] for n in range(4)]
                + [down_w.at[pl.ds(n * half, half)] for n in range(2)],
            ))
        ]
        for copy in weight_copies:
            copy.start()
        greet(relay.peers())
        relay.start()

        lanes = lax.broadcasted_iota(jnp.int32, (rows, tok), 0)

        def places(step):
            return nearest(z, step // ny, nz), nearest(y, step % ny, ny)

        def row_copies(step, slot):
            return [
                pltpu.make_async_copy(buf.at[slot], out.at[step], row_sem.at[slot, n])
                for n, (buf, out) in enumerate(
                    ((xr, xr_out), (er, er_out), (hid, hid_out), (dpre, dpre_out))
                )
            ]

        def sum_copies(step, slot):
            z_at, y_at = places(step)
            return [
                pltpu.make_async_copy(keep.at[slot, n], sum_refs[n].at[z_at, y_at], sum_sem.at[slot, n])
                for n in range(2)
            ]

        def give_copies(slot):
            return [
                pltpu.make_async_remote_copy(
                    src_ref=give.at[slot, n],
                    dst_ref=got.at[slot, n],
                    send_sem=give_sem.at[slot, n],
                    recv_sem=got_sem.at[slot, n],
                    device_id=sibling,
                    device_id_type=pl.DeviceIdType.MESH,
                )
                for n in range(2)
            ]

        def finish(step, slot):
            for n, copy in enumerate(give_copies(slot)):
                copy.wait_recv()
                for r in range(0, tok, 64):
                    here = pl.ds(r, 64)
                    keep[slot, n, here, :] = (
                        keep[slot, n, here, :].astype(F32) + got[slot, n, here, :].astype(F32)
                    ).astype(BF16)
            for copy in sum_copies(step, slot):
                copy.start()
            pl.semaphore_signal(free_sem, inc=1, device_id=sibling, device_id_type=pl.DeviceIdType.MESH)

        def block_copies(step, source, buffer, sems):
            z_at, y_at = places(step)
            return [
                pltpu.make_async_copy(source.at[z_at, c, y_at], buffer.at[n], sems.at[n])
                for n, c in enumerate((core, 1 - core))
            ]

        def cot_copies(step):
            return block_copies(step, cot_ref, cot_buf, cot_sem)

        def tok_copies(step):
            return block_copies(step, all_ref, tok_buf, tok_sem)

        def load_cots(step):
            for copy in cot_copies(step):
                copy.start()

        def load_tokens(step):
            z_at, y_at = places(step)
            z_rank, y_rank = step // ny, step % ny

            @pl.when(y_rank > 0)
            def _():
                relay.pass_on(z_at, y_at)

            for away in range(1, nz):

                @pl.when((y_rank == ny - 1) & (z_rank + 1 == away))
                def _(away=away):
                    relay.pass_on_z(away)

            relay.arrived(z_at, y_at, 1 - core)
            if isinstance(step, int):
                pltpu.make_async_copy(own_ref, tok_buf.at[0], tok_sem.at[0]).start()
                pltpu.make_async_copy(all_ref.at[z, 1 - core, y], tok_buf.at[1], tok_sem.at[1]).start()
                return
            for copy in tok_copies(step):
                copy.start()

        load_cots(0)
        load_tokens(0)
        for copy in weight_copies:
            copy.wait()

        def body(step, carry):
            z_at, y_at = places(step)
            slot = step % 2
            cores = (core, 1 - core)

            @pl.when(step >= 2)
            def _():
                for copy in row_copies(step - 2, slot):
                    copy.wait()
                for copy in sum_copies(step - 2, slot):
                    copy.wait()
                for copy in give_copies(slot):
                    copy.wait_send()

            for copy in tok_copies(step):
                copy.wait()
            picks = []
            scale_by = []
            for n, c in enumerate(cores):
                hit = lanes == slot_ref[z_at, c, y_at]
                picks.append(jnp.where(hit, 1.0, 0.0).astype(BF16))
                scale_by.append(
                    jnp.sum(jnp.where(hit, gate_ref[z_at, c, y_at], 0.0), axis=1, keepdims=True)
                )
                here = slice(n * rows, (n + 1) * rows)
                for col in range(0, width, chunk):
                    cols = slice(col, col + chunk)
                    xr[slot, here, cols] = mm(picks[n], tok_buf[n, :, cols]).astype(BF16)
            for copy in cot_copies(step):
                copy.wait()
            for n in range(2):
                here = slice(n * rows, (n + 1) * rows)
                for col in range(0, width, chunk):
                    cols = slice(col, col + chunk)
                    er[slot, here, cols] = (
                        scale_by[n] * mm(picks[n], cot_buf[n, :, cols])
                    ).astype(BF16)

            @pl.when(step + 1 < steps)
            def _():
                load_cots(step + 1)

            for m in range(0, full, half):
                gate_cols, up_cols = slice(m, m + half), slice(full + m, full + m + half)
                gate_pre = mm(xr[slot], in_w[:, gate_cols])
                up_pre = mm(xr[slot], in_w[:, up_cols])
                sig = jax.nn.sigmoid(gate_pre)
                act = gate_pre * sig
                hid[slot, :, gate_cols] = (act * up_pre).astype(BF16)
                dhid = mm(er[slot], down_w[gate_cols, :], NT).astype(BF16).astype(F32)
                dpre[slot, :, gate_cols] = (
                    dhid * up_pre * sig * (1.0 + gate_pre * (1.0 - sig))
                ).astype(BF16)
                dpre[slot, :, up_cols] = (dhid * act).astype(BF16)
            for copy in row_copies(step, slot):
                copy.start()
            for col in range(0, width, chunk):
                if col == width - chunk:

                    @pl.when(step + 1 < steps)
                    def _():
                        load_tokens(step + 1)

                cols = slice(col, col + chunk)
                part_sum = mm(hid[slot], down_w[:, cols])
                drow = mm(dpre[slot], in_w[cols, :], NT).astype(BF16)
                for n, dest in enumerate((keep, give)):
                    here = slice(n * rows, (n + 1) * rows)
                    dest[slot, 0, :, cols] = mm(picks[n], drow[here], TN).astype(BF16)
                    scaled = (part_sum[here] * scale_by[n]).astype(BF16)
                    dest[slot, 1, :, cols] = mm(picks[n], scaled, TN).astype(BF16)

            @pl.when(step >= 2)
            def _():
                pl.semaphore_wait(free_sem, 1)

            for copy in give_copies(slot):
                copy.start()

            @pl.when(step >= 1)
            def _():
                finish(step - 1, 1 - slot)

            return carry

        lax.fori_loop(0, steps, body, 0)
        last = (steps - 1) % 2
        finish(steps - 1, last)
        for step in (steps - 2, steps - 1):
            slot = step % 2
            for copy in row_copies(step, slot):
                copy.wait()
            for copy in sum_copies(step, slot):
                copy.wait()
            for copy in give_copies(slot):
                copy.wait_send()
        pl.semaphore_wait(free_sem, 2)

        relay.drain()

    anywhere = pl.BlockSpec(memory_space=pl.ANY)
    inside = pl.BlockSpec(memory_space=pltpu.VMEM)
    out = pl.pallas_call(
        kernel,
        in_specs=[anywhere, inside, inside] + [anywhere] * 7,
        out_specs=[anywhere] * 7,
        out_shape=[
            jax.ShapeDtypeStruct((nz, ny, tok, width), BF16),
            jax.ShapeDtypeStruct((nz, ny, tok, width), BF16),
            jax.ShapeDtypeStruct((steps, count, width), BF16),
            jax.ShapeDtypeStruct((steps, count, width), BF16),
            jax.ShapeDtypeStruct((steps, count, full), BF16),
            jax.ShapeDtypeStruct((steps, count, 2 * full), BF16),
            jax.ShapeDtypeStruct((nz, 2, ny, tok, width), BF16),
        ],
        scratch_shapes=[
            pltpu.VMEM((width, 2 * full), BF16),
            pltpu.VMEM((full, width), BF16),
            pltpu.VMEM((2, tok, width), BF16),
            pltpu.VMEM((2, tok, width), BF16),
            pltpu.VMEM((2, count, width), BF16),
            pltpu.VMEM((2, count, width), BF16),
            pltpu.VMEM((2, count, full), BF16),
            pltpu.VMEM((2, count, 2 * full), BF16),
            pltpu.VMEM((2, 2, tok, width), BF16),
            pltpu.VMEM((2, 2, tok, width), BF16),
            pltpu.VMEM((2, 2, tok, width), BF16),
            pltpu.SemaphoreType.DMA((5, steps, parts)),
            pltpu.SemaphoreType.DMA((2, steps, parts)),
            pltpu.SemaphoreType.DMA((6,)),
            pltpu.SemaphoreType.DMA((2,)),
            pltpu.SemaphoreType.DMA((2,)),
            pltpu.SemaphoreType.DMA((2, 4)),
            pltpu.SemaphoreType.DMA((2, 2)),
            pltpu.SemaphoreType.DMA((2, 2)),
            pltpu.SemaphoreType.DMA((2, 2)),
            pltpu.SemaphoreType.REGULAR,
        ],
        compiler_params=pltpu.CompilerParams(
            collective_id=collective_id, has_side_effects=True, vmem_limit_bytes=VMEM_BYTES
        ),
        name="expert_exchange",
    )(tokens, slots, gates, cots, *weights)
    return out[:6]


def return_sum(shares, collective_id):
    nz, ny, tok, width = shares.shape
    assert ny == 2

    def kernel(share_ref, out_ref, *scratch):
        back = Return(share_ref, out_ref, scratch)
        greet(back.peers())
        back.start()
        for turn in range(nz - 1):
            back.send(turn)
        back.finish()

    return pl.pallas_call(
        kernel,
        in_specs=[pl.BlockSpec(memory_space=pl.ANY)],
        out_specs=pl.BlockSpec(memory_space=pltpu.VMEM),
        out_shape=jax.ShapeDtypeStruct((tok, width), BF16),
        scratch_shapes=Return.scratch(nz, tok, width),
        compiler_params=pltpu.CompilerParams(
            collective_id=collective_id, has_side_effects=True, vmem_limit_bytes=VMEM_BYTES
        ),
        name="return_sum",
    )(shares)


def project_forward(normed, weights, gains, swaps, nh, nb, seqs, share, collective_id):
    tok, width = normed.shape
    tile, columns = weights[0].shape
    heads = columns // HEAD_DIM
    items = seqs * heads
    piece = tok // seqs
    span = nh * piece
    rows = nh * tok
    nz = nb // 2
    lots = nh * seqs
    count = len(swaps)

    def kernel(normed_ref, wq_ref, wk_ref, wv_ref, gain_ref, *refs):
        swap_in, refs = refs[:count], refs[count:]
        out_ref, qraw_ref, kraw_ref, inv_ref, group_ref, *refs = refs
        all_refs, refs = refs[:3], refs[3:]
        swap_out, refs = refs[:count], refs[count:]
        (
            vraw_ref, give_ref, sum_ref, norm_send, norm_recv, relay_send, relay_recv,
            sum_send, sum_recv, give_send, give_recv, swap_send, swap_recv,
        ) = refs
        head, blk = lax.axis_index("head"), lax.axis_index("blk")
        own_refs = (wq_ref, wk_ref, wv_ref)
        relay = Relay(
            [(own, everything, 1) for own, everything in zip(own_refs, all_refs)],
            nz, 1, relay_send, relay_recv, spread_y=False,
        )
        z, core = relay.z, relay.core
        swap = Swap(list(zip(swap_in, swap_out)), swap_send, swap_recv)
        others = [lax.rem(head + k, nh) for k in range(1, nh)]
        devices = [{"blk": blk, "head": other} for other in others]
        blks = [lax.rem(blk + k, nb) for k in range(1, nb)]
        greet(
            [(device, None) for device in devices]
            + [({"blk": other, "head": head}, None) for other in blks]
        )
        relay.start()

        def lines(slot):
            return pl.ds(pl.multiple_of(slot * tok, tok), tok)

        def norm_copy(k, slot):
            return pltpu.make_async_remote_copy(
                src_ref=normed_ref,
                dst_ref=group_ref.at[lines(slot)],
                send_sem=norm_send.at[k],
                recv_sem=norm_recv.at[slot],
                device_id=devices[k],
                device_id_type=pl.DeviceIdType.MESH,
            )

        def sum_copy(k, slot):
            return pltpu.make_async_remote_copy(
                src_ref=sum_ref.at[slot],
                dst_ref=sum_ref.at[slot],
                send_sem=sum_send.at[k],
                recv_sem=sum_recv.at[slot],
                device_id=devices[k],
                device_id_type=pl.DeviceIdType.MESH,
            )

        def give_copy(k, n, slot):
            return pltpu.make_async_remote_copy(
                src_ref=give_ref.at[blks[k] // share, n],
                dst_ref=out_ref.at[slot, n],
                send_sem=give_send.at[k, n],
                recv_sem=give_recv.at[slot, n],
                device_id={"blk": blks[k], "head": head},
                device_id_type=pl.DeviceIdType.MESH,
            )

        for k in range(nh - 1):
            norm_copy(k, head).start()
        swap.start()
        group_ref[lines(head), :] = normed_ref[...]
        for own, everything in zip(own_refs, all_refs):
            everything[z, core, 0] = own[...]

        raws = (qraw_ref, kraw_ref, vraw_ref)

        def multiply(rank):
            at = nearest(z, rank, nz)
            relay.arrived(at, 0, 1 - core)
            cols = pl.ds(pl.multiple_of(at * 2 * tile, 2 * tile), 2 * tile)
            for n in (2, 0, 1):
                product = mm(group_ref[:, cols], all_refs[n][at].reshape(2 * tile, columns))
                if rank == 0:
                    raws[n][...] = product
                else:
                    raws[n][...] += product

        for away in range(1, nz - 1):
            relay.pass_on_z(away)
        for k in range(nh - 1):
            norm_copy(k, others[k]).wait_recv()
        for rank in range(nz - 1):
            multiply(rank)
        relay.pass_on_z(nz - 1)
        multiply(nz - 1)

        def place(n, lot, hl):
            at, s = lot // seqs, lot % seqs
            return give_ref.at[s * heads + hl, n, pl.ds(at * piece, piece)]

        for lot in range(lots):
            here = slice(lot * piece, (lot + 1) * piece)
            for hl in range(heads):
                cols = slice(hl * HEAD_DIM, (hl + 1) * HEAD_DIM)
                place(2, lot, hl)[...] = vraw_ref[here, cols].astype(BF16)
            for n in range(2):
                total = jnp.zeros((piece, HEAD_DIM), F32)
                for hl in range(heads):
                    raw = raws[n][here, hl * HEAD_DIM : (hl + 1) * HEAD_DIM]
                    total = total + raw * raw
                sum_ref[head, n * lots + lot : n * lots + lot + 1, :] = jnp.sum(
                    total.T, axis=0, keepdims=True
                )
        for k in range(nh - 1):
            sum_copy(k, head).start()
        for k in range(nb - 1):
            give_copy(k, 2, blk).start()
        for k in range(nh - 1):
            sum_copy(k, others[k]).wait_recv()
        total_sums = sum_ref[0]
        for slot in range(1, nh):
            total_sums = total_sums + sum_ref[slot]
        inv_ref[...] = lax.rsqrt(total_sums / width + EPSILON)
        for n in range(2):
            for lot in range(lots):
                here = slice(lot * piece, (lot + 1) * piece)
                row = inv_ref[n * lots + lot : n * lots + lot + 1, :]
                inv = jnp.broadcast_to(row, (HEAD_DIM, piece)).T
                for hl in range(heads):
                    cols = slice(hl * HEAD_DIM, (hl + 1) * HEAD_DIM)
                    place(n, lot, hl)[...] = (
                        raws[n][here, cols] * inv * gain_ref[n : n + 1, cols]
                    ).astype(BF16)
            for k in range(nb - 1):
                give_copy(k, n, blk).start()
        for n in range(3):
            out_ref[blk, n] = give_ref[blk // share, n]
        for n in (2, 0, 1):
            for k in range(nb - 1):
                give_copy(k, n, blks[k]).wait_recv()
                give_copy(k, n, blk).wait_send()
        for k in range(nh - 1):
            norm_copy(k, head).wait_send()
            sum_copy(k, head).wait_send()
        swap.wait()
        relay.drain()

    anywhere = pl.BlockSpec(memory_space=pl.ANY)
    inside = pl.BlockSpec(memory_space=pltpu.VMEM)
    out = pl.pallas_call(
        kernel,
        in_specs=[inside] * 5 + [anywhere] * count,
        out_specs=[inside] * 8 + [anywhere] * count,
        out_shape=[
            jax.ShapeDtypeStruct((nb, 3, span, HEAD_DIM), BF16),
            jax.ShapeDtypeStruct((rows, columns), F32),
            jax.ShapeDtypeStruct((rows, columns), F32),
            jax.ShapeDtypeStruct((2 * lots, piece), F32),
            jax.ShapeDtypeStruct((rows, width), BF16),
        ]
        + [jax.ShapeDtypeStruct((nz, 2, 1, tile, columns), BF16)] * 3
        + [jax.ShapeDtypeStruct(v.shape, v.dtype) for v in swaps],
        scratch_shapes=[
            pltpu.VMEM((rows, columns), F32),
            pltpu.VMEM((items, 3, span, HEAD_DIM), BF16),
            pltpu.VMEM((nh, 2 * lots, piece), F32),
            pltpu.SemaphoreType.DMA((nh - 1,)),
            pltpu.SemaphoreType.DMA((nh,)),
            pltpu.SemaphoreType.DMA((5, nz, 3)),
            pltpu.SemaphoreType.DMA((2, nz, 3)),
            pltpu.SemaphoreType.DMA((nh - 1,)),
            pltpu.SemaphoreType.DMA((nh,)),
            pltpu.SemaphoreType.DMA((nb - 1, 3)),
            pltpu.SemaphoreType.DMA((nb, 3)),
            pltpu.SemaphoreType.DMA((count,)),
            pltpu.SemaphoreType.DMA((count,)),
        ],
        compiler_params=pltpu.CompilerParams(
            collective_id=collective_id, has_side_effects=True, vmem_limit_bytes=VMEM_BYTES
        ),
        name="project_forward",
    )(normed, *weights, gains, *swaps)
    gathered = [v.reshape(width, columns) for v in out[5:8]]
    return out[0], out[1:3], out[3], out[4], gathered, out[8:]


def project_backward(
    grads, raws, invs, gains, group, weights, swaps, sums, stats, nh, nb, collective_id
):
    rows, width = group.shape
    columns = raws[0].shape[1]
    items = grads.shape[0]
    heads = columns // HEAD_DIM
    seqs = items // heads
    tok = rows // nh
    piece = tok // seqs
    nz = nb // 2
    tile = width // nb
    lots = nh * seqs
    chunk = min(512, width)
    count = len(swaps)

    def kernel(grad_ref, qraw_ref, kraw_ref, inv_ref, gain_ref, group_ref, wq_ref, wk_ref, wv_ref, stat_ref, *refs):
        swap_in, refs = refs[:count], refs[count:]
        share_ref, refs = refs[: len(sums)], refs[len(sums) :]
        out_ref, *refs = refs
        tile_refs, refs = refs[:3], refs[3:]
        qk_ref, product_ref, stat_out, *refs = refs
        swap_out, refs = refs[:count], refs[count:]
        total_ref, refs = refs[: len(sums)], refs[len(sums) :]
        swap_send, swap_recv, *refs = refs
        stat_own, stat_row, stat_head, stat_blk, *refs = refs
        head_send, head_recv, blk_send, blk_recv, *refs = refs
        chain = None
        if sums:
            chain, refs = ZReturn(refs[0], share_ref[0], total_ref[0], refs[1:5]), refs[5:]
        swap = Swap(list(zip(swap_in, swap_out)), swap_send, swap_recv)
        d_ref, sum_ref, part_ref, got_ref, sum_send, sum_recv, part_send, part_recv, *refs = refs
        give = refs[0]
        back = TileReturn(give, tile_refs, refs[1:])
        head, blk = lax.axis_index("head"), lax.axis_index("blk")
        core, z = back.core, back.z
        others = [lax.rem(head + k, nh) for k in range(1, nh)]
        devices = [{"blk": blk, "head": other} for other in others]
        column = [{"blk": lax.rem(blk + k, nb), "head": head} for k in range(1, nb)]

        def head_copy(k):
            return pltpu.make_async_remote_copy(
                src_ref=stat_own,
                dst_ref=stat_head.at[nh - 2 - k],
                send_sem=head_send.at[k],
                recv_sem=head_recv.at[nh - 2 - k],
                device_id=devices[k],
                device_id_type=pl.DeviceIdType.MESH,
            )

        def blk_copy(k):
            return pltpu.make_async_remote_copy(
                src_ref=stat_row,
                dst_ref=stat_blk.at[nb - 2 - k],
                send_sem=blk_send.at[k],
                recv_sem=blk_recv.at[nb - 2 - k],
                device_id=column[k],
                device_id_type=pl.DeviceIdType.MESH,
            )

        def sum_copy(k, slot):
            return pltpu.make_async_remote_copy(
                src_ref=sum_ref.at[slot],
                dst_ref=sum_ref.at[slot],
                send_sem=sum_send.at[k],
                recv_sem=sum_recv.at[slot],
                device_id=devices[k],
                device_id_type=pl.DeviceIdType.MESH,
            )

        def part_copy(k):
            return pltpu.make_async_remote_copy(
                src_ref=part_ref.at[k],
                dst_ref=got_ref.at[nh - 2 - k],
                send_sem=part_send.at[k],
                recv_sem=part_recv.at[nh - 2 - k],
                device_id=devices[k],
                device_id_type=pl.DeviceIdType.MESH,
            )

        def grad_tile(n, lot, hl):
            at, s = lot // seqs, lot % seqs
            block, offset = divmod(at * piece, BLOCK)
            return grad_ref[s * heads + hl, block, n, offset : offset + piece, :]

        def upright(row):
            return jnp.broadcast_to(row, (HEAD_DIM, piece)).T

        for lot in range(lots):
            here = slice(lot * piece, (lot + 1) * piece)
            for n, raw_ref in enumerate((qraw_ref, kraw_ref)):
                total = jnp.zeros((piece, HEAD_DIM), F32)
                for hl in range(heads):
                    cols = slice(hl * HEAD_DIM, (hl + 1) * HEAD_DIM)
                    gained = grad_tile(n, lot, hl).astype(F32) * gain_ref[n : n + 1, cols]
                    total = total + gained * raw_ref[here, cols]
                sum_ref[head, n * lots + lot : n * lots + lot + 1, :] = jnp.sum(
                    total.T, axis=0, keepdims=True
                )
        greet([(device, None) for device in devices + column])
        for k in range(nh - 1):
            sum_copy(k, head).start()
        swap.start()
        edge = jnp.logical_or(z == 0, z == nz - 1)
        inner = jnp.logical_not(edge)
        if chain:
            chain.start()
            for turn in range(nz - 1):
                pl.when(edge)(lambda turn=turn: chain.send(turn))
        for lot in range(lots):
            here = slice(lot * piece, (lot + 1) * piece)
            for hl in range(heads):
                cols = slice(2 * columns + hl * HEAD_DIM, 2 * columns + (hl + 1) * HEAD_DIM)
                d_ref[here, cols] = grad_tile(2, lot, hl)
        for k in range(nh - 1):
            sum_copy(k, others[k]).wait_recv()
        total_sums = sum_ref[0]
        for slot in range(1, nh):
            total_sums = total_sums + sum_ref[slot]
        for n, raw_ref in enumerate((qraw_ref, kraw_ref)):
            gain_total = [jnp.zeros((1, HEAD_DIM), F32) for _ in range(heads)]
            for lot in range(lots):
                here = slice(lot * piece, (lot + 1) * piece)
                index = slice(n * lots + lot, n * lots + lot + 1)
                inv = upright(inv_ref[index, :])
                lean = inv * inv * inv * (upright(total_sums[index, :]) / width)
                for hl in range(heads):
                    cols = slice(hl * HEAD_DIM, (hl + 1) * HEAD_DIM)
                    grad = grad_tile(n, lot, hl).astype(F32)
                    raw = raw_ref[here, cols]
                    gain_total[hl] = gain_total[hl] + jnp.sum(grad * raw * inv, axis=0, keepdims=True)
                    d_ref[here, n * columns + hl * HEAD_DIM : n * columns + (hl + 1) * HEAD_DIM] = (
                        inv * (grad * gain_ref[n : n + 1, cols]) - raw * lean
                    ).astype(BF16)
            for hl in range(heads):
                qk_ref[n : n + 1, hl * HEAD_DIM : (hl + 1) * HEAD_DIM] = gain_total[hl]

        for turn, target in enumerate(back.targets):
            for at, dest in ((1 - core, give), (core, back.mine)):
                cols = pl.ds(pl.multiple_of((target * 2 + at) * tile, tile), tile)
                dest[target] = mm(group_ref[:, cols], d_ref[...], TN).astype(BF16)
            for part in range(back.parts):
                back.y_copy(target, part).start()
            if turn < nz - 1:
                pl.when(edge)(lambda turn=turn: back.send(turn))

        product_ref[...] = jnp.zeros_like(product_ref)

        def partial(at, store):
            lines = pl.ds(pl.multiple_of(at * tok, tok), tok)
            for col in range(0, width, chunk):
                cols = slice(col, col + chunk)
                total = mm(d_ref[lines, 0:columns], wq_ref[cols, :], NT)
                total = total + mm(d_ref[lines, columns : 2 * columns], wk_ref[cols, :], NT)
                total = total + mm(d_ref[lines, 2 * columns : 3 * columns], wv_ref[cols, :], NT)
                product_ref[:, cols] += jnp.sum(
                    total * group_ref[lines, cols].astype(F32), axis=0, keepdims=True
                )
                store(cols, total)

        sent = 0
        for k in range(nh - 1):

            def keep(cols, total, k=k):
                part_ref[k, :, cols] = total.astype(BF16)

            partial(others[k], keep)
            part_copy(k).start()
            while sent < nz - 1 and (k + 1) * (nz - 1) >= (sent + 2) * (nh - 1):
                if chain:
                    pl.when(inner)(lambda turn=sent: chain.send(turn))
                pl.when(inner)(lambda turn=sent: back.send(turn))
                sent += 1

        def keep_own(cols, total):
            out_ref[:, cols] = total

        partial(head, keep_own)
        stat_own[...] = stat_ref[...]
        lots_wide = width // 128
        for c in range(lots_wide):
            stat_own[c : c + 1, :] = product_ref[:, c * 128 : (c + 1) * 128]
        for n in range(2):
            for c in range(columns // 128):
                line = (2 + n) * lots_wide + head * (columns // 128) + c
                stat_own[pl.ds(line, 1), :] = qk_ref[n : n + 1, c * 128 : (c + 1) * 128]
        for k in range(nh - 1):
            head_copy(k).start()
        for turn in range(sent, nz - 1):
            if chain:
                pl.when(inner)(lambda turn=turn: chain.send(turn))
            pl.when(inner)(lambda turn=turn: back.send(turn))
        total = stat_own[...]
        for k in range(nh - 1):
            head_copy(nh - 2 - k).wait_recv()
            total = total + stat_head[k]
        stat_row[...] = total
        for k in range(nb - 1):
            blk_copy(k).start()
        for k in range(nh - 1):
            part_copy(nh - 2 - k).wait_recv()
            for r in range(0, tok, 64):
                here = pl.ds(r, 64)
                out_ref[here, :] += got_ref[k, here, :].astype(F32)
        back.finish()
        if chain:
            chain.finish()
        for k in range(nh - 1):
            sum_copy(k, head).wait_send()
            part_copy(k).wait_send()
            head_copy(k).wait_send()
        total = stat_row[...]
        for k in range(nb - 1):
            blk_copy(nb - 2 - k).wait_recv()
            total = total + stat_blk[k]
        stat_out[...] = total
        for k in range(nb - 1):
            blk_copy(k).wait_send()
        swap.wait()

    anywhere = pl.BlockSpec(memory_space=pl.ANY)
    inside = pl.BlockSpec(memory_space=pltpu.VMEM)
    out = pl.pallas_call(
        kernel,
        in_specs=[inside] * 10 + [anywhere] * (count + len(sums)),
        out_specs=[inside] * 7 + [anywhere] * count + [inside] * len(sums),
        out_shape=[jax.ShapeDtypeStruct((tok, width), F32)]
        + [jax.ShapeDtypeStruct((tile, columns), F32)] * 3
        + [jax.ShapeDtypeStruct((2, columns), F32), jax.ShapeDtypeStruct((1, width), F32)]
        + [jax.ShapeDtypeStruct(stats.shape, F32)]
        + [jax.ShapeDtypeStruct(v.shape, v.dtype) for v in swaps]
        + [jax.ShapeDtypeStruct((tok, width), BF16)] * len(sums),
        scratch_shapes=[
            pltpu.SemaphoreType.DMA((count,)),
            pltpu.SemaphoreType.DMA((count,)),
        ]
        + [pltpu.VMEM(stats.shape, F32)] * 2
        + [pltpu.VMEM((n - 1,) + stats.shape, F32) for n in (nh, nb)]
        + [pltpu.SemaphoreType.DMA((n - 1,)) for n in (nh, nh, nb, nb)]
        + ([pltpu.VMEM((nz, tok, width), BF16)] + ZReturn.scratch(nz, tok, width)) * len(sums)
        + [
            pltpu.VMEM((rows, 3 * columns), BF16),
            pltpu.VMEM((nh, 2 * lots, piece), F32),
            pltpu.VMEM((nh - 1, tok, width), BF16),
            pltpu.VMEM((nh - 1, tok, width), BF16),
            pltpu.SemaphoreType.DMA((nh - 1,)),
            pltpu.SemaphoreType.DMA((nh,)),
            pltpu.SemaphoreType.DMA((nh - 1,)),
            pltpu.SemaphoreType.DMA((nh - 1,)),
        ]
        + TileReturn.scratch(nz, tile, 3 * columns),
        compiler_params=pltpu.CompilerParams(
            collective_id=collective_id, has_side_effects=True, vmem_limit_bytes=VMEM_BYTES
        ),
        name="project_backward",
    )(grads, *raws, invs, gains, group, *weights, stats, *swaps, *sums)
    return out[0], out[1:4], out[6], out[7 : 7 + count], out[7 + count :]


def local(
    hidden_in,
    attn_gain,
    w_query,
    w_key,
    w_value,
    query_gain,
    key_gain,
    w_out,
    ffn_gain,
    w_gate,
    w_up,
    w_down,
    routes,
    gate_weights,
    block_starts,
    cotangent,
):
    head_count = lax.axis_size("head")
    blk_count = lax.axis_size("blk")
    head_index = lax.axis_index("head")
    blk_index = lax.axis_index("blk")
    piece, seqs, width = hidden_in.shape
    span = piece * head_count
    per = span // BLOCK
    columns = w_query.shape[1]
    heads_here = columns // HEAD_DIM
    top_count = routes.shape[2]
    experts = blk_count * head_count // 2
    devices = blk_count * head_count
    tok = piece * seqs
    capacity = max(2, 5 * tok * top_count // (4 * experts))
    rows = -(-capacity // 32) * 32
    items = seqs * heads_here
    share = blk_count // items
    scale = 1.0 / math.sqrt(HEAD_DIM)
    everyone = ("blk", "head")

    def own_rows(values):
        return values.transpose(1, 0, 2).reshape(tok, values.shape[2])

    def out_rows(values):
        return values.reshape(seqs, piece, width).transpose(1, 0, 2)

    nz, ny = blk_count // 2, head_count // 2

    def flip_head(values, bit):
        return lax.ppermute(values, "head", [(h, h ^ bit) for h in range(head_count)])

    def flip_blk(values, bit):
        return lax.ppermute(values, "blk", [(b, b ^ bit) for b in range(blk_count)])


    table = jnp.concatenate([own_rows(routes).astype(F32).T, own_rows(gate_weights).T], axis=0)

    hidden_f = own_rows(hidden_in).astype(F32)
    grad_y_b = own_rows(cotangent)
    grad_y = grad_y_b.astype(F32)

    inv_one = inverse_rms(hidden_f)
    normed = (hidden_f * inv_one * attn_gain).astype(BF16)
    gain_query = lax.dynamic_slice_in_dim(query_gain, head_index * columns, columns)
    gain_key = lax.dynamic_slice_in_dim(key_gain, head_index * columns, columns)
    qk_gains = jnp.stack([gain_query, gain_key])
    out_w = lax.all_gather(w_out, "blk", axis=1, tiled=True)
    qkv, raws, invs, group, qkv_cols, (gate_other,) = project_forward(
        normed, (w_query, w_key, w_value), qk_gains, (w_gate[0],), head_count, blk_count, seqs,
        share, 5,
    )

    def to_items(values):
        parts = values.reshape(head_count, seqs, piece, heads_here, HEAD_DIM)
        parts = parts.transpose(1, 3, 0, 2, 4).reshape(items, span, HEAD_DIM)
        return jnp.repeat(parts, share, axis=0) if share > 1 else parts

    def from_items(values):
        if share > 1:
            values = values.reshape(items, share, span, HEAD_DIM).astype(F32).sum(1)
        parts = values.reshape(seqs, heads_here, head_count, piece, HEAD_DIM)
        return parts.transpose(2, 0, 3, 1, 4).reshape(head_count * tok, columns)

    def swap(values):
        return lax.all_to_all(values, "blk", split_axis=0, concat_axis=0, tiled=True)

    item = blk_index // share
    starts = lax.dynamic_index_in_dim(block_starts, item // heads_here, 0, keepdims=False)
    qkv = qkv.reshape(blk_count, 3, per, BLOCK, HEAD_DIM)
    total_blocks = blk_count * per
    key_block = jnp.arange(total_blocks, dtype=jnp.int32)
    bias = jnp.where(key_block[None, :] >= starts[:, None], 0.0, -1e30).astype(F32).reshape(-1)
    heads_out, heads_out_t, log_total, all_cots, tables, up_other, down_other = attend_forward(
        bias, qkv, grad_y_b, table, (w_up[0], w_down[0]), nz, ny, scale, share, 2
    )
    expert_weights = (w_gate[0], gate_other, w_up[0], up_other, w_down[0], down_other)

    expert = (blk_index * head_count + head_index) // 2
    named = tables[..., :top_count, :] == expert.astype(F32)
    hit = jnp.any(named, axis=-2)
    gates = jnp.sum(jnp.where(named, tables[..., top_count:, :], 0.0), axis=-2)[..., None, :]
    before = jnp.triu(jnp.ones((tok, tok), BF16), 1)
    ranks = jnp.dot(
        hit.reshape(-1, tok).astype(BF16), before, preferred_element_type=F32
    ).astype(jnp.int32)
    slots = jnp.where(hit, ranks.reshape(hit.shape), -1)[..., None, :]

    attended = from_items(heads_out.reshape(blk_count, span, HEAD_DIM)).astype(BF16)
    branch = lax.psum_scatter(
        mm(attended, out_w).astype(BF16), "head", scatter_dimension=0, tiled=True
    ).astype(F32)
    middle = hidden_f + branch
    inv_two = inverse_rms(middle)
    normed_two = (middle * inv_two * ffn_gain).astype(BF16)

    dx_share, moe_share, xr, er, hid, dpre = expert_exchange(
        normed_two, all_cots, slots, gates, expert_weights, head_count, blk_count, rows, 0
    )

    def halvings(count):
        return [1 << i for i in reversed(range(count.bit_length() - 1))]

    def halve(values, flip, bit, mine):
        pair = values.reshape((2, values.shape[0] // 2) + values.shape[1:])
        kept = lax.dynamic_index_in_dim(pair, mine, 0, keepdims=False)
        sent = lax.dynamic_index_in_dim(pair, 1 - mine, 0, keepdims=False)
        return kept, flip(sent.astype(BF16), bit)

    y_bits = [(flip_head, 2 * b, (head_index // (2 * b)) % 2) for b in halvings(ny)]
    z_bits = [(flip_blk, 2 * b, (blk_index // (2 * b)) % 2) for b in halvings(nz)]

    def give_back(values, bits):
        for flip, bit, mine in bits:
            kept, came = halve(values, flip, bit, mine)
            values = kept.astype(F32) + came.astype(F32)
        return values[0]

    if ny == 2:
        grad_normed_two = return_sum(dx_share, 1)
    else:
        grad_normed_two = give_back(dx_share.swapaxes(0, 1), y_bits)
        grad_normed_two = give_back(grad_normed_two, z_bits).astype(BF16)
    grad_normed_two, moe_share = lax.optimization_barrier((grad_normed_two, moe_share))
    grad_normed_two = grad_normed_two.astype(F32)
    xr, er = xr.reshape(-1, width), er.reshape(-1, width)
    hid, dpre = [v.reshape(-1, v.shape[-1]) for v in (hid, dpre)]
    half = w_gate.shape[2]
    dgate, dgate_other, dup, dup_other = [dpre[:, n * half : (n + 1) * half] for n in range(4)]

    halves = [
        mm(hid[:, :half], er, TN), mm(xr, dgate, TN), mm(xr, dup, TN),
        mm(hid[:, half:], er, TN), mm(xr, dgate_other, TN), mm(xr, dup_other, TN),
    ]
    gained_two = grad_normed_two * ffn_gain
    ffn_gain_part = jnp.sum(grad_normed_two * middle * inv_two, 0)
    grad_middle = (
        grad_y
        + inv_two * gained_two
        - middle * inv_two * inv_two * inv_two * jnp.mean(gained_two * middle, -1, keepdims=True)
    )
    grad_branch = grad_middle.astype(BF16)
    grad_group = lax.all_gather(grad_branch, "head", axis=0, tiled=True)
    grad_group, *halves = lax.optimization_barrier((grad_group, *halves))
    others = [v.astype(BF16) for v in halves[3:]]
    grad_attended = mm(grad_group, out_w, NT).astype(BF16)
    out_part = mm(attended, grad_group, TN)
    grad_heads = swap(to_items(grad_attended)).reshape(blk_count * per, BLOCK, HEAD_DIM)
    own_sum = ny == 2
    middle_row = half // 2
    grad_qkv, (down_first, gate_part, up_part), sums = attend_backward(
        bias, qkv, grad_heads, heads_out_t, log_total,
        (others[0][:middle_row], others[1], others[2]), [moe_share] * own_sum, scale, share, 3,
    )
    if share > 1:
        grad_qkv = grad_qkv.reshape((items, share) + grad_qkv.shape[1:])
        grad_qkv = grad_qkv.astype(F32).sum(1).astype(BF16)
    if own_sum:
        expert_sum = sums[0].astype(F32)
    else:
        expert_sum = give_back(give_back(moe_share.swapaxes(0, 1), y_bits), z_bits)
    result = middle + expert_sum
    square_parts = jnp.stack(
        [jnp.sum(result * result), jnp.sum(branch * branch), jnp.sum(expert_sum * expert_sum)]
    )
    zero_width = jnp.zeros((width,), F32)
    stats = jnp.concatenate(
        [zero_width, ffn_gain_part, zero_width, zero_width, jnp.pad(square_parts, (0, 8 * 128 - 3))]
    ).reshape(-1, 128)
    grad_normed, (grad_query, grad_key, grad_value), totals, (down_last,), _ = project_backward(
        grad_qkv, raws, invs, qk_gains, group, qkv_cols, (others[0][middle_row:],), (), stats,
        head_count, blk_count, 4,
    )
    grad_down, grad_gate, grad_up = [
        (mine + other.astype(F32))[None]
        for mine, other in zip(
            halves[:3], (jnp.concatenate([down_first, down_last]), gate_part, up_part)
        )
    ]
    grad_normed = rounded(grad_normed)
    gained_one = grad_normed * attn_gain
    grad_hidden_in = (
        grad_middle
        + inv_one * gained_one
        - hidden_f
        * inv_one
        * inv_one
        * inv_one
        * jnp.mean(gained_one * hidden_f, -1, keepdims=True)
    )

    def over_blk(values, dim):
        return lax.psum_scatter(
            values.astype(BF16), "blk", scatter_dimension=dim, tiled=True
        ).astype(F32)

    grad_out = over_blk(out_part, 1)
    *totals, squares = jnp.split(totals.reshape(-1), [width, 2 * width, 3 * width, 4 * width])
    entry_count = tok * width * devices
    stream_stats = jnp.sqrt(squares[:3] / entry_count + EPSILON)
    return (
        out_rows(result.astype(BF16)),
        out_rows(grad_hidden_in.astype(BF16)),
        totals[0] / attn_gain,
        grad_query,
        grad_key,
        grad_value,
        totals[2],
        totals[3],
        grad_out,
        totals[1],
        grad_gate,
        grad_up,
        grad_down,
        stream_stats,
    )


def solution(mesh):
    rows3 = P(("blk", "head"), None, None)
    placed = (
        rows3, P(), P("blk", "head"), P("blk", "head"), P("blk", "head"), P(), P(),
        P("head", "blk"), P(), rows3, rows3, rows3, rows3, rows3, P(), rows3,
    )
    return jax.shard_map(
        local,
        mesh=mesh,
        in_specs=placed,
        out_specs=(
            rows3, rows3, P(), P("blk", "head"), P("blk", "head"), P("blk", "head"), P(), P(),
            P("head", "blk"), P(), rows3, rows3, rows3, P(),
        ),
        check_vma=False,
    )
```

```python
import functools
import math

import jax
import jax.numpy as jnp
from jax import lax
from jax.experimental import pallas as pl
from jax.experimental.pallas import tpu as pltpu
from jax.sharding import PartitionSpec as P

HEAD_DIM = 128
BLOCK = 256
EPSILON = 1e-06
F32 = jnp.float32
BF16 = jnp.bfloat16
VMEM_BYTES = 58 * 1024 * 1024

NN = (((1,), (0,)), ((), ()))
NT = (((1,), (1,)), ((), ()))
TN = (((0,), (0,)), ((), ()))


def mm(left, right, dims=NN):
    return lax.dot_general(left, right, dims, preferred_element_type=F32)


def rounded(values):
    return lax.optimization_barrier(values.astype(BF16)).astype(F32)


def inverse_rms(values):
    return lax.rsqrt(jnp.mean(values * values, axis=-1, keepdims=True) + EPSILON)


def nearest(here, rank, count):
    below = here
    above = count - 1 - here
    swing = jnp.where(rank % 2 == 1, here - (rank + 1) // 2, here + rank // 2)
    far = jnp.where(below < above, rank, count - 1 - rank)
    return jnp.where(rank <= 2 * jnp.minimum(below, above), swing, far)


def greet(peers):
    barrier = pltpu.get_barrier_semaphore()
    count = 0
    for device, condition in peers:

        def signal(device=device):
            pl.semaphore_signal(
                barrier, inc=1, device_id=device, device_id_type=pl.DeviceIdType.MESH
            )

        if condition is None:
            signal()
            count = count + 1
        else:
            pl.when(condition)(signal)
            count = count + jnp.where(condition, 1, 0)
    pl.semaphore_wait(barrier, count)


class Relay:
    def __init__(self, arrays, nz, ny, send_sem, recv_sem, spread_y=True):
        self.arrays, self.nz, self.ny = arrays, nz, ny
        self.send_sem, self.recv_sem = send_sem, recv_sem
        head, blk = lax.axis_index("head"), lax.axis_index("blk")
        x, y = head % 2, head // 2 if spread_y else 0
        self.y = y
        self.core, self.z = core, z = blk % 2, blk // 2

        def device(z_at, y_at, core_at):
            return {"blk": z_at * 2 + core_at, "head": y_at * 2 + x if spread_y else head}

        self.sibling = device(z, y, 1 - core)
        self.targets = [
            self.sibling, device(z, y + 1, core), device(z, y - 1, core),
            device(z + 1, y, core), device(z - 1, y, core),
        ]
        self.present = [None, y < ny - 1, y > 0, z < nz - 1, z > 0]
        self.ways = range(5) if spread_y else (0, 3, 4)
        self.pieces = []
        for n, (own, everything, parts) in enumerate(arrays):
            rows = own.shape[0] // parts
            for part in range(parts):
                self.pieces.append((n, pl.ds(part * rows, rows)))

    @staticmethod
    def when(condition, work):
        if condition is None:
            work()
        else:
            pl.when(condition)(work)

    def peers(self):
        return list(zip(self.targets, self.present))

    def conditions(self, z_at, y_at):
        column = y_at == self.y
        there = self.present
        return [
            None, (y_at <= self.y) & there[1], (y_at >= self.y) & there[2],
            column & (z_at <= self.z) & there[3], column & (z_at >= self.z) & there[4],
        ]

    def copy(self, z_at, y_at, core_at, piece, way, own=False):
        n, here = self.pieces[piece]
        everything = self.arrays[n][1]
        place = everything.at[z_at, core_at, y_at, here]
        return pltpu.make_async_remote_copy(
            src_ref=self.arrays[n][0].at[here] if own else place,
            dst_ref=place,
            send_sem=self.send_sem.at[way, z_at * self.ny + y_at, piece],
            recv_sem=self.recv_sem.at[core_at, z_at * self.ny + y_at, piece],
            device_id=self.targets[way],
            device_id_type=pl.DeviceIdType.MESH,
        )

    def start(self):
        for piece in range(len(self.pieces)):
            for way in reversed(self.ways):
                self.when(self.present[way], lambda way=way, piece=piece: self.copy(
                    self.z, self.y, self.core, piece, way, own=True).start())

    def keep(self, stages, sems):
        loads = [
            pltpu.make_async_copy(own, stage, sems.at[n])
            for n, ((own, _, _), stage) in enumerate(zip(self.arrays, stages))
        ]
        for copy in loads:
            copy.start()
        for copy in loads:
            copy.wait()
        stores = [
            pltpu.make_async_copy(stage, everything.at[self.z, self.core, self.y], sems.at[n])
            for n, ((_, everything, _), stage) in enumerate(zip(self.arrays, stages))
        ]
        for copy in stores:
            copy.start()
        return stores

    def arrived(self, z_at, y_at, core_at):
        for piece in range(len(self.pieces)):
            self.copy(z_at, y_at, core_at, piece, 0).wait_recv()

    def pass_on(self, z_at, y_at):
        for piece in range(len(self.pieces)):
            self.copy(z_at, y_at, self.core, piece, 0).wait_recv()
            conditions = self.conditions(z_at, y_at)
            for way in self.ways:
                self.when(conditions[way], lambda way=way, piece=piece: self.copy(
                    z_at, y_at, self.core, piece, way).start())

    def pass_on_z(self, away):
        pl.when(self.z - away >= 0)(lambda: self.pass_on(self.z - away, self.y))
        pl.when(self.z + away < self.nz)(lambda: self.pass_on(self.z + away, self.y))

    def drain(self):
        def one(index, carry):
            z_at, y_at = index // self.ny, index % self.ny
            conditions = self.conditions(z_at, y_at)
            for way in self.ways:
                for piece in range(len(self.pieces)):
                    self.when(conditions[way], lambda way=way, piece=piece: self.copy(
                        z_at, y_at, self.core, piece, way).wait_send())
            return carry

        lax.fori_loop(0, self.nz * self.ny, one, 0)


class Swap:
    def __init__(self, pairs, send_sem, recv_sem):
        head, blk = lax.axis_index("head"), lax.axis_index("blk")
        self.neighbour = {"blk": blk, "head": head + 1 - 2 * (head % 2)}
        self.copies = [
            pltpu.make_async_remote_copy(
                src_ref=source,
                dst_ref=target,
                send_sem=send_sem.at[n],
                recv_sem=recv_sem.at[n],
                device_id=self.neighbour,
                device_id_type=pl.DeviceIdType.MESH,
            )
            for n, (source, target) in enumerate(pairs)
        ]

    def peers(self):
        return [(self.neighbour, None)]

    def start(self):
        for copy in self.copies:
            copy.start()

    def wait(self):
        for copy in self.copies:
            copy.wait()


class Deliver:
    def __init__(self, stage, out_ref, send_sem, recv_sem):
        self.stage, self.out_ref = stage, out_ref
        self.send_sem, self.recv_sem = send_sem, recv_sem
        self.count, self.per = out_ref.shape[:2]
        self.blk, self.head = lax.axis_index("blk"), lax.axis_index("head")
        self.others = [lax.rem(self.blk + k, self.count) for k in range(1, self.count)]

    def device(self, blk):
        return {"blk": blk, "head": self.head}

    def peers(self):
        return [(self.device(other), None) for other in self.others]

    def copy(self, block, source, owner):
        at = lax.rem(block, self.per)
        return pltpu.make_async_remote_copy(
            src_ref=self.stage.at[block],
            dst_ref=self.out_ref.at[source, at],
            send_sem=self.send_sem.at[block],
            recv_sem=self.recv_sem.at[source, at],
            device_id=self.device(owner),
            device_id_type=pl.DeviceIdType.MESH,
        )

    def send(self, block):
        owner = block // self.per
        pl.when(owner != self.blk)(lambda: self.copy(block, self.blk, owner).start())

        @pl.when(owner == self.blk)
        def _():
            self.out_ref[self.blk, lax.rem(block, self.per)] = self.stage[block]

    def wait(self):
        for other in self.others:
            for at in range(self.per):
                self.copy(self.blk * self.per + at, other, other).wait_recv()

        def sent(block, carry):
            owner = block // self.per
            pl.when(owner != self.blk)(lambda: self.copy(block, self.blk, owner).wait_send())
            return carry

        lax.fori_loop(0, self.count * self.per, sent, 0)


class Return:
    parts = 2

    @classmethod
    def scratch(cls, nz, tok, width):
        return [
            pltpu.VMEM((nz, tok, width), BF16),
            pltpu.VMEM((nz, tok, width), BF16),
            pltpu.VMEM((nz + 1, tok, width), BF16),
            pltpu.SemaphoreType.DMA((nz, cls.parts)),
            pltpu.SemaphoreType.DMA((nz, cls.parts)),
            pltpu.SemaphoreType.DMA((nz, cls.parts)),
            pltpu.SemaphoreType.DMA((nz, cls.parts)),
            pltpu.SemaphoreType.DMA((nz + 1, cls.parts)),
        ]

    def __init__(self, share_ref, out_ref, scratch):
        self.share_ref, self.out_ref = share_ref, out_ref
        (
            self.mine, self.from_y, self.from_z,
            self.mine_sem, self.y_send, self.y_recv, self.z_send, self.z_recv,
        ) = scratch
        self.nz, tok = self.mine.shape[:2]
        self.piece = tok // self.parts
        self.step_rows = min(64, self.piece)
        head, blk = lax.axis_index("head"), lax.axis_index("blk")
        x, self.y, self.z = head % 2, head // 2, blk // 2
        self.beside = {"blk": blk, "head": (1 - self.y) * 2 + x}
        self.onward = [{"blk": blk + 2, "head": head}, {"blk": blk - 2, "head": head}]
        self.has = [self.z > 0, self.z < self.nz - 1]
        self.targets = [nearest(self.z, rank, self.nz) for rank in reversed(range(self.nz))]

    def peers(self):
        return [(self.beside, None), (self.onward[1], self.has[0]), (self.onward[0], self.has[1])]

    def cut(self, part):
        return pl.ds(part * self.piece, self.piece)

    def own_copy(self, target, part):
        return pltpu.make_async_copy(
            self.share_ref.at[target, self.y, self.cut(part)],
            self.mine.at[target, self.cut(part)],
            self.mine_sem.at[target, part],
        )

    def own_wait(self, target, part):
        self.own_copy(target, part).wait()

    def y_wait(self, target, part):
        self.y_copy(target, part).wait_recv()

    def y_drain(self):
        for target in self.targets:
            for part in range(self.parts):
                self.y_copy(target, part).wait_send()

    def y_copy(self, target, part):
        return pltpu.make_async_remote_copy(
            src_ref=self.share_ref.at[target, 1 - self.y, self.cut(part)],
            dst_ref=self.from_y.at[target, self.cut(part)],
            send_sem=self.y_send.at[target, part],
            recv_sem=self.y_recv.at[target, part],
            device_id=self.beside,
            device_id_type=pl.DeviceIdType.MESH,
        )

    def slot(self, way, target, at):
        return target if way == 0 else jnp.where(target == at, self.nz, target)

    def z_copy(self, way, target, part, at=None):
        device = self.onward[way] if at is None else self.beside
        at = (self.z + 1, self.z - 1)[way] if at is None else at
        slot = self.slot(way, target, at)
        return pltpu.make_async_remote_copy(
            src_ref=self.mine.at[target, self.cut(part)],
            dst_ref=self.from_z.at[slot, self.cut(part)],
            send_sem=self.z_send.at[target, part],
            recv_sem=self.z_recv.at[slot, part],
            device_id=device,
            device_id_type=pl.DeviceIdType.MESH,
        )

    def start(self):
        for target in self.targets:
            for part in range(self.parts):
                self.y_copy(target, part).start()
                self.own_copy(target, part).start()

    def add(self, target, part, ways, out=None, beside=True):
        for r in range(part * self.piece, (part + 1) * self.piece, self.step_rows):
            here = pl.ds(r, self.step_rows)
            total = self.mine[target, here, :].astype(F32)
            if beside and self.from_y is not None:
                total = total + self.from_y[target, here, :].astype(F32)
            for way in ways:
                total = total + self.from_z[self.slot(way, target, self.z), here, :].astype(F32)
            if out is None:
                self.mine[target, here, :] = total.astype(BF16)
            else:
                self.store(out, here, total)

    def store(self, out, here, total):
        out[here, :] = total.astype(out.dtype)

    def send(self, turn, part=None):
        target = self.targets[turn]
        for part in range(self.parts) if part is None else (part,):
            self.own_wait(target, part)
            self.y_wait(target, part)
            for way in range(2):
                going = target > self.z if way == 0 else target < self.z

                @pl.when(going & self.has[way])
                def _(way=way, part=part):
                    self.z_copy(way, target, part, self.z).wait_recv()
                    self.add(target, part, (way,))

                @pl.when(going & jnp.logical_not(self.has[way]))
                def _(part=part):
                    self.add(target, part, ())

                @pl.when(going)
                def _(way=way, part=part):
                    self.z_copy(way, target, part).start()

    def pair(self, turn):
        target = self.targets[turn]
        for part in range(self.parts):
            self.own_wait(target, part)
            self.y_wait(target, part)
            self.add(target, part, ())
            for way in range(2):
                first = (target > self.z if way == 0 else target < self.z) & jnp.logical_not(
                    self.has[way]
                )
                pl.when(first)(lambda way=way, part=part: self.z_copy(way, target, part).start())

    def link(self, turn):
        target = self.targets[turn]
        for part in range(self.parts):
            for way in range(2):
                later = (target > self.z if way == 0 else target < self.z) & self.has[way]

                @pl.when(later)
                def _(way=way, part=part):
                    self.z_copy(way, target, part, self.z).wait_recv()
                    self.add(target, part, (way,), beside=False)
                    self.z_copy(way, target, part).start()

    def finish(self, paired=False):
        z, has = self.z, self.has
        for part in range(self.parts):
            if not paired:
                self.own_wait(z, part)
                self.y_wait(z, part)
            for way in range(2):
                pl.when(has[way])(lambda way=way, part=part: self.z_copy(way, z, part, z).wait_recv())
            for condition, ways in (
                (has[0] & has[1], (0, 1)),
                (has[0] & jnp.logical_not(has[1]), (0,)),
                (jnp.logical_not(has[0]) & has[1], (1,)),
            ):
                pl.when(condition)(
                    lambda ways=ways, part=part: self.add(z, part, ways, self.out_ref, not paired)
                )
        self.y_drain()
        for target in self.targets[:-1]:
            for part in range(self.parts):
                self.z_copy(0, target, part, self.z).wait_send()


class ZReturn(Return):
    @classmethod
    def scratch(cls, nz, tok, width):
        return [
            pltpu.VMEM((nz + 1, tok, width), BF16),
            pltpu.SemaphoreType.DMA((nz, cls.parts)),
            pltpu.SemaphoreType.DMA((nz, cls.parts)),
            pltpu.SemaphoreType.DMA((nz + 1, cls.parts)),
        ]

    def __init__(self, mine, share_ref, out_ref, scratch):
        from_z, mine_sem, z_send, z_recv = scratch
        super().__init__(
            share_ref, out_ref, (mine, None, from_z, mine_sem, None, None, z_send, z_recv)
        )

    def own_copy(self, target, part):
        return pltpu.make_async_copy(
            self.share_ref.at[target, self.cut(part)],
            self.mine.at[target, self.cut(part)],
            self.mine_sem.at[target, part],
        )

    def y_wait(self, target, part):
        pass

    def y_drain(self):
        pass

    def start(self):
        for target in self.targets:
            for part in range(self.parts):
                self.own_copy(target, part).start()


class TileReturn(Return):
    def __init__(self, give_ref, out_refs, scratch):
        super().__init__(give_ref, out_refs, scratch)
        blk = lax.axis_index("blk")
        self.core = blk % 2
        self.beside = {"blk": blk + 1 - 2 * self.core, "head": lax.axis_index("head")}

    @classmethod
    def scratch(cls, nz, tok, width):
        return [pltpu.VMEM((nz, tok, width), BF16)] + super().scratch(nz, tok, width)

    def own_copy(self, target, part):
        return None

    def own_wait(self, target, part):
        pass

    def y_copy(self, target, part):
        return pltpu.make_async_remote_copy(
            src_ref=self.share_ref.at[target, self.cut(part)],
            dst_ref=self.from_y.at[target, self.cut(part)],
            send_sem=self.y_send.at[target, part],
            recv_sem=self.y_recv.at[target, part],
            device_id=self.beside,
            device_id_type=pl.DeviceIdType.MESH,
        )

    def store(self, out, here, total):
        size = total.shape[1] // len(out)
        for n, ref in enumerate(out):
            ref[here, :] = total[:, n * size : (n + 1) * size]


def attend_forward(bias, qkv, cots, table, swaps, nz, ny, scale, share, collective_id):
    src, _, per, block, dim = qkv.shape
    blocks = src * per
    parts = 2
    events = [(blocks * 10 // 16, blocks * 3 // 16), (blocks * 14 // 16, blocks * 7 // 16)]

    count = len(swaps)

    def kernel(bias_ref, qkv_ref, cot_ref, table_ref, *refs):
        swap_in, refs = refs[:count], refs[count:]
        out_ref, out_t_ref, lse_ref, cots_ref, tables_ref, *refs = refs
        swap_out, refs = refs[:count], refs[count:]
        (
            vt_ref, cot_stage, table_stage, send_sem, recv_sem, own_sem, swap_send, swap_recv,
            out_stage, out_send, out_recv,
        ) = refs
        swap = Swap(list(zip(swap_in, swap_out)), swap_send, swap_recv)
        deliver = Deliver(out_stage, out_ref, out_send, out_recv)
        relay = Relay(
            [(cot_ref, cots_ref, parts), (table_ref, tables_ref, 1)], nz, ny, send_sem, recv_sem
        )
        greet(deliver.peers() + relay.peers()[1:3] + swap.peers())
        relay.start()
        swap.start()
        kept = relay.keep((cot_stage, table_stage), own_sem)

        def flip(j, carry):
            vt_ref[j] = qkv_ref[j // per, 2, j % per].astype(F32).T.astype(BF16)
            return carry

        lax.fori_loop(0, blocks, flip, 0)
        own = lax.axis_index("blk") % share

        def query_block(turn, carry):
            step = jnp.where(relay.core == 0, turn, blocks - 1 - turn)
            for n, event in enumerate(events):
                if n + 1 < nz:
                    pl.when(turn == jnp.where(relay.core == 0, *event))(
                        lambda n=n: relay.pass_on_z(n + 1)
                    )

            def work():
                query = qkv_ref[step // per, 0, step % per]

                def body(j, carry):
                    top, total, acc = carry
                    scores = mm(qkv_ref[j // per, 1, j % per], query, NT) * scale
                    scores = scores + bias_ref[step * blocks + j]
                    new_top = jnp.maximum(top, jnp.max(scores, axis=0, keepdims=True))
                    weights = jnp.exp(scores - new_top)
                    shrink = jnp.exp(top - new_top)
                    total = total * shrink + jnp.sum(weights, axis=0, keepdims=True)
                    acc = acc * shrink + mm(vt_ref[j], weights.astype(BF16))
                    return new_top, total, acc

                top, total, acc = lax.fori_loop(
                    0,
                    step + 1,
                    body,
                    (
                        jnp.full((1, block), -1e30, F32),
                        jnp.zeros((1, block), F32),
                        jnp.zeros((dim, block), F32),
                    ),
                )
                result = acc / total
                out_t_ref[step] = result
                out_stage[step] = result.T.astype(BF16)
                lse_ref[step] = top + jnp.log(total)

            if share == 1:
                work()
            else:
                mine = step % share == own
                pl.when(mine)(work)

                @pl.when(jnp.logical_not(mine))
                def _():
                    out_t_ref[step] = jnp.zeros((dim, block), F32)
                    out_stage[step] = jnp.zeros((block, dim), BF16)
                    lse_ref[step] = jnp.zeros((1, block), F32)

            deliver.send(step)
            return carry

        lax.fori_loop(0, blocks, query_block, 0)
        for away in range(len(events) + 1, nz):
            relay.pass_on_z(away)
        for turn in range(1, ny):
            for rank in range(nz):
                relay.pass_on(nearest(relay.z, rank, nz), nearest(relay.y, turn, ny))

        def from_sibling(index, carry):
            relay.arrived(index // ny, index % ny, 1 - relay.core)
            return carry

        lax.fori_loop(0, nz * ny, from_sibling, 0)
        relay.drain()
        deliver.wait()
        swap.wait()
        for copy in kept:
            copy.wait()

    anywhere = pl.BlockSpec(memory_space=pl.ANY)
    inside = pl.BlockSpec(memory_space=pltpu.VMEM)
    return pl.pallas_call(
        kernel,
        in_specs=[pl.BlockSpec(memory_space=pltpu.SMEM), inside, anywhere, anywhere]
        + [anywhere] * count,
        out_specs=[inside] * 3 + [anywhere] * (2 + count),
        out_shape=[
            jax.ShapeDtypeStruct((src, per, block, dim), BF16),
            jax.ShapeDtypeStruct((blocks, dim, block), F32),
            jax.ShapeDtypeStruct((blocks, 1, block), F32),
            jax.ShapeDtypeStruct((nz, 2, ny) + cots.shape, cots.dtype),
            jax.ShapeDtypeStruct((nz, 2, ny) + table.shape, table.dtype),
        ]
        + [jax.ShapeDtypeStruct(v.shape, v.dtype) for v in swaps],
        scratch_shapes=[
            pltpu.VMEM((blocks, dim, block), BF16),
            pltpu.VMEM(cots.shape, cots.dtype),
            pltpu.VMEM(table.shape, table.dtype),
            pltpu.SemaphoreType.DMA((5, nz * ny, parts + 1)),
            pltpu.SemaphoreType.DMA((2, nz * ny, parts + 1)),
            pltpu.SemaphoreType.DMA((2,)),
            pltpu.SemaphoreType.DMA((count,)),
            pltpu.SemaphoreType.DMA((count,)),
            pltpu.VMEM((blocks, block, dim), BF16),
            pltpu.SemaphoreType.DMA((blocks,)),
            pltpu.SemaphoreType.DMA((src, per)),
        ],
        compiler_params=pltpu.CompilerParams(
            collective_id=collective_id, has_side_effects=True, vmem_limit_bytes=VMEM_BYTES
        ),
        name="attend_forward",
    )(bias, qkv, cots, table, *swaps)


def attend_backward(bias, qkv, grad_out, out_t, lse, swaps, shares, scale, share, collective_id):
    src, _, per, block, dim = qkv.shape
    blocks = src * per
    count = len(swaps)
    events = [blocks * n // 16 for n in (3, 7, 13)]

    def kernel(bias_ref, qkv_ref, go_ref, out_t_ref, lse_ref, *refs):
        swap_in, refs = refs[:count], refs[count:]
        share_ref, refs = refs[: len(shares)], refs[len(shares) :]
        grad_ref, *refs = refs
        swap_out, refs = refs[:count], refs[count:]
        sum_ref, refs = refs[: len(shares)], refs[len(shares) :]
        dk_ref, dv_ref, delta_ref, swap_send, swap_recv, stage, out_send, out_recv, *refs = refs
        deliver = Deliver(stage, grad_ref, out_send, out_recv)
        swap = Swap(list(zip(swap_in, swap_out)), swap_send, swap_recv)
        back = Return(share_ref[0], sum_ref[0], refs) if shares else None
        greet(deliver.peers() + swap.peers() + (back.peers()[:1] if back else []))
        if back:
            back.start()
        swap.start()
        dk_ref[...] = jnp.zeros_like(dk_ref)
        dv_ref[...] = jnp.zeros_like(dv_ref)
        own = lax.axis_index("blk") % share
        core = lax.axis_index("blk") % 2

        def block_delta(i, carry):
            delta_ref[i] = jnp.sum(go_ref[i].astype(F32).T * out_t_ref[i], axis=0, keepdims=True)
            return carry

        lax.fori_loop(0, blocks, block_delta, 0)

        def pair(i, j):
            scores = mm(qkv_ref[j // per, 1, j % per], qkv_ref[i // per, 0, i % per], NT) * scale
            probs = jnp.exp(scores + bias_ref[i * blocks + j] - lse_ref[i])
            grad_probs = mm(qkv_ref[j // per, 2, j % per], go_ref[i], NT)
            return probs.astype(BF16), (probs * (grad_probs - delta_ref[i])).astype(BF16)

        def down(turn):
            i = blocks - 1 - turn

            def work():
                query, go = qkv_ref[i // per, 0, i % per], go_ref[i]

                def body(j, dq):
                    probs, grad_scores = pair(i, j)
                    dv_ref[j] += mm(probs, go)
                    dk_ref[j] += mm(grad_scores, query)
                    return dq + mm(grad_scores, qkv_ref[j // per, 1, j % per], TN)

                dq = lax.fori_loop(0, i + 1, body, jnp.zeros((block, dim), F32))
                stage[i, 0] = (dq * scale).astype(BF16)

            if share == 1:
                work()
            else:
                mine = i % share == own
                pl.when(mine)(work)

                @pl.when(jnp.logical_not(mine))
                def _():
                    stage[i, 0] = jnp.zeros((block, dim), BF16)

            stage[i, 1] = (dk_ref[i] * scale).astype(BF16)
            stage[i, 2] = dv_ref[i].astype(BF16)
            deliver.send(i)

        def up(j):
            key = qkv_ref[j // per, 1, j % per]

            def body(turn, carry):
                dk, dv = carry
                i = own + share * turn
                probs, grad_scores = pair(i, j)
                dk_ref[i] += mm(grad_scores, key, TN)
                query = qkv_ref[i // per, 0, i % per]
                return dk + mm(grad_scores, query), dv + mm(probs, go_ref[i])

            zero = jnp.zeros((block, dim), F32)
            first = jnp.maximum(j - own + share - 1, 0) // share
            dk, dv = lax.fori_loop(first, blocks // share, body, (zero, zero))
            stage[j, 0] = (dk_ref[j] * scale).astype(BF16)
            stage[j, 1] = (dk * scale).astype(BF16)
            stage[j, 2] = dv.astype(BF16)
            deliver.send(j)

        def rounds(work):
            def one(turn, carry):
                for n, event in enumerate(events):
                    if back and n < back.nz:
                        pl.when(turn == event)(lambda n=n: back.pair(n))
                if back:
                    pl.when(turn == events[-1])(lambda: back.link(0))
                work(turn)
                return carry

            lax.fori_loop(0, blocks, one, 0)

        pl.when(core == 0)(lambda: rounds(down))
        pl.when(core == 1)(lambda: rounds(up))
        if back:
            for n in range(min(len(events), back.nz), back.nz):
                back.pair(n)
            for n in range(1, back.nz - 1):
                back.link(n)
            back.finish(True)
        deliver.wait()
        swap.wait()

    anywhere = pl.BlockSpec(memory_space=pl.ANY)
    inside = pl.BlockSpec(memory_space=pltpu.VMEM)
    nz, _, tok, width = shares[0].shape if shares else (0, 0, 0, 0)
    out = pl.pallas_call(
        kernel,
        in_specs=[pl.BlockSpec(memory_space=pltpu.SMEM)] + [inside] * 4
        + [anywhere] * (count + len(shares)),
        out_specs=[inside] + [anywhere] * count + [inside] * len(shares),
        out_shape=[jax.ShapeDtypeStruct((src, per, 3, block, dim), BF16)]
        + [jax.ShapeDtypeStruct(v.shape, v.dtype) for v in swaps]
        + [jax.ShapeDtypeStruct((tok, width), BF16)] * len(shares),
        scratch_shapes=[
            pltpu.VMEM((blocks, block, dim), F32),
            pltpu.VMEM((blocks, block, dim), F32),
            pltpu.VMEM((blocks, 1, block), F32),
            pltpu.SemaphoreType.DMA((count,)),
            pltpu.SemaphoreType.DMA((count,)),
            pltpu.VMEM((blocks, 3, block, dim), BF16),
            pltpu.SemaphoreType.DMA((blocks,)),
            pltpu.SemaphoreType.DMA((src, per)),
        ]
        + (Return.scratch(nz, tok, width) if shares else []),
        compiler_params=pltpu.CompilerParams(
            collective_id=collective_id, has_side_effects=True, vmem_limit_bytes=VMEM_BYTES
        ),
        name="attend_backward",
    )(bias, qkv, grad_out, out_t, lse, *swaps, *shares)
    return out[0], out[1 : 1 + count], out[1 + count :]


def expert_exchange(tokens, cots, slots, gates, weights, nh, nb, rows, collective_id):
    tok, width = tokens.shape
    half = weights[0].shape[1]
    nz, ny = nb // 2, nh // 2
    steps = nz * ny
    count = 2 * rows
    parts = 2
    chunk = min(512, width)
    full = 2 * half

    def kernel(own_ref, slot_ref, gate_ref, cot_ref, *refs):
        weight_refs = refs[0:6]
        *sum_refs, xr_out, er_out, hid_out, dpre_out, all_ref = refs[6:13]
        (
            in_w, down_w, tok_buf, cot_buf, xr, er, hid, dpre, keep, give, got,
            send_sem, recv_sem, weight_sem, tok_sem, cot_sem, row_sem, sum_sem, give_sem, got_sem, free_sem,
        ) = refs[13:]
        relay = Relay([(own_ref, all_ref, parts)], nz, ny, send_sem, recv_sem)
        y, core, z, sibling = relay.y, relay.core, relay.z, relay.sibling
        weight_copies = [
            pltpu.make_async_copy(ref, place, weight_sem.at[n])
            for n, (ref, place) in enumerate(zip(
                weight_refs,
                [in_w.at[:, pl.ds(n * half, half)] for n in range(4)]
                + [down_w.at[pl.ds(n * half, half)] for n in range(2)],
            ))
        ]
        for copy in weight_copies:
            copy.start()
        greet(relay.peers())
        relay.start()

        lanes = lax.broadcasted_iota(jnp.int32, (rows, tok), 0)

        def places(step):
            return nearest(z, step // ny, nz), nearest(y, step % ny, ny)

        def row_copies(step, slot):
            return [
                pltpu.make_async_copy(buf.at[slot], out.at[step], row_sem.at[slot, n])
                for n, (buf, out) in enumerate(
                    ((xr, xr_out), (er, er_out), (hid, hid_out), (dpre, dpre_out))
                )
            ]

        def sum_copies(step, slot):
            z_at, y_at = places(step)
            return [
                pltpu.make_async_copy(keep.at[slot, n], sum_refs[n].at[z_at, y_at], sum_sem.at[slot, n])
                for n in range(2)
            ]

        def give_copies(slot):
            return [
                pltpu.make_async_remote_copy(
                    src_ref=give.at[slot, n],
                    dst_ref=got.at[slot, n],
                    send_sem=give_sem.at[slot, n],
                    recv_sem=got_sem.at[slot, n],
                    device_id=sibling,
                    device_id_type=pl.DeviceIdType.MESH,
                )
                for n in range(2)
            ]

        def finish(step, slot):
            for n, copy in enumerate(give_copies(slot)):
                copy.wait_recv()
                for r in range(0, tok, 64):
                    here = pl.ds(r, 64)
                    keep[slot, n, here, :] = (
                        keep[slot, n, here, :].astype(F32) + got[slot, n, here, :].astype(F32)
                    ).astype(BF16)
            for copy in sum_copies(step, slot):
                copy.start()
            pl.semaphore_signal(free_sem, inc=1, device_id=sibling, device_id_type=pl.DeviceIdType.MESH)

        def block_copies(step, source, buffer, sems):
            z_at, y_at = places(step)
            return [
                pltpu.make_async_copy(source.at[z_at, c, y_at], buffer.at[n], sems.at[n])
                for n, c in enumerate((core, 1 - core))
            ]

        def cot_copies(step):
            return block_copies(step, cot_ref, cot_buf, cot_sem)

        def tok_copies(step):
            return block_copies(step, all_ref, tok_buf, tok_sem)

        def load_cots(step):
            for copy in cot_copies(step):
                copy.start()

        def load_tokens(step):
            z_at, y_at = places(step)
            z_rank, y_rank = step // ny, step % ny

            @pl.when(y_rank > 0)
            def _():
                relay.pass_on(z_at, y_at)

            for away in range(1, nz):

                @pl.when((y_rank == ny - 1) & (z_rank + 1 == away))
                def _(away=away):
                    relay.pass_on_z(away)

            relay.arrived(z_at, y_at, 1 - core)
            if isinstance(step, int):
                pltpu.make_async_copy(own_ref, tok_buf.at[0], tok_sem.at[0]).start()
                pltpu.make_async_copy(all_ref.at[z, 1 - core, y], tok_buf.at[1], tok_sem.at[1]).start()
                return
            for copy in tok_copies(step):
                copy.start()

        load_cots(0)
        load_tokens(0)
        for copy in weight_copies:
            copy.wait()

        def body(step, carry):
            z_at, y_at = places(step)
            slot = step % 2
            cores = (core, 1 - core)

            @pl.when(step >= 2)
            def _():
                for copy in row_copies(step - 2, slot):
                    copy.wait()
                for copy in sum_copies(step - 2, slot):
                    copy.wait()
                for copy in give_copies(slot):
                    copy.wait_send()

            for copy in tok_copies(step):
                copy.wait()
            picks = []
            scale_by = []
            for n, c in enumerate(cores):
                hit = lanes == slot_ref[z_at, c, y_at]
                picks.append(jnp.where(hit, 1.0, 0.0).astype(BF16))
                scale_by.append(
                    jnp.sum(jnp.where(hit, gate_ref[z_at, c, y_at], 0.0), axis=1, keepdims=True)
                )
                here = slice(n * rows, (n + 1) * rows)
                for col in range(0, width, chunk):
                    cols = slice(col, col + chunk)
                    xr[slot, here, cols] = mm(picks[n], tok_buf[n, :, cols]).astype(BF16)
            for copy in cot_copies(step):
                copy.wait()
            for n in range(2):
                here = slice(n * rows, (n + 1) * rows)
                for col in range(0, width, chunk):
                    cols = slice(col, col + chunk)
                    er[slot, here, cols] = (
                        scale_by[n] * mm(picks[n], cot_buf[n, :, cols])
                    ).astype(BF16)

            @pl.when(step + 1 < steps)
            def _():
                load_cots(step + 1)

            for m in range(0, full, half):
                gate_cols, up_cols = slice(m, m + half), slice(full + m, full + m + half)
                gate_pre = mm(xr[slot], in_w[:, gate_cols])
                up_pre = mm(xr[slot], in_w[:, up_cols])
                sig = jax.nn.sigmoid(gate_pre)
                act = gate_pre * sig
                hid[slot, :, gate_cols] = (act * up_pre).astype(BF16)
                dhid = mm(er[slot], down_w[gate_cols, :], NT).astype(BF16).astype(F32)
                dpre[slot, :, gate_cols] = (
                    dhid * up_pre * sig * (1.0 + gate_pre * (1.0 - sig))
                ).astype(BF16)
                dpre[slot, :, up_cols] = (dhid * act).astype(BF16)
            for copy in row_copies(step, slot):
                copy.start()
            for col in range(0, width, chunk):
                if col == width - chunk:

                    @pl.when(step + 1 < steps)
                    def _():
                        load_tokens(step + 1)

                cols = slice(col, col + chunk)
                part_sum = mm(hid[slot], down_w[:, cols])
                drow = mm(dpre[slot], in_w[cols, :], NT).astype(BF16)
                for n, dest in enumerate((keep, give)):
                    here = slice(n * rows, (n + 1) * rows)
                    dest[slot, 0, :, cols] = mm(picks[n], drow[here], TN).astype(BF16)
                    scaled = (part_sum[here] * scale_by[n]).astype(BF16)
                    dest[slot, 1, :, cols] = mm(picks[n], scaled, TN).astype(BF16)

            @pl.when(step >= 2)
            def _():
                pl.semaphore_wait(free_sem, 1)

            for copy in give_copies(slot):
                copy.start()

            @pl.when(step >= 1)
            def _():
                finish(step - 1, 1 - slot)

            return carry

        lax.fori_loop(0, steps, body, 0)
        last = (steps - 1) % 2
        finish(steps - 1, last)
        for step in (steps - 2, steps - 1):
            slot = step % 2
            for copy in row_copies(step, slot):
                copy.wait()
            for copy in sum_copies(step, slot):
                copy.wait()
            for copy in give_copies(slot):
                copy.wait_send()
        pl.semaphore_wait(free_sem, 2)

        relay.drain()

    anywhere = pl.BlockSpec(memory_space=pl.ANY)
    inside = pl.BlockSpec(memory_space=pltpu.VMEM)
    out = pl.pallas_call(
        kernel,
        in_specs=[anywhere, inside, inside] + [anywhere] * 7,
        out_specs=[anywhere] * 7,
        out_shape=[
            jax.ShapeDtypeStruct((nz, ny, tok, width), BF16),
            jax.ShapeDtypeStruct((nz, ny, tok, width), BF16),
            jax.ShapeDtypeStruct((steps, count, width), BF16),
            jax.ShapeDtypeStruct((steps, count, width), BF16),
            jax.ShapeDtypeStruct((steps, count, full), BF16),
            jax.ShapeDtypeStruct((steps, count, 2 * full), BF16),
            jax.ShapeDtypeStruct((nz, 2, ny, tok, width), BF16),
        ],
        scratch_shapes=[
            pltpu.VMEM((width, 2 * full), BF16),
            pltpu.VMEM((full, width), BF16),
            pltpu.VMEM((2, tok, width), BF16),
            pltpu.VMEM((2, tok, width), BF16),
            pltpu.VMEM((2, count, width), BF16),
            pltpu.VMEM((2, count, width), BF16),
            pltpu.VMEM((2, count, full), BF16),
            pltpu.VMEM((2, count, 2 * full), BF16),
            pltpu.VMEM((2, 2, tok, width), BF16),
            pltpu.VMEM((2, 2, tok, width), BF16),
            pltpu.VMEM((2, 2, tok, width), BF16),
            pltpu.SemaphoreType.DMA((5, steps, parts)),
            pltpu.SemaphoreType.DMA((2, steps, parts)),
            pltpu.SemaphoreType.DMA((6,)),
            pltpu.SemaphoreType.DMA((2,)),
            pltpu.SemaphoreType.DMA((2,)),
            pltpu.SemaphoreType.DMA((2, 4)),
            pltpu.SemaphoreType.DMA((2, 2)),
            pltpu.SemaphoreType.DMA((2, 2)),
            pltpu.SemaphoreType.DMA((2, 2)),
            pltpu.SemaphoreType.REGULAR,
        ],
        compiler_params=pltpu.CompilerParams(
            collective_id=collective_id, has_side_effects=True, vmem_limit_bytes=VMEM_BYTES
        ),
        name="expert_exchange",
    )(tokens, slots, gates, cots, *weights)
    return out[:6]


def return_sum(shares, collective_id):
    nz, ny, tok, width = shares.shape
    assert ny == 2

    def kernel(share_ref, out_ref, *scratch):
        back = Return(share_ref, out_ref, scratch)
        greet(back.peers())
        back.start()
        for turn in range(nz - 1):
            back.send(turn)
        back.finish()

    return pl.pallas_call(
        kernel,
        in_specs=[pl.BlockSpec(memory_space=pl.ANY)],
        out_specs=pl.BlockSpec(memory_space=pltpu.VMEM),
        out_shape=jax.ShapeDtypeStruct((tok, width), BF16),
        scratch_shapes=Return.scratch(nz, tok, width),
        compiler_params=pltpu.CompilerParams(
            collective_id=collective_id, has_side_effects=True, vmem_limit_bytes=VMEM_BYTES
        ),
        name="return_sum",
    )(shares)


def project_forward(normed, weights, gains, swaps, nh, nb, seqs, share, collective_id):
    tok, width = normed.shape
    tile, columns = weights[0].shape
    heads = columns // HEAD_DIM
    items = seqs * heads
    piece = tok // seqs
    span = nh * piece
    rows = nh * tok
    nz = nb // 2
    lots = nh * seqs
    count = len(swaps)

    def kernel(normed_ref, wq_ref, wk_ref, wv_ref, gain_ref, *refs):
        swap_in, refs = refs[:count], refs[count:]
        out_ref, qraw_ref, kraw_ref, inv_ref, group_ref, *refs = refs
        all_refs, refs = refs[:3], refs[3:]
        swap_out, refs = refs[:count], refs[count:]
        (
            vraw_ref, give_ref, sum_ref, norm_send, norm_recv, relay_send, relay_recv,
            sum_send, sum_recv, give_send, give_recv, swap_send, swap_recv,
        ) = refs
        head, blk = lax.axis_index("head"), lax.axis_index("blk")
        own_refs = (wq_ref, wk_ref, wv_ref)
        relay = Relay(
            [(own, everything, 1) for own, everything in zip(own_refs, all_refs)],
            nz, 1, relay_send, relay_recv, spread_y=False,
        )
        z, core = relay.z, relay.core
        swap = Swap(list(zip(swap_in, swap_out)), swap_send, swap_recv)
        others = [lax.rem(head + k, nh) for k in range(1, nh)]
        devices = [{"blk": blk, "head": other} for other in others]
        blks = [lax.rem(blk + k, nb) for k in range(1, nb)]
        greet(
            [(device, None) for device in devices]
            + [({"blk": other, "head": head}, None) for other in blks]
        )
        relay.start()

        def lines(slot):
            return pl.ds(pl.multiple_of(slot * tok, tok), tok)

        def norm_copy(k, slot):
            return pltpu.make_async_remote_copy(
                src_ref=normed_ref,
                dst_ref=group_ref.at[lines(slot)],
                send_sem=norm_send.at[k],
                recv_sem=norm_recv.at[slot],
                device_id=devices[k],
                device_id_type=pl.DeviceIdType.MESH,
            )

        def sum_copy(k, slot):
            return pltpu.make_async_remote_copy(
                src_ref=sum_ref.at[slot],
                dst_ref=sum_ref.at[slot],
                send_sem=sum_send.at[k],
                recv_sem=sum_recv.at[slot],
                device_id=devices[k],
                device_id_type=pl.DeviceIdType.MESH,
            )

        def give_copy(k, n, slot):
            return pltpu.make_async_remote_copy(
                src_ref=give_ref.at[blks[k] // share, n],
                dst_ref=out_ref.at[slot, n],
                send_sem=give_send.at[k, n],
                recv_sem=give_recv.at[slot, n],
                device_id={"blk": blks[k], "head": head},
                device_id_type=pl.DeviceIdType.MESH,
            )

        for k in range(nh - 1):
            norm_copy(k, head).start()
        swap.start()
        group_ref[lines(head), :] = normed_ref[...]
        for own, everything in zip(own_refs, all_refs):
            everything[z, core, 0] = own[...]

        raws = (qraw_ref, kraw_ref, vraw_ref)

        def multiply(rank):
            at = nearest(z, rank, nz)
            relay.arrived(at, 0, 1 - core)
            cols = pl.ds(pl.multiple_of(at * 2 * tile, 2 * tile), 2 * tile)
            for n in (2, 0, 1):
                product = mm(group_ref[:, cols], all_refs[n][at].reshape(2 * tile, columns))
                if rank == 0:
                    raws[n][...] = product
                else:
                    raws[n][...] += product

        for away in range(1, nz - 1):
            relay.pass_on_z(away)
        for k in range(nh - 1):
            norm_copy(k, others[k]).wait_recv()
        for rank in range(nz - 1):
            multiply(rank)
        relay.pass_on_z(nz - 1)
        multiply(nz - 1)

        def place(n, lot, hl):
            at, s = lot // seqs, lot % seqs
            return give_ref.at[s * heads + hl, n, pl.ds(at * piece, piece)]

        for lot in range(lots):
            here = slice(lot * piece, (lot + 1) * piece)
            for hl in range(heads):
                cols = slice(hl * HEAD_DIM, (hl + 1) * HEAD_DIM)
                place(2, lot, hl)[...] = vraw_ref[here, cols].astype(BF16)
            for n in range(2):
                total = jnp.zeros((piece, HEAD_DIM), F32)
                for hl in range(heads):
                    raw = raws[n][here, hl * HEAD_DIM : (hl + 1) * HEAD_DIM]
                    total = total + raw * raw
                sum_ref[head, n * lots + lot : n * lots + lot + 1, :] = jnp.sum(
                    total.T, axis=0, keepdims=True
                )
        for k in range(nh - 1):
            sum_copy(k, head).start()
        for k in range(nb - 1):
            give_copy(k, 2, blk).start()
        for k in range(nh - 1):
            sum_copy(k, others[k]).wait_recv()
        total_sums = sum_ref[0]
        for slot in range(1, nh):
            total_sums = total_sums + sum_ref[slot]
        inv_ref[...] = lax.rsqrt(total_sums / width + EPSILON)
        for n in range(2):
            for lot in range(lots):
                here = slice(lot * piece, (lot + 1) * piece)
                row = inv_ref[n * lots + lot : n * lots + lot + 1, :]
                inv = jnp.broadcast_to(row, (HEAD_DIM, piece)).T
                for hl in range(heads):
                    cols = slice(hl * HEAD_DIM, (hl + 1) * HEAD_DIM)
                    place(n, lot, hl)[...] = (
                        raws[n][here, cols] * inv * gain_ref[n : n + 1, cols]
                    ).astype(BF16)
            for k in range(nb - 1):
                give_copy(k, n, blk).start()
        for n in range(3):
            out_ref[blk, n] = give_ref[blk // share, n]
        for n in (2, 0, 1):
            for k in range(nb - 1):
                give_copy(k, n, blks[k]).wait_recv()
                give_copy(k, n, blk).wait_send()
        for k in range(nh - 1):
            norm_copy(k, head).wait_send()
            sum_copy(k, head).wait_send()
        swap.wait()
        relay.drain()

    anywhere = pl.BlockSpec(memory_space=pl.ANY)
    inside = pl.BlockSpec(memory_space=pltpu.VMEM)
    out = pl.pallas_call(
        kernel,
        in_specs=[inside] * 5 + [anywhere] * count,
        out_specs=[inside] * 8 + [anywhere] * count,
        out_shape=[
            jax.ShapeDtypeStruct((nb, 3, span, HEAD_DIM), BF16),
            jax.ShapeDtypeStruct((rows, columns), F32),
            jax.ShapeDtypeStruct((rows, columns), F32),
            jax.ShapeDtypeStruct((2 * lots, piece), F32),
            jax.ShapeDtypeStruct((rows, width), BF16),
        ]
        + [jax.ShapeDtypeStruct((nz, 2, 1, tile, columns), BF16)] * 3
        + [jax.ShapeDtypeStruct(v.shape, v.dtype) for v in swaps],
        scratch_shapes=[
            pltpu.VMEM((rows, columns), F32),
            pltpu.VMEM((items, 3, span, HEAD_DIM), BF16),
            pltpu.VMEM((nh, 2 * lots, piece), F32),
            pltpu.SemaphoreType.DMA((nh - 1,)),
            pltpu.SemaphoreType.DMA((nh,)),
            pltpu.SemaphoreType.DMA((5, nz, 3)),
            pltpu.SemaphoreType.DMA((2, nz, 3)),
            pltpu.SemaphoreType.DMA((nh - 1,)),
            pltpu.SemaphoreType.DMA((nh,)),
            pltpu.SemaphoreType.DMA((nb - 1, 3)),
            pltpu.SemaphoreType.DMA((nb, 3)),
            pltpu.SemaphoreType.DMA((count,)),
            pltpu.SemaphoreType.DMA((count,)),
        ],
        compiler_params=pltpu.CompilerParams(
            collective_id=collective_id, has_side_effects=True, vmem_limit_bytes=VMEM_BYTES
        ),
        name="project_forward",
    )(normed, *weights, gains, *swaps)
    gathered = [v.reshape(width, columns) for v in out[5:8]]
    return out[0], out[1:3], out[3], out[4], gathered, out[8:]


def project_backward(
    grads, raws, invs, gains, group, weights, swaps, sums, stats, nh, nb, collective_id
):
    rows, width = group.shape
    columns = raws[0].shape[1]
    items = grads.shape[0]
    heads = columns // HEAD_DIM
    seqs = items // heads
    tok = rows // nh
    piece = tok // seqs
    nz = nb // 2
    tile = width // nb
    lots = nh * seqs
    chunk = min(512, width)
    count = len(swaps)

    def kernel(grad_ref, qraw_ref, kraw_ref, inv_ref, gain_ref, group_ref, wq_ref, wk_ref, wv_ref, stat_ref, *refs):
        swap_in, refs = refs[:count], refs[count:]
        share_ref, refs = refs[: len(sums)], refs[len(sums) :]
        out_ref, *refs = refs
        tile_refs, refs = refs[:3], refs[3:]
        qk_ref, product_ref, stat_out, *refs = refs
        swap_out, refs = refs[:count], refs[count:]
        total_ref, refs = refs[: len(sums)], refs[len(sums) :]
        swap_send, swap_recv, *refs = refs
        stat_own, stat_row, stat_head, stat_blk, *refs = refs
        head_send, head_recv, blk_send, blk_recv, *refs = refs
        chain = None
        if sums:
            chain, refs = ZReturn(refs[0], share_ref[0], total_ref[0], refs[1:5]), refs[5:]
        swap = Swap(list(zip(swap_in, swap_out)), swap_send, swap_recv)
        d_ref, sum_ref, part_ref, got_ref, sum_send, sum_recv, part_send, part_recv, *refs = refs
        give = refs[0]
        back = TileReturn(give, tile_refs, refs[1:])
        head, blk = lax.axis_index("head"), lax.axis_index("blk")
        core, z = back.core, back.z
        others = [lax.rem(head + k, nh) for k in range(1, nh)]
        devices = [{"blk": blk, "head": other} for other in others]
        column = [{"blk": lax.rem(blk + k, nb), "head": head} for k in range(1, nb)]

        def head_copy(k):
            return pltpu.make_async_remote_copy(
                src_ref=stat_own,
                dst_ref=stat_head.at[nh - 2 - k],
                send_sem=head_send.at[k],
                recv_sem=head_recv.at[nh - 2 - k],
                device_id=devices[k],
                device_id_type=pl.DeviceIdType.MESH,
            )

        def blk_copy(k):
            return pltpu.make_async_remote_copy(
                src_ref=stat_row,
                dst_ref=stat_blk.at[nb - 2 - k],
                send_sem=blk_send.at[k],
                recv_sem=blk_recv.at[nb - 2 - k],
                device_id=column[k],
                device_id_type=pl.DeviceIdType.MESH,
            )

        def sum_copy(k, slot):
            return pltpu.make_async_remote_copy(
                src_ref=sum_ref.at[slot],
                dst_ref=sum_ref.at[slot],
                send_sem=sum_send.at[k],
                recv_sem=sum_recv.at[slot],
                device_id=devices[k],
                device_id_type=pl.DeviceIdType.MESH,
            )

        def part_copy(k):
            return pltpu.make_async_remote_copy(
                src_ref=part_ref.at[k],
                dst_ref=got_ref.at[nh - 2 - k],
                send_sem=part_send.at[k],
                recv_sem=part_recv.at[nh - 2 - k],
                device_id=devices[k],
                device_id_type=pl.DeviceIdType.MESH,
            )

        def grad_tile(n, lot, hl):
            at, s = lot // seqs, lot % seqs
            block, offset = divmod(at * piece, BLOCK)
            return grad_ref[s * heads + hl, block, n, offset : offset + piece, :]

        def upright(row):
            return jnp.broadcast_to(row, (HEAD_DIM, piece)).T

        for lot in range(lots):
            here = slice(lot * piece, (lot + 1) * piece)
            for n, raw_ref in enumerate((qraw_ref, kraw_ref)):
                total = jnp.zeros((piece, HEAD_DIM), F32)
                for hl in range(heads):
                    cols = slice(hl * HEAD_DIM, (hl + 1) * HEAD_DIM)
                    gained = grad_tile(n, lot, hl).astype(F32) * gain_ref[n : n + 1, cols]
                    total = total + gained * raw_ref[here, cols]
                sum_ref[head, n * lots + lot : n * lots + lot + 1, :] = jnp.sum(
                    total.T, axis=0, keepdims=True
                )
        greet([(device, None) for device in devices + column])
        for k in range(nh - 1):
            sum_copy(k, head).start()
        swap.start()
        edge = jnp.logical_or(z == 0, z == nz - 1)
        inner = jnp.logical_not(edge)
        if chain:
            chain.start()
            for turn in range(nz - 1):
                pl.when(edge)(lambda turn=turn: chain.send(turn))
        for lot in range(lots):
            here = slice(lot * piece, (lot + 1) * piece)
            for hl in range(heads):
                cols = slice(2 * columns + hl * HEAD_DIM, 2 * columns + (hl + 1) * HEAD_DIM)
                d_ref[here, cols] = grad_tile(2, lot, hl)
        for k in range(nh - 1):
            sum_copy(k, others[k]).wait_recv()
        total_sums = sum_ref[0]
        for slot in range(1, nh):
            total_sums = total_sums + sum_ref[slot]
        for n, raw_ref in enumerate((qraw_ref, kraw_ref)):
            gain_total = [jnp.zeros((1, HEAD_DIM), F32) for _ in range(heads)]
            for lot in range(lots):
                here = slice(lot * piece, (lot + 1) * piece)
                index = slice(n * lots + lot, n * lots + lot + 1)
                inv = upright(inv_ref[index, :])
                lean = inv * inv * inv * (upright(total_sums[index, :]) / width)
                for hl in range(heads):
                    cols = slice(hl * HEAD_DIM, (hl + 1) * HEAD_DIM)
                    grad = grad_tile(n, lot, hl).astype(F32)
                    raw = raw_ref[here, cols]
                    gain_total[hl] = gain_total[hl] + jnp.sum(grad * raw * inv, axis=0, keepdims=True)
                    d_ref[here, n * columns + hl * HEAD_DIM : n * columns + (hl + 1) * HEAD_DIM] = (
                        inv * (grad * gain_ref[n : n + 1, cols]) - raw * lean
                    ).astype(BF16)
            for hl in range(heads):
                qk_ref[n : n + 1, hl * HEAD_DIM : (hl + 1) * HEAD_DIM] = gain_total[hl]

        for turn, target in enumerate(back.targets):
            for at, dest in ((1 - core, give), (core, back.mine)):
                cols = pl.ds(pl.multiple_of((target * 2 + at) * tile, tile), tile)
                dest[target] = mm(group_ref[:, cols], d_ref[...], TN).astype(BF16)
            for part in range(back.parts):
                back.y_copy(target, part).start()
            if turn < nz - 1:
                pl.when(edge)(lambda turn=turn: back.send(turn))

        product_ref[...] = jnp.zeros_like(product_ref)

        def partial(at, store):
            lines = pl.ds(pl.multiple_of(at * tok, tok), tok)
            for col in range(0, width, chunk):
                cols = slice(col, col + chunk)
                total = mm(d_ref[lines, 0:columns], wq_ref[cols, :], NT)
                total = total + mm(d_ref[lines, columns : 2 * columns], wk_ref[cols, :], NT)
                total = total + mm(d_ref[lines, 2 * columns : 3 * columns], wv_ref[cols, :], NT)
                product_ref[:, cols] += jnp.sum(
                    total * group_ref[lines, cols].astype(F32), axis=0, keepdims=True
                )
                store(cols, total)

        sent = 0
        for k in range(nh - 1):

            def keep(cols, total, k=k):
                part_ref[k, :, cols] = total.astype(BF16)

            partial(others[k], keep)
            part_copy(k).start()
            while sent < nz - 1 and (k + 1) * (nz - 1) >= (sent + 2) * (nh - 1):
                if chain:
                    pl.when(inner)(lambda turn=sent: chain.send(turn))
                pl.when(inner)(lambda turn=sent: back.send(turn))
                sent += 1

        def keep_own(cols, total):
            out_ref[:, cols] = total

        partial(head, keep_own)
        stat_own[...] = stat_ref[...]
        lots_wide = width // 128
        for c in range(lots_wide):
            stat_own[c : c + 1, :] = product_ref[:, c * 128 : (c + 1) * 128]
        for n in range(2):
            for c in range(columns // 128):
                line = (2 + n) * lots_wide + head * (columns // 128) + c
                stat_own[pl.ds(line, 1), :] = qk_ref[n : n + 1, c * 128 : (c + 1) * 128]
        for k in range(nh - 1):
            head_copy(k).start()
        for turn in range(sent, nz - 1):
            if chain:
                pl.when(inner)(lambda turn=turn: chain.send(turn))
            pl.when(inner)(lambda turn=turn: back.send(turn))
        total = stat_own[...]
        for k in range(nh - 1):
            head_copy(nh - 2 - k).wait_recv()
            total = total + stat_head[k]
        stat_row[...] = total
        for k in range(nb - 1):
            blk_copy(k).start()
        for k in range(nh - 1):
            part_copy(nh - 2 - k).wait_recv()
            for r in range(0, tok, 64):
                here = pl.ds(r, 64)
                out_ref[here, :] += got_ref[k, here, :].astype(F32)
        back.finish()
        if chain:
            chain.finish()
        for k in range(nh - 1):
            sum_copy(k, head).wait_send()
            part_copy(k).wait_send()
            head_copy(k).wait_send()
        total = stat_row[...]
        for k in range(nb - 1):
            blk_copy(nb - 2 - k).wait_recv()
            total = total + stat_blk[k]
        stat_out[...] = total
        for k in range(nb - 1):
            blk_copy(k).wait_send()
        swap.wait()

    anywhere = pl.BlockSpec(memory_space=pl.ANY)
    inside = pl.BlockSpec(memory_space=pltpu.VMEM)
    out = pl.pallas_call(
        kernel,
        in_specs=[inside] * 10 + [anywhere] * (count + len(sums)),
        out_specs=[inside] * 7 + [anywhere] * count + [inside] * len(sums),
        out_shape=[jax.ShapeDtypeStruct((tok, width), F32)]
        + [jax.ShapeDtypeStruct((tile, columns), F32)] * 3
        + [jax.ShapeDtypeStruct((2, columns), F32), jax.ShapeDtypeStruct((1, width), F32)]
        + [jax.ShapeDtypeStruct(stats.shape, F32)]
        + [jax.ShapeDtypeStruct(v.shape, v.dtype) for v in swaps]
        + [jax.ShapeDtypeStruct((tok, width), BF16)] * len(sums),
        scratch_shapes=[
            pltpu.SemaphoreType.DMA((count,)),
            pltpu.SemaphoreType.DMA((count,)),
        ]
        + [pltpu.VMEM(stats.shape, F32)] * 2
        + [pltpu.VMEM((n - 1,) + stats.shape, F32) for n in (nh, nb)]
        + [pltpu.SemaphoreType.DMA((n - 1,)) for n in (nh, nh, nb, nb)]
        + ([pltpu.VMEM((nz, tok, width), BF16)] + ZReturn.scratch(nz, tok, width)) * len(sums)
        + [
            pltpu.VMEM((rows, 3 * columns), BF16),
            pltpu.VMEM((nh, 2 * lots, piece), F32),
            pltpu.VMEM((nh - 1, tok, width), BF16),
            pltpu.VMEM((nh - 1, tok, width), BF16),
            pltpu.SemaphoreType.DMA((nh - 1,)),
            pltpu.SemaphoreType.DMA((nh,)),
            pltpu.SemaphoreType.DMA((nh - 1,)),
            pltpu.SemaphoreType.DMA((nh - 1,)),
        ]
        + TileReturn.scratch(nz, tile, 3 * columns),
        compiler_params=pltpu.CompilerParams(
            collective_id=collective_id, has_side_effects=True, vmem_limit_bytes=VMEM_BYTES
        ),
        name="project_backward",
    )(grads, *raws, invs, gains, group, *weights, stats, *swaps, *sums)
    return out[0], out[1:4], out[6], out[7 : 7 + count], out[7 + count :]


def local(
    hidden_in,
    attn_gain,
    w_query,
    w_key,
    w_value,
    query_gain,
    key_gain,
    w_out,
    ffn_gain,
    w_gate,
    w_up,
    w_down,
    routes,
    gate_weights,
    block_starts,
    cotangent,
):
    head_count = lax.axis_size("head")
    blk_count = lax.axis_size("blk")
    head_index = lax.axis_index("head")
    blk_index = lax.axis_index("blk")
    piece, seqs, width = hidden_in.shape
    span = piece * head_count
    per = span // BLOCK
    columns = w_query.shape[1]
    heads_here = columns // HEAD_DIM
    top_count = routes.shape[2]
    experts = blk_count * head_count // 2
    devices = blk_count * head_count
    tok = piece * seqs
    capacity = max(2, 5 * tok * top_count // (4 * experts))
    rows = -(-capacity // 32) * 32
    items = seqs * heads_here
    share = blk_count // items
    scale = 1.0 / math.sqrt(HEAD_DIM)
    everyone = ("blk", "head")

    def own_rows(values):
        return values.transpose(1, 0, 2).reshape(tok, values.shape[2])

    def out_rows(values):
        return values.reshape(seqs, piece, width).transpose(1, 0, 2)

    nz, ny = blk_count // 2, head_count // 2

    def flip_head(values, bit):
        return lax.ppermute(values, "head", [(h, h ^ bit) for h in range(head_count)])

    def flip_blk(values, bit):
        return lax.ppermute(values, "blk", [(b, b ^ bit) for b in range(blk_count)])


    table = jnp.concatenate([own_rows(routes).astype(F32).T, own_rows(gate_weights).T], axis=0)

    hidden_f = own_rows(hidden_in).astype(F32)
    grad_y_b = own_rows(cotangent)
    grad_y = grad_y_b.astype(F32)

    inv_one = inverse_rms(hidden_f)
    normed = (hidden_f * inv_one * attn_gain).astype(BF16)
    gain_query = lax.dynamic_slice_in_dim(query_gain, head_index * columns, columns)
    gain_key = lax.dynamic_slice_in_dim(key_gain, head_index * columns, columns)
    qk_gains = jnp.stack([gain_query, gain_key])
    out_w = lax.all_gather(w_out, "blk", axis=1, tiled=True)
    qkv, raws, invs, group, qkv_cols, (gate_other,) = project_forward(
        normed, (w_query, w_key, w_value), qk_gains, (w_gate[0],), head_count, blk_count, seqs,
        share, 5,
    )

    def to_items(values):
        parts = values.reshape(head_count, seqs, piece, heads_here, HEAD_DIM)
        parts = parts.transpose(1, 3, 0, 2, 4).reshape(items, span, HEAD_DIM)
        return jnp.repeat(parts, share, axis=0) if share > 1 else parts

    def from_items(values):
        if share > 1:
            values = values.reshape(items, share, span, HEAD_DIM).astype(F32).sum(1)
        parts = values.reshape(seqs, heads_here, head_count, piece, HEAD_DIM)
        return parts.transpose(2, 0, 3, 1, 4).reshape(head_count * tok, columns)

    def swap(values):
        return lax.all_to_all(values, "blk", split_axis=0, concat_axis=0, tiled=True)

    item = blk_index // share
    starts = lax.dynamic_index_in_dim(block_starts, item // heads_here, 0, keepdims=False)
    qkv = qkv.reshape(blk_count, 3, per, BLOCK, HEAD_DIM)
    total_blocks = blk_count * per
    key_block = jnp.arange(total_blocks, dtype=jnp.int32)
    bias = jnp.where(key_block[None, :] >= starts[:, None], 0.0, -1e30).astype(F32).reshape(-1)
    heads_out, heads_out_t, log_total, all_cots, tables, up_other, down_other = attend_forward(
        bias, qkv, grad_y_b, table, (w_up[0], w_down[0]), nz, ny, scale, share, 2
    )
    expert_weights = (w_gate[0], gate_other, w_up[0], up_other, w_down[0], down_other)

    expert = (blk_index * head_count + head_index) // 2
    named = tables[..., :top_count, :] == expert.astype(F32)
    hit = jnp.any(named, axis=-2)
    gates = jnp.sum(jnp.where(named, tables[..., top_count:, :], 0.0), axis=-2)[..., None, :]
    before = jnp.triu(jnp.ones((tok, tok), BF16), 1)
    ranks = jnp.dot(
        hit.reshape(-1, tok).astype(BF16), before, preferred_element_type=F32
    ).astype(jnp.int32)
    slots = jnp.where(hit, ranks.reshape(hit.shape), -1)[..., None, :]

    attended = from_items(heads_out.reshape(blk_count, span, HEAD_DIM)).astype(BF16)
    branch = lax.psum_scatter(
        mm(attended, out_w).astype(BF16), "head", scatter_dimension=0, tiled=True
    ).astype(F32)
    middle = hidden_f + branch
    inv_two = inverse_rms(middle)
    normed_two = (middle * inv_two * ffn_gain).astype(BF16)

    dx_share, moe_share, xr, er, hid, dpre = expert_exchange(
        normed_two, all_cots, slots, gates, expert_weights, head_count, blk_count, rows, 0
    )

    def halvings(count):
        return [1 << i for i in reversed(range(count.bit_length() - 1))]

    def halve(values, flip, bit, mine):
        pair = values.reshape((2, values.shape[0] // 2) + values.shape[1:])
        kept = lax.dynamic_index_in_dim(pair, mine, 0, keepdims=False)
        sent = lax.dynamic_index_in_dim(pair, 1 - mine, 0, keepdims=False)
        return kept, flip(sent.astype(BF16), bit)

    y_bits = [(flip_head, 2 * b, (head_index // (2 * b)) % 2) for b in halvings(ny)]
    z_bits = [(flip_blk, 2 * b, (blk_index // (2 * b)) % 2) for b in halvings(nz)]

    def give_back(values, bits):
        for flip, bit, mine in bits:
            kept, came = halve(values, flip, bit, mine)
            values = kept.astype(F32) + came.astype(F32)
        return values[0]

    if ny == 2:
        grad_normed_two = return_sum(dx_share, 1)
    else:
        grad_normed_two = give_back(dx_share.swapaxes(0, 1), y_bits)
        grad_normed_two = give_back(grad_normed_two, z_bits).astype(BF16)
    grad_normed_two, moe_share = lax.optimization_barrier((grad_normed_two, moe_share))
    grad_normed_two = grad_normed_two.astype(F32)
    xr, er = xr.reshape(-1, width), er.reshape(-1, width)
    hid, dpre = [v.reshape(-1, v.shape[-1]) for v in (hid, dpre)]
    half = w_gate.shape[2]
    dgate, dgate_other, dup, dup_other = [dpre[:, n * half : (n + 1) * half] for n in range(4)]

    halves = [
        mm(hid[:, :half], er, TN), mm(xr, dgate, TN), mm(xr, dup, TN),
        mm(hid[:, half:], er, TN), mm(xr, dgate_other, TN), mm(xr, dup_other, TN),
    ]
    gained_two = grad_normed_two * ffn_gain
    ffn_gain_part = jnp.sum(grad_normed_two * middle * inv_two, 0)
    grad_middle = (
        grad_y
        + inv_two * gained_two
        - middle * inv_two * inv_two * inv_two * jnp.mean(gained_two * middle, -1, keepdims=True)
    )
    grad_branch = grad_middle.astype(BF16)
    grad_group = lax.all_gather(grad_branch, "head", axis=0, tiled=True)
    grad_group, *halves = lax.optimization_barrier((grad_group, *halves))
    others = [v.astype(BF16) for v in halves[3:]]
    grad_attended = mm(grad_group, out_w, NT).astype(BF16)
    out_part = mm(attended, grad_group, TN)
    grad_heads = swap(to_items(grad_attended)).reshape(blk_count * per, BLOCK, HEAD_DIM)
    own_sum = ny == 2
    middle_row = half // 2
    grad_qkv, (down_first, gate_part, up_part), sums = attend_backward(
        bias, qkv, grad_heads, heads_out_t, log_total,
        (others[0][:middle_row], others[1], others[2]), [moe_share] * own_sum, scale, share, 3,
    )
    if share > 1:
        grad_qkv = grad_qkv.reshape((items, share) + grad_qkv.shape[1:])
        grad_qkv = grad_qkv.astype(F32).sum(1).astype(BF16)
    if own_sum:
        expert_sum = sums[0].astype(F32)
    else:
        expert_sum = give_back(give_back(moe_share.swapaxes(0, 1), y_bits), z_bits)
    result = middle + expert_sum
    square_parts = jnp.stack(
        [jnp.sum(result * result), jnp.sum(branch * branch), jnp.sum(expert_sum * expert_sum)]
    )
    zero_width = jnp.zeros((width,), F32)
    stats = jnp.concatenate(
        [zero_width, ffn_gain_part, zero_width, zero_width, jnp.pad(square_parts, (0, 8 * 128 - 3))]
    ).reshape(-1, 128)
    grad_normed, (grad_query, grad_key, grad_value), totals, (down_last,), _ = project_backward(
        grad_qkv, raws, invs, qk_gains, group, qkv_cols, (others[0][middle_row:],), (), stats,
        head_count, blk_count, 4,
    )
    grad_down, grad_gate, grad_up = [
        (mine + other.astype(F32))[None]
        for mine, other in zip(
            halves[:3], (jnp.concatenate([down_first, down_last]), gate_part, up_part)
        )
    ]
    grad_normed = rounded(grad_normed)
    gained_one = grad_normed * attn_gain
    grad_hidden_in = (
        grad_middle
        + inv_one * gained_one
        - hidden_f
        * inv_one
        * inv_one
        * inv_one
        * jnp.mean(gained_one * hidden_f, -1, keepdims=True)
    )

    def over_blk(values, dim):
        return lax.psum_scatter(
            values.astype(BF16), "blk", scatter_dimension=dim, tiled=True
        ).astype(F32)

    grad_out = over_blk(out_part, 1)
    *totals, squares = jnp.split(totals.reshape(-1), [width, 2 * width, 3 * width, 4 * width])
    entry_count = tok * width * devices
    stream_stats = jnp.sqrt(squares[:3] / entry_count + EPSILON)
    return (
        out_rows(result.astype(BF16)),
        out_rows(grad_hidden_in.astype(BF16)),
        totals[0] / attn_gain,
        grad_query,
        grad_key,
        grad_value,
        totals[2],
        totals[3],
        grad_out,
        totals[1],
        grad_gate,
        grad_up,
        grad_down,
        stream_stats,
    )


def solution(mesh):
    rows3 = P(("blk", "head"), None, None)
    placed = (
        rows3, P(), P("blk", "head"), P("blk", "head"), P("blk", "head"), P(), P(),
        P("head", "blk"), P(), rows3, rows3, rows3, rows3, rows3, P(), rows3,
    )
    return jax.shard_map(
        local,
        mesh=mesh,
        in_specs=placed,
        out_specs=(
            rows3, rows3, P(), P("blk", "head"), P("blk", "head"), P("blk", "head"), P(), P(),
            P("head", "blk"), P(), rows3, rows3, rows3, P(),
        ),
        check_vma=False,
    )
```
